32 devices in a mesh: groups: 2 (over y), lat: 4 (over z), lon: 4 (over x, core).
Axes of the slice: x: 2, y: 2, z: 4, core: 2. Of those that a mesh axis runs over, the one named last changes fastest.
Arguments:
- profiles: bfloat16 [4, 137, 32, 2048], P('groups', None, 'lat', 'lon'), parts along dimension 0, may hold values from -6 to 6
- obs_cell: int32 [8, 1536], P(('groups', 'lon'), 'lat'), parts along dimension 0, may hold values from 0 to 4095
- obs_weight: float32 [18, 4, 1536], P('groups', 'lon', 'lat'), parts along dimension 0, may hold values from 0 to 1
- batch_instr: int32 [8, 96], P(('groups', 'lon'), 'lat'), parts along dimension 0, may hold values from 0 to 15
- batch_dest: int32 [8, 96], P(('groups', 'lon'), 'lat'), parts along dimension 0, may hold values from -1 to 47, as said below
- absorption: bfloat16 [16, 128, 137], replicated, may hold values from 0.00049972534 to 0.19921875
- cotangent: float32 [8, 768, 128], P(('groups', 'lon'), 'lat'), parts along dimension 0, may hold values from -6 to 6
Outputs:
- brightness_signal: float32 [8, 768, 128], P(('groups', 'lon'), 'lat'), parts along dimension 0
- profile_grad: float32 [4, 137, 32, 2048], P('groups', None, 'lat', 'lon'), parts along dimension 0
The draws below stay inside these ranges and needn't reach their ends.
There are 2 independent parts, one for each index of `groups`. The reference program is written for one: setup_inputs(seed, part) draws one part's arguments, and reference() takes and returns one part's arrays. A program takes and returns all parts, laid end to end along the dimension named above; an argument that names none is the same for every part. Nothing has to cross between parts.
Inputs may be any that keep to these rules, and one draw needn't show every extreme that they name: On each device the live batch slots (batch_dest >= 0) come first and are followed by empty ones (-1); the observation data of empty slots are drawn but unused. Within each longitude sector every processing slot 0 to 47 is named exactly once; slot g belongs to the lat device g // 12 of that sector. No device sends more than 6 of its batches to one lat device, and in every draw some device sends exactly 6 to one; in every sector some device owns 24 live batches.
All inputs are finite; a program needn't handle non-finite values.
Results may differ from the reference program's by a relative error of at most 0.014.
Values may be sent and summed in bfloat16 or wider, within the bound.
No kernel may reach another device: no remote copies, remote signals or barrier semaphores. Data moves between devices by JAX's collectives and lax.ppermute only.
A program may use at most 128 MiB of HBM per device.

```python
import math
import jax
import jax.numpy as jnp
from jax import lax

LEV = 137
CH = 128
INSTR = 16
CLAT = 8
CLON = 512
BATCH = 16
PROC = 12
OWN_MAX = 24
NLAT = 32
NLON = 2048
SLOTS_OWN = 96
OBS_OWN = 1536
OBS_PROC = 768
N_LAT = 4
N_LON = 4


def sector_routes(key):
    total_slots = N_LAT * PROC
    others = N_LAT - 1
    key_order, key_moves, key_cycle = jax.random.split(key, 3)
    spare_batches = total_slots - OWN_MAX
    level_base = spare_batches // others
    leftover = spare_batches % others
    counts_rest = level_base + (lax.iota(jnp.int32, others) < leftover).astype(jnp.int32)
    pair_count = others // 2
    left_part = counts_rest[0:2 * pair_count:2]
    right_part = counts_rest[1:2 * pair_count:2]
    headroom = jnp.minimum(left_part, OWN_MAX - right_part)
    shifted = jax.random.randint(key_moves, (pair_count,), 0, headroom + 1)
    counts_rest = counts_rest.at[0:2 * pair_count:2].add(-shifted)
    counts_rest = counts_rest.at[1:2 * pair_count:2].add(shifted)
    ordered_counts = jnp.concatenate([jnp.full((1,), OWN_MAX, jnp.int32), counts_rest])
    placement_order = jax.random.permutation(key_order, N_LAT)
    counts = jnp.zeros((N_LAT,), jnp.int32).at[placement_order].set(ordered_counts)
    offsets = jnp.cumsum(counts) - counts
    slot_index = lax.iota(jnp.int32, OWN_MAX)
    running = offsets[:, None] + slot_index[None, :]
    device_cycle = jax.random.permutation(key_cycle, N_LAT).astype(jnp.int32)
    target = device_cycle[running % N_LAT] * PROC + running // N_LAT
    filled = jnp.where(slot_index[None, :] < counts[:, None], target, -1)
    return filled.reshape(N_LAT * OWN_MAX).astype(jnp.int32)


def draw_batch_dest(key, part):
    key = jax.random.fold_in(key, 11)
    sector_keys = jax.random.split(key, N_LON)
    return jax.vmap(sector_routes)(sector_keys)


def place_ends(array, own_key, smallest, high):
    longest = array.shape.index(max(array.shape))
    spots = []
    for shift in (0, 1):
        where = [jax.random.randint(jax.random.fold_in(own_key, axis), (), 0, length) for axis, length in enumerate(array.shape)]
        where[longest] = (where[longest] + shift) % array.shape[longest]
        spots.append(tuple(where))
    return array.at[spots[0]].set(smallest).at[spots[1]].set(high)


def steps_of(own_key, shape, shards, least, high):
    gain = 1.0
    for position, blocks in shards:
        draws = jax.random.uniform(jax.random.fold_in(jax.random.fold_in(own_key, 6), position), (blocks,), jnp.float32, least / len(shards), high / len(shards))
        gain = gain * jnp.repeat(jnp.exp(draws), shape[position] // blocks).reshape((-1,) + (1,) * (len(shape) - 1 - position))
    return gain


def scatter_about(rng, dims, width, most, cuts=(), dtype=jnp.bfloat16):
    array = width * jax.random.normal(rng, dims, jnp.float32)
    if cuts:
        array = array * steps_of(rng, dims, cuts, -0.22, 0.18)
    return jnp.clip(array, -most, most).astype(dtype)


def setup_inputs(seed: int = 0, part: int = 0) -> dict:
    key_list = jax.random.split(jax.random.key(seed), 8)
    own_keys = jax.random.split(jax.random.fold_in(key_list[7], part), 8)
    profiles = scatter_about(own_keys[0], (2, LEV, NLAT, NLON), 1.0, 6.0, ((2, 4), (3, 4)))
    obs_cell = place_ends(jax.random.randint(own_keys[1], (N_LON, OBS_OWN), 0, CLAT * CLON), jax.random.fold_in(own_keys[1], 1), 0, (CLAT * CLON) - 1).astype(jnp.int32)
    obs_weight = jnp.clip(1.0 * jax.random.uniform(own_keys[2], (9, N_LON, OBS_OWN), jnp.float32) ** steps_of(own_keys[2], (9, N_LON, OBS_OWN), ((1, 4), (2, 4)), -0.2, 0.2), 0.0, 1.0)
    batch_instr = place_ends(jax.random.randint(own_keys[3], (N_LON, SLOTS_OWN), 0, INSTR), jax.random.fold_in(own_keys[3], 1), 0, INSTR - 1).astype(jnp.int32)
    batch_dest = draw_batch_dest(jax.random.fold_in(jax.random.fold_in(key_list[7], part), 71), part)
    absorption = jnp.clip(jnp.exp(jax.random.uniform(key_list[5], (INSTR, CH, LEV), jnp.float32, math.log(0.00049972534), math.log(0.19921875))), 0.00049972534, 0.19921875).astype(jnp.bfloat16)
    cotangent = scatter_about(own_keys[6], (N_LON, OBS_PROC, CH), 1.0, 6.0, ((0, 4), (1, 4)), jnp.float32)
    return dict(profiles=profiles, obs_cell=obs_cell, obs_weight=obs_weight, batch_instr=batch_instr, batch_dest=batch_dest, absorption=absorption, cotangent=cotangent)


def block_operator(arriving_vertical_stacks, absorb_rows, scaled_source_term):
    thermal_state = arriving_vertical_stacks[:, :, 0, :].astype(jnp.float32)
    humidity = arriving_vertical_stacks[:, :, 1, :].astype(jnp.float32)
    clipped_vertical_sounding = jnp.tanh(humidity)
    absorber = 1.0 + 0.5 * clipped_vertical_sounding
    coeffs = absorb_rows.astype(jnp.float32)
    depth = (coeffs[:, None, :, :] * absorber[:, :, None, :]).astype(jnp.bfloat16)
    levels = depth.shape[-1]
    higher_layer = (lax.iota(jnp.int32, levels)[:, None] <= lax.iota(jnp.int32, levels)[None, :]).astype(jnp.float32)
    flat_depth = depth.reshape(-1, levels).astype(jnp.float32)
    cumulative = jnp.dot(flat_depth, higher_layer, precision=lax.Precision.HIGHEST).reshape(depth.shape)
    passing_fraction = jnp.exp(-cumulative)
    previous = jnp.concatenate([jnp.ones(passing_fraction.shape[:-1] + (1,), jnp.float32), passing_fraction[..., :-1]], axis=-1)
    layer_kernel_factor = previous - passing_fraction
    brightness_signal = jnp.sum(layer_kernel_factor * thermal_state[:, :, None, :], axis=-1)
    thermal_sensitivity = jnp.sum(scaled_source_term[..., None] * layer_kernel_factor, axis=2)
    following_layer_entry = jnp.concatenate([thermal_state[..., 1:], jnp.zeros(thermal_state.shape[:-1] + (1,), jnp.float32)], axis=-1)
    passing_fraction_sensitivity = scaled_source_term[..., None] * (following_layer_entry - thermal_state)[:, :, None, :]
    grad_cumulative = (-passing_fraction_sensitivity * passing_fraction).astype(jnp.bfloat16)
    flat_grad = grad_cumulative.reshape(-1, levels).astype(jnp.float32)
    grad_depth = jnp.dot(flat_grad, higher_layer.T, precision=lax.Precision.HIGHEST).reshape(depth.shape)
    grad_absorber = jnp.sum(grad_depth * coeffs[:, None, :, :], axis=2)
    moisture_sensitivity = grad_absorber * 0.5 * (1.0 - clipped_vertical_sounding * clipped_vertical_sounding)
    return brightness_signal, jnp.stack([thermal_sensitivity, moisture_sensitivity], axis=2)


def reference(profiles, obs_cell, obs_weight, batch_instr, batch_dest, absorption, cotangent):
    lat_cells = CLAT * N_LAT
    lon_cells = CLON * N_LON
    pad_width = lon_cells + 2
    feature_width = 2 * LEV
    obs_device = OWN_MAX * BATCH
    padded = jnp.pad(profiles, ((0, 0), (0, 0), (1, 1), (1, 1)))
    flattened = padded.reshape(feature_width, -1).T
    cells = obs_cell.reshape(N_LON, N_LAT, obs_device)
    lat_index = lax.iota(jnp.int32, N_LAT)[None, :, None]
    lon_index = lax.iota(jnp.int32, N_LON)[:, None, None]
    row_global = lat_index * CLAT + cells // CLON
    col_global = lon_index * CLON + cells % CLON
    anchor = (row_global * pad_width + col_global).astype(jnp.int32)
    weights = obs_weight.reshape(9, N_LON, N_LAT, obs_device)
    gathered = jnp.zeros((N_LON, N_LAT, obs_device, feature_width), jnp.float32)
    for stencil_pos in range(9):
        offset = (stencil_pos // 3) * pad_width + stencil_pos % 3
        picked = flattened[anchor + offset].astype(jnp.float32)
        gathered = gathered + weights[stencil_pos][..., None] * picked
    interpolated = gathered.astype(jnp.bfloat16).reshape(N_LON, N_LAT * OWN_MAX, BATCH, 2, LEV)
    proc_slots = N_LAT * PROC
    owner_slots = N_LAT * OWN_MAX
    target = jnp.where(batch_dest >= 0, batch_dest, proc_slots).astype(jnp.int32)
    lon_rows = jnp.broadcast_to(lax.iota(jnp.int32, N_LON)[:, None], target.shape)
    slot_ids = jnp.broadcast_to(lax.iota(jnp.int32, owner_slots)[None, :], target.shape)
    source = jnp.zeros((N_LON, proc_slots), jnp.int32).at[lon_rows, target].set(slot_ids, mode="drop")
    proc_columns = jnp.take_along_axis(interpolated, source[:, :, None, None, None], axis=1)
    proc_instr = jnp.take_along_axis(batch_instr, source, axis=1)
    proc_absorb = absorption[proc_instr]
    scaled_source_term = cotangent.reshape(N_LON, proc_slots, BATCH, CH)
    blocks = N_LON * N_LAT
    brightness_signal, gradient = lax.map(
        lambda items: block_operator(items[0], items[1], items[2]),
        (proc_columns.reshape(blocks, PROC, BATCH, 2, LEV),
         proc_absorb.reshape(blocks, PROC, CH, LEV),
         scaled_source_term.reshape(blocks, PROC, BATCH, CH)))
    brightness_signal = brightness_signal.reshape(N_LON, N_LAT * PROC * BATCH, CH)
    gradient = gradient.reshape(N_LON, proc_slots, BATCH, 2, LEV)
    proc_rows = jnp.broadcast_to(lax.iota(jnp.int32, N_LON)[:, None], source.shape)
    owner_grad = jnp.zeros((N_LON, owner_slots, BATCH, 2, LEV), jnp.float32).at[proc_rows, source].set(gradient)
    owner_grad = owner_grad.reshape(N_LON, N_LAT, obs_device, feature_width)
    summed = jnp.zeros(((lat_cells + 2) * pad_width, feature_width), jnp.float32)
    for stencil_pos in range(9):
        offset = (stencil_pos // 3) * pad_width + stencil_pos % 3
        contrib = weights[stencil_pos][..., None] * owner_grad
        summed = summed.at[(anchor + offset).reshape(-1)].add(contrib.reshape(-1, feature_width))
    grid_grad = summed.reshape(lat_cells + 2, pad_width, 2, LEV)[1:-1, 1:-1]
    profile_grad = jnp.transpose(grid_grad, (2, 3, 0, 1))
    return brightness_signal, profile_grad
```

```python
import functools

import jax
import jax.numpy as jnp
from jax import lax
from jax.experimental import pallas as pl
from jax.experimental.pallas import tpu as pltpu
from jax.sharding import PartitionSpec as P

F32 = jnp.float32
BF16 = jnp.bfloat16
LOG2E = 1.4426950408889634
LANES = 128
EDGE = 16
NEAR = ((0, -1), (0, 1), (-1, -1), (-1, 1), (1, -1), (1, 1))
VMEM = pl.BlockSpec(memory_space=pltpu.VMEM)
SMEM = pl.BlockSpec(memory_space=pltpu.SMEM)
NN = (((1,), (0,)), ((), ()))
NT = (((1,), (1,)), ((), ()))
TN = (((0,), (0,)), ((), ()))


def dot(a, b, dims=NN):
    return lax.dot_general(a, b, dims, preferred_element_type=F32)


def round_up(value, unit):
    return -(-value // unit) * unit


def params(mib=48):
    return pltpu.CompilerParams(vmem_limit_bytes=mib * 1024 * 1024)


def iota(shape, dim):
    return lax.broadcasted_iota(jnp.int32, shape, dim)


def split_cells(cells, width):
    if width & (width - 1) == 0:
        return lax.shift_right_logical(cells, width.bit_length() - 1), cells & (width - 1)
    row = lax.div(cells, width)
    return row, cells - row * width


def fill_columns(cells_ref, weight_ref, columns_ref):
    width, obs = columns_ref.shape[1:]
    _, col = split_cells(cells_ref[...], width)
    weights = [weight_ref[k] for k in range(9)]
    step = 32

    def chunk(i, carry):
        base = pl.multiple_of(i * step, step)
        for lane in range(0, obs, LANES):
            part = slice(lane, lane + LANES)
            away = iota((step, LANES), 0) + base - col[:, part]
            hit = [away == b - 1 for b in range(3)]
            for a in range(3):
                value = jnp.zeros((step, LANES), F32)
                for b in range(3):
                    value = jnp.where(hit[b], weights[3 * a + b][:, part], value)
                columns_ref[a, pl.ds(base, step), part] = value.astype(BF16)
        return carry

    lax.fori_loop(0, width // step, chunk, 0)


def row_stencil(columns_ref, row_of, r):
    total = None
    for a in range(3):
        keep = jnp.where(row_of == r - a + 1, 1.0, 0.0).astype(BF16)
        term = columns_ref[a] * keep
        total = term if total is None else total + term
    return total


def edge_weights(cells_ref, weight_ref, rows, width):
    lines = len(NEAR) * EDGE
    obs = cells_ref.shape[1]
    row, col = split_cells(cells_ref[...], width)
    line = iota((lines, obs), 0)
    near = lax.shift_right_logical(line, 4)
    k = line & (EDGE - 1)
    none = -99
    row_at = jnp.full((lines, obs), none, jnp.int32)
    col_at = jnp.where((near & 1) == 0, -1, width)
    row_at = jnp.where((near == 0) & (k >= rows), k - rows, row_at)
    row_at = jnp.where((near == 1) & (k < rows), k, row_at)
    row_at = jnp.where((near == 2) & (k == 2 * rows - 1), -1, row_at)
    row_at = jnp.where((near == 3) & (k == rows - 1), -1, row_at)
    row_at = jnp.where((near == 4) & (k == rows), rows, row_at)
    row_at = jnp.where((near == 5) & (k == 0), rows, row_at)
    total = jnp.zeros((lines, obs), F32)
    for a in range(3):
        for b in range(3):
            hit = (row_at == row + (a - 1)) & (col_at == col + (b - 1))
            total = total + jnp.where(hit, weight_ref[3 * a + b], 0.0)
    return total.astype(BF16)


def pack_kernel(dims, profiles_ref, cot_ref, mid_ref, top_ref, bottom_ref, edge_ref, cot_out_ref, wide_ref):
    levels, rows, width, pad = dims
    for lane in range(0, width, LANES):
        part = profiles_ref[:, :, lane : lane + LANES]
        wide_ref[lane // LANES] = part.astype(F32).reshape(2 * levels * rows, LANES)
    edges = jnp.zeros((EDGE, 2 * pad), F32)
    k = iota((EDGE, LANES), 0)
    at_lane = iota((EDGE, LANES), 1)
    for r in range(rows):
        out = top_ref if r == 0 else bottom_ref if r == rows - 1 else mid_ref.at[r - 1]
        for v in range(2):
            for lane in range(0, width, LANES):
                value = wide_ref[lane // LANES, pl.ds(v * levels * rows + r, levels, stride=rows), :]
                value = jnp.concatenate([value, jnp.zeros((pad - levels, LANES), F32)], axis=0)
                out[v * pad : (v + 1) * pad, lane : lane + LANES] = value.astype(BF16)
        west = jnp.where((k == r) & (at_lane == 0), 1.0, 0.0).astype(BF16)
        east = jnp.where((k == rows + r) & (at_lane == LANES - 1), 1.0, 0.0).astype(BF16)
        edges = edges + dot(west, out[:, :LANES], NT) + dot(east, out[:, width - LANES :], NT)
    edges = edges.astype(BF16)

    def spread(s, carry):
        edge_ref[s] = jnp.zeros(edge_ref.shape[1:], BF16)
        edge_ref[s, :, : 2 * pad] = edges
        return carry

    lax.fori_loop(0, edge_ref.shape[0], spread, 0)
    cot = cot_ref[0].astype(BF16)

    def share(s, carry):
        cot_out_ref[s] = cot
        return carry

    lax.fori_loop(0, cot_out_ref.shape[0], share, 0)


def neighbour(n, grid):
    n_lat, n_lon = grid
    i = lax.axis_index("lat") + NEAR[n][0]
    j = lax.axis_index("lon") + NEAR[n][1]
    valid = (i >= 0) & (i < n_lat) & (j >= 0) & (j < n_lon)
    return jnp.where(valid, i * n_lon + j, 0), valid


def transfer_kernel(
    dims,
    cells_ref,
    weight_ref,
    instr_ref,
    dest_ref,
    absorb_ref,
    mid_ref,
    top_ref,
    bottom_ref,
    above_ref,
    below_ref,
    edge_ref,
    cot_ref,
    grad_ref,
    grad_above_ref,
    grad_below_ref,
    grad_edge_ref,
    rad_ref,
    columns_ref,
    halo_ref,
    field_ref,
    rate_ref,
    step_ref,
    cot_rows_ref,
    cot_t_ref,
    absorb_t_ref,
    signal_ref,
    s_part_ref,
    r_part_ref,
    shift_ref,
):
    levels, rows, width, pad, batch, grid = dims
    obs = cells_ref.shape[1]
    slots = obs // batch
    channels = cot_ref.shape[1]
    instruments = absorb_ref.shape[1]
    fill_columns(cells_ref, weight_ref, columns_ref)
    row, _ = split_cells(cells_ref[...], width)

    field_ref[...] = dot(above_ref[...], row_stencil(columns_ref, row, -1))
    field_ref[...] += dot(below_ref[...], row_stencil(columns_ref, row, rows))
    for r in range(rows):
        source = top_ref if r == 0 else bottom_ref if r == rows - 1 else mid_ref.at[r - 1]
        field_ref[...] += dot(source[...], row_stencil(columns_ref, row, r))
    for n in range(len(NEAR)):
        at, valid = neighbour(n, grid)
        halo_ref[n * EDGE : (n + 1) * EDGE, :] = edge_ref[at].astype(F32) * jnp.where(valid, 1.0, 0.0)
    edge_w = edge_weights(cells_ref, weight_ref, rows, width)
    field_ref[...] += dot(halo_ref[:, : 2 * pad].astype(BF16), edge_w, TN)

    for q in range(slots):
        where = dest_ref[0, q]
        start = pl.multiple_of(jnp.maximum(where, 0) * batch, batch)
        value = cot_ref[pl.ds(start, batch), :].astype(F32)
        cot_rows_ref[q * batch : (q + 1) * batch, :] = jnp.where(where >= 0, value, 0.0)
    for lane in range(0, obs, LANES):
        cot_t_ref[:, lane : lane + LANES] = cot_rows_ref[lane : lane + LANES, :].T
    lane_slot = lax.shift_right_logical(iota((1, obs), 1), batch.bit_length() - 1)
    chosen = jnp.zeros((1, obs), jnp.int32)
    for q in range(slots):
        chosen = jnp.where(lane_slot == q, instr_ref[0, q], chosen)
    pick = jnp.where(iota((instruments, obs), 0) == chosen, 1.0, 0.0)
    pick_bf = pick.astype(BF16)

    def turn(l, carry):
        absorb_t_ref[l] = absorb_ref[l].astype(F32).T.astype(BF16)
        return carry

    lax.fori_loop(0, levels, turn, 0)

    temperature = field_ref[0:pad, :]
    step_ref[...] = field_ref[1 : pad + 1, :] - temperature
    bent = jnp.tanh(field_ref[pad : 2 * pad, :])
    rate_ref[...] = -LOG2E * (1.0 + 0.5 * bent)
    tail = jnp.zeros((obs // LANES, (pad - levels) * 8, LANES), F32)
    s_part_ref[:, levels * 8 :, :] = tail
    r_part_ref[:, levels * 8 :, :] = tail
    part = 64
    for lane in range(0, obs, LANES):
        lanes = slice(lane, lane + LANES)
        group = lane // LANES
        for c0 in range(0, channels, part):
            first = c0 == 0
            cs = slice(c0, c0 + part)

            def level(l, row_base, j, rates, steps, cum, signal):
                a = dot(absorb_t_ref[l, cs, :], pick_bf[:, lanes])
                cot = cot_t_ref[cs, lanes]
                cum = cum + a * rates[j : j + 1]
                transmit = jnp.exp2(cum)
                r_sum = jnp.sum((cot * signal * a).reshape(part // 8, 8, LANES), axis=0)
                s_sum = jnp.sum((cot * transmit).reshape(part // 8, 8, LANES), axis=0)
                signal = signal + transmit * steps[j : j + 1]
                at = pl.ds(pl.multiple_of(row_base + 8 * j, 8), 8)
                if first:
                    r_part_ref[group, at, :] = r_sum
                    s_part_ref[group, at, :] = s_sum
                else:
                    r_part_ref[group, at, :] += r_sum
                    s_part_ref[group, at, :] += s_sum
                return cum, signal

            def block(b, carry):
                cum, signal = carry
                base = pl.multiple_of(b * 8, 8)
                rates = rate_ref[pl.ds(base, 8), lanes]
                steps = step_ref[pl.ds(base, 8), lanes]
                for j in range(8):
                    cum, signal = level(base + j, b * 64, j, rates, steps, cum, signal)
                return cum, signal

            start = jnp.zeros((part, LANES), F32)
            full = levels // 8
            cum, signal = lax.fori_loop(0, full, block, (start, start))
            rates = rate_ref[full * 8 : full * 8 + 8, lanes]
            steps = step_ref[full * 8 : full * 8 + 8, lanes]
            for j in range(levels - full * 8):
                cum, signal = level(full * 8 + j, full * 64, j, rates, steps, cum, signal)
            signal_ref[cs, lanes] = signal

    rad_ref[...] = jnp.zeros(rad_ref.shape, BF16)
    for lane in range(0, obs, LANES):
        lanes = slice(lane, lane + LANES)
        value = (signal_ref[:, lanes] + field_ref[0:1, lanes]).T.astype(BF16)
        for q in range(LANES // batch):
            where = dest_ref[0, lane // batch + q]

            @pl.when(where >= 0)
            def _():
                start = pl.multiple_of(where * batch, batch)
                rad_ref[pl.ds(start, batch), :] = value[q * batch : (q + 1) * batch, :]

    held = cot_t_ref[...] * signal_ref[...]
    held_hi = held.astype(BF16)
    held_lo = (held - held_hi.astype(F32)).astype(BF16)

    def contract(l0, count):
        rows_in = absorb_ref[pl.ds(l0, count)].reshape(count * instruments, channels)
        value = dot(rows_in, held_hi) + dot(rows_in, held_lo)
        value = value.reshape(count, instruments, obs) * pick[None]
        value = jnp.sum(value.reshape(count, instruments // 8, 8, obs), axis=1)
        at = pl.ds(pl.multiple_of(l0 * 8, 8), count * 8)
        value = value.reshape(count * 8, obs)
        for lane in range(0, obs, LANES):
            r_part_ref[lane // LANES, at, :] -= value[:, lane : lane + LANES]

    def contract_block(b, carry):
        contract(b * 8, 8)
        return carry

    lax.fori_loop(0, levels // 8, contract_block, 0)
    if levels % 8:
        contract(levels // 8 * 8, levels % 8)

    for lane in range(0, obs, LANES):
        lanes = slice(lane, lane + LANES)
        group = lane // LANES
        s_sum = s_part_ref[group, pl.ds(0, pad, stride=8), :]
        r_sum = r_part_ref[group, pl.ds(0, pad, stride=8), :]
        for k in range(1, 8):
            s_sum = s_sum + s_part_ref[group, pl.ds(k, pad, stride=8), :]
            r_sum = r_sum + r_part_ref[group, pl.ds(k, pad, stride=8), :]
        shift_ref[7:8, lanes] = jnp.sum(cot_t_ref[:, lanes], axis=0, keepdims=True)
        shift_ref[8 : 8 + pad, lanes] = s_sum
        grad_ref[0:pad, lanes] = (shift_ref[7 : 7 + pad, lanes] - s_sum).astype(BF16)
        bent = jnp.tanh(field_ref[pad : 2 * pad, lanes])
        grad_ref[pad : 2 * pad, lanes] = (0.5 * (1.0 - bent * bent) * r_sum).astype(BF16)

    grad = grad_ref[...]
    grad_above_ref[...] = dot(grad, row_stencil(columns_ref, row, -1), NT).astype(BF16)
    grad_below_ref[...] = dot(grad, row_stencil(columns_ref, row, rows), NT).astype(BF16)
    out = dot(edge_w, grad, NT).astype(BF16)

    def clear(s, carry):
        grad_edge_ref[s] = jnp.zeros(grad_edge_ref.shape[1:], BF16)
        return carry

    lax.fori_loop(0, grad_edge_ref.shape[0], clear, 0)
    for n in range(len(NEAR)):
        at, valid = neighbour(n, grid)

        @pl.when(valid)
        def _():
            grad_edge_ref[at, :, : 2 * pad] = out[n * EDGE : (n + 1) * EDGE, :]


def scatter_kernel(
    dims,
    cells_ref,
    weight_ref,
    grad_ref,
    from_above_ref,
    from_below_ref,
    edge_ref,
    rad_ref,
    out_ref,
    rad_out_ref,
    columns_ref,
    halo_ref,
    wide_ref,
):
    levels, rows, width, pad, grid = dims
    rad_out_ref[...] = jnp.sum(rad_ref[...].astype(F32), axis=0)[None]
    fill_columns(cells_ref, weight_ref, columns_ref)
    row, _ = split_cells(cells_ref[...], width)
    total = jnp.zeros(edge_ref.shape[1:], F32)
    for n in range(len(NEAR)):
        at, valid = neighbour(n, grid)
        halo_ref[n * EDGE : (n + 1) * EDGE, :] = edge_ref[at].astype(F32) * jnp.where(valid, 1.0, 0.0)
    edges = halo_ref[:, : 2 * pad].T.astype(BF16)
    lines = edges.shape[1]
    k = iota((lines, LANES), 0) & (EDGE - 1)
    at_lane = iota((lines, LANES), 1)
    for r in range(rows):
        value = dot(grad_ref[...], row_stencil(columns_ref, row, r), NT)
        if r == 0:
            value = value + from_above_ref[...].astype(F32)
        if r == rows - 1:
            value = value + from_below_ref[...].astype(F32)
        west = jnp.where((k == r) & (at_lane == 0), 1.0, 0.0).astype(BF16)
        east = jnp.where((k == rows + r) & (at_lane == LANES - 1), 1.0, 0.0).astype(BF16)
        first = value[:, :LANES] + dot(edges, west)
        last = value[:, width - LANES :] + dot(edges, east)
        value = jnp.concatenate([first, value[:, LANES : width - LANES], last], axis=1)
        for v in range(2):
            at = pl.ds(v * levels * rows + r, levels, stride=rows)
            for lane in range(0, width, LANES):
                wide_ref[lane // LANES, at, :] = value[v * pad : v * pad + levels, lane : lane + LANES]
    for lane in range(0, width, LANES):
        out_ref[:, lane : lane + LANES] = wide_ref[lane // LANES]


def per_device(profiles, obs_cell, obs_weight, batch_instr, batch_dest, absorption, cotangent):
    n_lat, n_lon = lax.axis_size("lat"), lax.axis_size("lon")
    grid = (n_lat, n_lon)
    levels, rows, width = profiles.shape[1:]
    instruments, channels, _ = absorption.shape
    obs = obs_cell.shape[1]
    slots = batch_dest.shape[1]
    batch = obs // slots
    proc = cotangent.shape[1]
    pad = round_up(levels, 16)
    feat = round_up(2 * pad, LANES)
    up = [(i, i + 1) for i in range(n_lat - 1)]
    down = [(b, a) for a, b in up]
    shape = jax.ShapeDtypeStruct

    mid, top, bottom, edge, cot = pl.pallas_call(
        functools.partial(pack_kernel, (levels, rows, width, pad)),
        out_shape=(
            shape((rows - 2, 2 * pad, width), BF16),
            shape((2 * pad, width), BF16),
            shape((2 * pad, width), BF16),
            shape((n_lat * n_lon, EDGE, feat), BF16),
            shape((n_lat, proc, channels), BF16),
        ),
        in_specs=[VMEM, VMEM],
        out_specs=(VMEM,) * 5,
        scratch_shapes=[pltpu.VMEM((width // LANES, 2 * levels * rows, LANES), F32)],
        compiler_params=params(),
        name="pack",
    )(profiles.reshape(2 * levels, rows, width), cotangent)

    above = lax.ppermute(bottom, "lat", up)
    below = lax.ppermute(top, "lat", down)
    edge_in = lax.all_to_all(edge, ("lat", "lon"), 0, 0, tiled=True)
    cot_in = lax.all_to_all(cot, "lat", 0, 0, tiled=True).reshape(n_lat * proc, channels)

    lines = len(NEAR) * EDGE
    grad, grad_above, grad_below, grad_edge, rad = pl.pallas_call(
        functools.partial(transfer_kernel, (levels, rows, width, pad, batch, grid)),
        out_shape=(
            shape((2 * pad, obs), BF16),
            shape((2 * pad, width), BF16),
            shape((2 * pad, width), BF16),
            shape((n_lat * n_lon, EDGE, feat), BF16),
            shape((n_lat * proc, channels), BF16),
        ),
        in_specs=[VMEM, VMEM, SMEM, SMEM] + [VMEM] * 8,
        out_specs=(VMEM,) * 5,
        scratch_shapes=[
            pltpu.VMEM((3, width, obs), BF16),
            pltpu.VMEM((lines, feat), F32),
            pltpu.VMEM((2 * pad, obs), F32),
            pltpu.VMEM((pad, obs), F32),
            pltpu.VMEM((pad, obs), F32),
            pltpu.VMEM((obs, channels), F32),
            pltpu.VMEM((channels, obs), F32),
            pltpu.VMEM((levels, channels, instruments), BF16),
            pltpu.VMEM((channels, obs), F32),
            pltpu.VMEM((obs // LANES, pad * 8, LANES), F32),
            pltpu.VMEM((obs // LANES, pad * 8, LANES), F32),
            pltpu.VMEM((pad + 8, obs), F32),
        ],
        compiler_params=params(),
        name="transfer",
    )(
        obs_cell,
        obs_weight,
        batch_instr,
        batch_dest,
        jnp.transpose(absorption, (2, 0, 1)),
        mid,
        top,
        bottom,
        above,
        below,
        edge_in,
        cot_in,
    )

    from_below = lax.ppermute(grad_above, "lat", down)
    from_above = lax.ppermute(grad_below, "lat", up)
    grad_edge_in = lax.all_to_all(grad_edge, ("lat", "lon"), 0, 0, tiled=True)
    rad_in = lax.all_to_all(rad.reshape(n_lat, proc, channels), "lat", 0, 0, tiled=True)

    gradient, radiance = pl.pallas_call(
        functools.partial(scatter_kernel, (levels, rows, width, pad, grid)),
        out_shape=(
            shape((2 * levels * rows, width), F32),
            shape((1, proc, channels), F32),
        ),
        in_specs=[VMEM] * 7,
        out_specs=(VMEM,) * 2,
        scratch_shapes=[
            pltpu.VMEM((3, width, obs), BF16),
            pltpu.VMEM((lines, feat), F32),
            pltpu.VMEM((width // LANES, 2 * levels * rows, LANES), F32),
        ],
        compiler_params=params(),
        name="scatter",
    )(obs_cell, obs_weight, grad, from_above, from_below, grad_edge_in, rad_in)
    return radiance, gradient.reshape(2, levels, rows, width)


def solution(mesh):
    placed = (
        P("groups", None, "lat", "lon"),
        P(("groups", "lon"), "lat"),
        P("groups", "lon", "lat"),
        P(("groups", "lon"), "lat"),
        P(("groups", "lon"), "lat"),
        P(),
        P(("groups", "lon"), "lat", None),
    )
    return jax.shard_map(
        per_device,
        mesh=mesh,
        in_specs=placed,
        out_specs=(P(("groups", "lon"), "lat", None), P("groups", None, "lat", "lon")),
        check_vma=False,
    )
```

```python
import functools

import jax
import jax.numpy as jnp
from jax import lax
from jax.experimental import pallas as pl
from jax.experimental.pallas import tpu as pltpu
from jax.sharding import PartitionSpec as P

F32 = jnp.float32
BF16 = jnp.bfloat16
LOG2E = 1.4426950408889634
LANES = 128
EDGE = 16
BLOCKS = 3
VMEM = pl.BlockSpec(memory_space=pltpu.VMEM)
SMEM = pl.BlockSpec(memory_space=pltpu.SMEM)
NN = (((1,), (0,)), ((), ()))
NT = (((1,), (1,)), ((), ()))
TN = (((0,), (0,)), ((), ()))


def dot(a, b, dims=NN):
    return lax.dot_general(a, b, dims, preferred_element_type=F32)


def round_up(value, unit):
    return -(-value // unit) * unit


def params(mib=48):
    return pltpu.CompilerParams(vmem_limit_bytes=mib * 1024 * 1024)


def iota(shape, dim):
    return lax.broadcasted_iota(jnp.int32, shape, dim)


def split_cells(cells, width):
    if width & (width - 1) == 0:
        return lax.shift_right_logical(cells, width.bit_length() - 1), cells & (width - 1)
    row = lax.div(cells, width)
    return row, cells - row * width


def fill_columns(cells_ref, weight_ref, columns_ref):
    width, obs = columns_ref.shape[1:]
    _, col = split_cells(cells_ref[...], width)
    weights = [weight_ref[k] for k in range(9)]
    step = 32

    def chunk(i, carry):
        base = pl.multiple_of(i * step, step)
        for lane in range(0, obs, LANES):
            part = slice(lane, lane + LANES)
            away = iota((step, LANES), 0) + base - col[:, part]
            hit = [away == b - 1 for b in range(3)]
            for a in range(3):
                value = jnp.zeros((step, LANES), F32)
                for b in range(3):
                    value = jnp.where(hit[b], weights[3 * a + b][:, part], value)
                columns_ref[a, pl.ds(base, step), part] = value.astype(BF16)
        return carry

    lax.fori_loop(0, width // step, chunk, 0)


def row_stencil(columns_ref, row_of, r):
    total = None
    for a in range(3):
        keep = jnp.where(row_of == r - a + 1, 1.0, 0.0).astype(BF16)
        term = columns_ref[a] * keep
        total = term if total is None else total + term
    return total


def edge_weights(cells_ref, weight_ref, rows, width):
    lines = BLOCKS * EDGE
    obs = cells_ref.shape[1]
    row, col = split_cells(cells_ref[...], width)
    line = iota((lines, obs), 0)
    block = lax.shift_right_logical(line, 4)
    k = line & (EDGE - 1)
    none = -99
    west = k >= rows
    col_at = jnp.where(west, -1, width)
    row_at = jnp.where(west, k - rows, k)
    row_at = jnp.where(block == 1, jnp.where(row_at == rows - 1, -1, none), row_at)
    row_at = jnp.where(block == 2, jnp.where(row_at == 0, rows, none), row_at)
    total = jnp.zeros((lines, obs), F32)
    for a in range(3):
        for b in range(3):
            hit = (row_at == row + (a - 1)) & (col_at == col + (b - 1))
            total = total + jnp.where(hit, weight_ref[3 * a + b], 0.0)
    return total.astype(BF16)


def pack_kernel(dims, profiles_ref, mid_ref, top_ref, bottom_ref, edge_ref, wide_ref):
    levels, rows, width, pad = dims
    for lane in range(0, width, LANES):
        part = profiles_ref[:, :, lane : lane + LANES]
        wide_ref[lane // LANES] = part.astype(F32).reshape(2 * levels * rows, LANES)
    edges = jnp.zeros((EDGE, 2 * pad), F32)
    k = iota((EDGE, LANES), 0)
    at_lane = iota((EDGE, LANES), 1)
    for r in range(rows):
        out = top_ref if r == 0 else bottom_ref if r == rows - 1 else mid_ref.at[r - 1]
        for v in range(2):
            for lane in range(0, width, LANES):
                value = wide_ref[lane // LANES, pl.ds(v * levels * rows + r, levels, stride=rows), :]
                value = jnp.concatenate([value, jnp.zeros((pad - levels, LANES), F32)], axis=0)
                out[v * pad : (v + 1) * pad, lane : lane + LANES] = value.astype(BF16)
        west = jnp.where((k == r) & (at_lane == 0), 1.0, 0.0).astype(BF16)
        east = jnp.where((k == rows + r) & (at_lane == LANES - 1), 1.0, 0.0).astype(BF16)
        edges = edges + dot(west, out[:, :LANES], NT) + dot(east, out[:, width - LANES :], NT)
    edge_ref[...] = jnp.zeros(edge_ref.shape, BF16)
    edge_ref[:, : 2 * pad] = edges.astype(BF16)


def blend_kernel(rows, cot_ref, from_west_ref, from_east_ref, send_ref, edge_ref):
    proc = cot_ref.shape[1]
    west = iota(edge_ref.shape, 0) >= rows
    edge = jnp.where(west, from_west_ref[...].astype(F32), from_east_ref[...].astype(F32)).astype(BF16)
    edge_ref[...] = edge
    cot = cot_ref[0].astype(BF16)

    def share(s, carry):
        send_ref[s, 0:proc, :] = cot
        for t in range(edge.shape[1] // LANES):
            send_ref[s, proc + EDGE * t : proc + EDGE * (t + 1), :] = edge[:, t * LANES : (t + 1) * LANES]
        return carry

    lax.fori_loop(0, send_ref.shape[0], share, 0)


def lat_block(ref, proc, side):
    at = lax.axis_index("lat") + side
    valid = (at >= 0) & (at < ref.shape[0])
    at = jnp.where(valid, at, 0)
    keep = jnp.where(valid, 1.0, 0.0)
    parts = [ref[at, proc + EDGE * t : proc + EDGE * (t + 1), :] for t in range((ref.shape[1] - proc) // EDGE)]
    return [part.astype(F32) * keep for part in parts]


def gather_rows(rows, row, columns_ref, mid_ref, top_ref, bottom_ref, field_ref):
    for r in range(rows):
        source = top_ref if r == 0 else bottom_ref if r == rows - 1 else mid_ref.at[r - 1]
        value = dot(source[...], row_stencil(columns_ref, row, r))
        if r == 0:
            field_ref[...] = value
        else:
            field_ref[...] += value


def gather_halo(rows, row, columns_ref, above_ref, below_ref, field_ref):
    field_ref[...] += dot(above_ref[...], row_stencil(columns_ref, row, -1))
    field_ref[...] += dot(below_ref[...], row_stencil(columns_ref, row, rows))


def gather_edges(pad, proc, edge_ref, lat_ref, halo_ref, edge_w, field_ref):
    halo_ref[0:EDGE, :] = edge_ref[...].astype(F32)
    for n, side in enumerate((-1, 1)):
        for t, part in enumerate(lat_block(lat_ref, proc, side)):
            halo_ref[(n + 1) * EDGE : (n + 2) * EDGE, t * LANES : (t + 1) * LANES] = part
    field_ref[...] += dot(halo_ref[:, : 2 * pad].astype(BF16), edge_w, TN)


def departures(batch, proc, dest_ref, lat_ref, cot_rows_ref, cot_t_ref):
    obs = cot_rows_ref.shape[0]
    owned = proc // batch
    for q in range(obs // batch):
        where = dest_ref[0, q]
        slot = jnp.maximum(where, 0)
        lat = lax.div(slot, owned)
        start = pl.multiple_of((slot - lat * owned) * batch, batch)
        value = lat_ref[lat, pl.ds(start, batch), :].astype(F32)
        cot_rows_ref[q * batch : (q + 1) * batch, :] = jnp.where(where >= 0, value, 0.0)
    for lane in range(0, obs, LANES):
        cot_t_ref[:, lane : lane + LANES] = cot_rows_ref[lane : lane + LANES, :].T


def chosen_instruments(batch, obs, instr_ref):
    lane_slot = lax.shift_right_logical(iota((1, obs), 1), batch.bit_length() - 1)
    chosen = jnp.zeros((1, obs), jnp.int32)
    for q in range(obs // batch):
        chosen = jnp.where(lane_slot == q, instr_ref[0, q], chosen)
    return chosen


def turn_absorption(absorb_ref, turned_ref):
    levels, instruments, channels = absorb_ref.shape
    per = LANES // instruments
    for b in range(turned_ref.shape[0]):
        count = min(per, levels - b * per)
        block = absorb_ref[b * per : b * per + count].astype(F32).reshape(count * instruments, channels)
        if count < per:
            block = jnp.concatenate([block, jnp.zeros(((per - count) * instruments, channels), F32)], axis=0)
        turned_ref[b] = block.T


def prepare_levels(pad, field_ref, step_ref, rate_ref):
    step_ref[...] = field_ref[1 : pad + 1, :] - field_ref[0:pad, :]
    rate_ref[...] = -LOG2E * (1.0 + 0.5 * jnp.tanh(field_ref[pad : 2 * pad, :]))


def walk_levels(levels, instruments, chosen, turned_ref, cot_t_ref, rate_ref, step_ref, signal_ref, s_part_ref, r_part_ref):
    channels, obs = cot_t_ref.shape
    groups, padded, _ = s_part_ref.shape
    per = LANES // instruments
    tail = jnp.zeros((groups, padded - levels * 8, LANES), F32)
    s_part_ref[:, levels * 8 :, :] = tail
    r_part_ref[:, levels * 8 :, :] = tail
    for lane in range(0, obs, LANES):
        lanes = slice(lane, lane + LANES)
        group = lane // LANES

        def level(b, row_base, j, rates, steps, cum, signal):
            index = jnp.broadcast_to(chosen[:, lanes] + instruments * j, (8, LANES))
            a = jnp.concatenate(
                [
                    jnp.take_along_axis(turned_ref[b, c : c + 8, :], index, axis=1, mode="promise_in_bounds")
                    for c in range(0, channels, 8)
                ],
                axis=0,
            )
            cot = cot_t_ref[:, lanes]
            cum = cum + a * rates[j : j + 1]
            transmit = jnp.exp2(cum)
            at = pl.ds(pl.multiple_of(row_base + 8 * j, 8), 8)
            r_part_ref[group, at, :] = jnp.sum((cot * signal * a).reshape(channels // 8, 8, LANES), axis=0)
            s_part_ref[group, at, :] = jnp.sum((cot * transmit).reshape(channels // 8, 8, LANES), axis=0)
            signal = signal + transmit * steps[j : j + 1]
            return cum, signal

        def block(b, carry):
            cum, signal = carry
            base = pl.multiple_of(b * per, per)
            rates = rate_ref[pl.ds(base, per), lanes]
            steps = step_ref[pl.ds(base, per), lanes]
            for j in range(per):
                cum, signal = level(b, b * (8 * per), j, rates, steps, cum, signal)
            return cum, signal

        start = jnp.zeros((channels, LANES), F32)
        full = levels // per
        cum, signal = lax.fori_loop(0, full, block, (start, start))
        if levels % per:
            rates = rate_ref[full * per : (full + 1) * per, lanes]
            steps = step_ref[full * per : (full + 1) * per, lanes]
            for j in range(levels % per):
                cum, signal = level(full, full * (8 * per), j, rates, steps, cum, signal)
        signal_ref[:, lanes] = signal


def radiances(batch, proc, dest_ref, signal_ref, field_ref, send_ref):
    obs = signal_ref.shape[1]
    owned = proc // batch
    send_ref[...] = jnp.zeros(send_ref.shape, BF16)
    for lane in range(0, obs, LANES):
        lanes = slice(lane, lane + LANES)
        value = (signal_ref[:, lanes] + field_ref[0:1, lanes]).T.astype(BF16)
        for q in range(LANES // batch):
            where = dest_ref[0, lane // batch + q]

            @pl.when(where >= 0)
            def _():
                lat = lax.div(where, owned)
                start = pl.multiple_of((where - lat * owned) * batch, batch)
                send_ref[lat, pl.ds(start, batch), :] = value[q * batch : (q + 1) * batch, :]


def held_part(levels, pick, absorb_ref, cot_t_ref, signal_ref, r_part_ref):
    channels, obs = cot_t_ref.shape
    instruments = absorb_ref.shape[1]
    held = cot_t_ref[...] * signal_ref[...]
    held_hi = held.astype(BF16)
    held_lo = (held - held_hi.astype(F32)).astype(BF16)

    def contract(l0, count):
        rows_in = absorb_ref[pl.ds(l0, count)].reshape(count * instruments, channels)
        value = dot(rows_in, held_hi) + dot(rows_in, held_lo)
        value = value.reshape(count, instruments, obs) * pick[None]
        value = jnp.sum(value.reshape(count, instruments // 8, 8, obs), axis=1)
        at = pl.ds(pl.multiple_of(l0 * 8, 8), count * 8)
        value = value.reshape(count * 8, obs)
        for lane in range(0, obs, LANES):
            r_part_ref[lane // LANES, at, :] -= value[:, lane : lane + LANES]

    def contract_block(b, carry):
        contract(b * 8, 8)
        return carry

    lax.fori_loop(0, levels // 8, contract_block, 0)
    if levels % 8:
        contract(levels // 8 * 8, levels % 8)


def gradients(pad, s_part_ref, r_part_ref, cot_t_ref, field_ref, shift_ref, grad_ref):
    obs = cot_t_ref.shape[1]
    for lane in range(0, obs, LANES):
        lanes = slice(lane, lane + LANES)
        group = lane // LANES
        s_sum = s_part_ref[group, pl.ds(0, pad, stride=8), :]
        r_sum = r_part_ref[group, pl.ds(0, pad, stride=8), :]
        for k in range(1, 8):
            s_sum = s_sum + s_part_ref[group, pl.ds(k, pad, stride=8), :]
            r_sum = r_sum + r_part_ref[group, pl.ds(k, pad, stride=8), :]
        shift_ref[7:8, lanes] = jnp.sum(cot_t_ref[:, lanes], axis=0, keepdims=True)
        shift_ref[8 : 8 + pad, lanes] = s_sum
        grad_ref[0:pad, lanes] = (shift_ref[7 : 7 + pad, lanes] - s_sum).astype(BF16)
        bent = jnp.tanh(field_ref[pad : 2 * pad, lanes])
        grad_ref[pad : 2 * pad, lanes] = (0.5 * (1.0 - bent * bent) * r_sum).astype(BF16)


def scatter_outside(rows, pad, proc, row, columns_ref, edge_w, grad_ref, above_ref, below_ref, edge_ref, send_ref):
    grad = grad_ref[...]
    above_ref[...] = dot(grad, row_stencil(columns_ref, row, -1), NT).astype(BF16)
    below_ref[...] = dot(grad, row_stencil(columns_ref, row, rows), NT).astype(BF16)
    out = dot(edge_w, grad, NT)
    edge_ref[...] = jnp.zeros(edge_ref.shape, F32)
    edge_ref[:, : 2 * pad] = out
    for n, side in enumerate((-1, 1)):
        at = lax.axis_index("lat") + side

        @pl.when((at >= 0) & (at < send_ref.shape[0]))
        def _():
            for t in range(edge_ref.shape[1] // LANES):
                part = edge_ref[(n + 1) * EDGE : (n + 2) * EDGE, t * LANES : (t + 1) * LANES]
                send_ref[at, proc + EDGE * t : proc + EDGE * (t + 1), :] = part.astype(BF16)


def gather_kernel(
    dims, cells_ref, weight_ref, absorb_ref, mid_ref, top_ref, bottom_ref, field_ref, turned_ref, columns_ref
):
    rows, width = dims
    fill_columns(cells_ref, weight_ref, columns_ref)
    row, _ = split_cells(cells_ref[...], width)
    gather_rows(rows, row, columns_ref, mid_ref, top_ref, bottom_ref, field_ref)
    turn_absorption(absorb_ref, turned_ref)


def transfer_kernel(
    dims,
    cells_ref,
    weight_ref,
    instr_ref,
    dest_ref,
    absorb_ref,
    field_in_ref,
    turned_ref,
    columns_ref,
    above_ref,
    below_ref,
    edge_ref,
    lat_ref,
    grad_ref,
    grad_above_ref,
    grad_below_ref,
    grad_edge_ref,
    send_ref,
    halo_ref,
    field_ref,
    rate_ref,
    step_ref,
    cot_rows_ref,
    cot_t_ref,
    signal_ref,
    s_part_ref,
    r_part_ref,
    shift_ref,
):
    levels, rows, width, pad, batch, proc = dims
    obs = cells_ref.shape[1]
    instruments = absorb_ref.shape[1]
    row, _ = split_cells(cells_ref[...], width)
    edge_w = edge_weights(cells_ref, weight_ref, rows, width)
    field_ref[...] = field_in_ref[...]
    gather_halo(rows, row, columns_ref, above_ref, below_ref, field_ref)
    gather_edges(pad, proc, edge_ref, lat_ref, halo_ref, edge_w, field_ref)
    departures(batch, proc, dest_ref, lat_ref, cot_rows_ref, cot_t_ref)
    chosen = chosen_instruments(batch, obs, instr_ref)
    prepare_levels(pad, field_ref, step_ref, rate_ref)
    walk_levels(
        levels, instruments, chosen, turned_ref, cot_t_ref, rate_ref, step_ref, signal_ref, s_part_ref, r_part_ref
    )
    radiances(batch, proc, dest_ref, signal_ref, field_ref, send_ref)
    pick = jnp.where(iota((instruments, obs), 0) == chosen, 1.0, 0.0)
    held_part(levels, pick, absorb_ref, cot_t_ref, signal_ref, r_part_ref)
    gradients(pad, s_part_ref, r_part_ref, cot_t_ref, field_ref, shift_ref, grad_ref)
    scatter_outside(
        rows, pad, proc, row, columns_ref, edge_w, grad_ref, grad_above_ref, grad_below_ref, halo_ref, send_ref
    )
    grad_edge_ref[...] = halo_ref[0:EDGE, :].astype(BF16)


def corner_kernel(proc, edge_ref, lat_ref, out_ref):
    ups, downs = lat_block(lat_ref, proc, -1), lat_block(lat_ref, proc, 1)
    for t in range(edge_ref.shape[1] // LANES):
        lanes = slice(t * LANES, (t + 1) * LANES)
        out_ref[:, lanes] = (edge_ref[:, lanes].astype(F32) + ups[t] + downs[t]).astype(BF16)


def scatter_kernel(
    dims,
    cells_ref,
    columns_ref,
    grad_ref,
    from_above_ref,
    from_below_ref,
    from_west_ref,
    from_east_ref,
    lat_ref,
    out_ref,
    rad_out_ref,
    halo_ref,
    wide_ref,
):
    levels, rows, width, pad, proc = dims
    rad_out_ref[...] = jnp.sum(lat_ref[:, 0:proc, :].astype(F32), axis=0)[None]
    row, _ = split_cells(cells_ref[...], width)
    west = iota(halo_ref.shape, 0) < rows
    halo_ref[...] = jnp.where(west, from_west_ref[...].astype(F32), from_east_ref[...].astype(F32))
    edges = halo_ref[:, : 2 * pad].T.astype(BF16)
    k = iota((EDGE, LANES), 0)
    at_lane = iota((EDGE, LANES), 1)
    for r in range(rows):
        value = dot(grad_ref[...], row_stencil(columns_ref, row, r), NT)
        if r == 0:
            value = value + from_above_ref[...].astype(F32)
        if r == rows - 1:
            value = value + from_below_ref[...].astype(F32)
        first_at = jnp.where((k == r) & (at_lane == 0), 1.0, 0.0).astype(BF16)
        last_at = jnp.where((k == rows + r) & (at_lane == LANES - 1), 1.0, 0.0).astype(BF16)
        first = value[:, :LANES] + dot(edges, first_at)
        last = value[:, width - LANES :] + dot(edges, last_at)
        value = jnp.concatenate([first, value[:, LANES : width - LANES], last], axis=1)
        for v in range(2):
            at = pl.ds(v * levels * rows + r, levels, stride=rows)
            for lane in range(0, width, LANES):
                wide_ref[lane // LANES, at, :] = value[v * pad : v * pad + levels, lane : lane + LANES]
    for lane in range(0, width, LANES):
        out_ref[:, lane : lane + LANES] = wide_ref[lane // LANES]


def per_device(profiles, obs_cell, obs_weight, batch_instr, batch_dest, absorption, cotangent):
    n_lat, n_lon = lax.axis_size("lat"), lax.axis_size("lon")
    levels, rows, width = profiles.shape[1:]
    instruments, channels, _ = absorption.shape
    obs = obs_cell.shape[1]
    slots = batch_dest.shape[1]
    batch = obs // slots
    proc = cotangent.shape[1]
    pad = round_up(levels, 16)
    feat = round_up(2 * pad, LANES)
    lat_rows = proc + EDGE * (feat // LANES)
    blocks = -(-levels * instruments // LANES)
    up = [(i, i + 1) for i in range(n_lat - 1)]
    down = [(b, a) for a, b in up]
    east = [(j, j + 1) for j in range(n_lon - 1)]
    west = [(b, a) for a, b in east]
    shape = jax.ShapeDtypeStruct
    row_shape = shape((2 * pad, width), BF16)
    edge_shape = shape((EDGE, feat), BF16)
    lat_shape = shape((n_lat, lat_rows, channels), BF16)
    absorb = jnp.transpose(absorption, (2, 0, 1))

    mid, top, bottom, edge = pl.pallas_call(
        functools.partial(pack_kernel, (levels, rows, width, pad)),
        out_shape=(shape((rows - 2, 2 * pad, width), BF16), row_shape, row_shape, edge_shape),
        in_specs=[VMEM],
        out_specs=(VMEM,) * 4,
        scratch_shapes=[pltpu.VMEM((width // LANES, 2 * levels * rows, LANES), F32)],
        compiler_params=params(),
        name="pack",
    )(profiles.reshape(2 * levels, rows, width))

    from_west = lax.ppermute(edge, "lon", east)
    from_east = lax.ppermute(edge, "lon", west)
    above = lax.ppermute(bottom, "lat", up)
    below = lax.ppermute(top, "lat", down)

    lat_send, side = pl.pallas_call(
        functools.partial(blend_kernel, rows),
        out_shape=(lat_shape, edge_shape),
        in_specs=[VMEM] * 3,
        out_specs=(VMEM,) * 2,
        compiler_params=params(),
        name="blend",
    )(cotangent, from_west, from_east)
    lat_in = lax.all_to_all(lat_send, "lat", 0, 0, tiled=True)

    field, turned, columns = pl.pallas_call(
        functools.partial(gather_kernel, (rows, width)),
        out_shape=(
            shape((2 * pad, obs), F32),
            shape((blocks, channels, LANES), F32),
            shape((3, width, obs), BF16),
        ),
        in_specs=[VMEM] * 6,
        out_specs=(VMEM,) * 3,
        compiler_params=params(),
        name="gather",
    )(obs_cell, obs_weight, absorb, mid, top, bottom)

    grad, grad_above, grad_below, grad_edge, lat_back = pl.pallas_call(
        functools.partial(transfer_kernel, (levels, rows, width, pad, batch, proc)),
        out_shape=(shape((2 * pad, obs), BF16), row_shape, row_shape, edge_shape, lat_shape),
        in_specs=[VMEM, VMEM, SMEM, SMEM] + [VMEM] * 8,
        out_specs=(VMEM,) * 5,
        scratch_shapes=[
            pltpu.VMEM((BLOCKS * EDGE, feat), F32),
            pltpu.VMEM((2 * pad, obs), F32),
            pltpu.VMEM((pad, obs), F32),
            pltpu.VMEM((pad, obs), F32),
            pltpu.VMEM((obs, channels), F32),
            pltpu.VMEM((channels, obs), F32),
            pltpu.VMEM((channels, obs), F32),
            pltpu.VMEM((obs // LANES, pad * 8, LANES), F32),
            pltpu.VMEM((obs // LANES, pad * 8, LANES), F32),
            pltpu.VMEM((pad + 8, obs), F32),
        ],
        compiler_params=params(),
        name="transfer",
    )(
        obs_cell,
        obs_weight,
        batch_instr,
        batch_dest,
        absorb,
        field,
        turned,
        columns,
        above,
        below,
        side,
        lat_in,
    )

    from_below = lax.ppermute(grad_above, "lat", down)
    from_above = lax.ppermute(grad_below, "lat", up)
    lat_got = lax.all_to_all(lat_back, "lat", 0, 0, tiled=True)
    grad_side = pl.pallas_call(
        functools.partial(corner_kernel, proc),
        out_shape=edge_shape,
        in_specs=[VMEM] * 2,
        out_specs=VMEM,
        compiler_params=params(),
        name="corner",
    )(grad_edge, lat_got)
    grad_from_west = lax.ppermute(grad_side, "lon", east)
    grad_from_east = lax.ppermute(grad_side, "lon", west)

    gradient, radiance = pl.pallas_call(
        functools.partial(scatter_kernel, (levels, rows, width, pad, proc)),
        out_shape=(
            shape((2 * levels * rows, width), F32),
            shape((1, proc, channels), F32),
        ),
        in_specs=[VMEM] * 8,
        out_specs=(VMEM,) * 2,
        scratch_shapes=[
            pltpu.VMEM((EDGE, feat), F32),
            pltpu.VMEM((width // LANES, 2 * levels * rows, LANES), F32),
        ],
        compiler_params=params(),
        name="scatter",
    )(obs_cell, columns, grad, from_above, from_below, grad_from_west, grad_from_east, lat_got)
    return radiance, gradient.reshape(2, levels, rows, width)


def solution(mesh):
    placed = (
        P("groups", None, "lat", "lon"),
        P(("groups", "lon"), "lat"),
        P("groups", "lon", "lat"),
        P(("groups", "lon"), "lat"),
        P(("groups", "lon"), "lat"),
        P(),
        P(("groups", "lon"), "lat", None),
    )
    return jax.shard_map(
        per_device,
        mesh=mesh,
        in_specs=placed,
        out_specs=(P(("groups", "lon"), "lat", None), P("groups", None, "lat", "lon")),
        check_vma=False,
    )
```

```python
import functools

import jax
import jax.numpy as jnp
from jax import lax
from jax.experimental import pallas as pl
from jax.experimental.pallas import tpu as pltpu
from jax.sharding import PartitionSpec as P

F32 = jnp.float32
BF16 = jnp.bfloat16
LOG2E = 1.4426950408889634
LANES = 128
EDGE = 16
BLOCKS = 2
VMEM = pl.BlockSpec(memory_space=pltpu.VMEM)
SMEM = pl.BlockSpec(memory_space=pltpu.SMEM)
HBM = pl.BlockSpec(memory_space=pl.ANY)
SMALL = pl.CostEstimate(flops=1000, bytes_accessed=1000, transcendentals=0)
NN = (((1,), (0,)), ((), ()))
NT = (((1,), (1,)), ((), ()))
TN = (((0,), (0,)), ((), ()))


def dot(a, b, dims=NN):
    return lax.dot_general(a, b, dims, preferred_element_type=F32)


def round_up(value, unit):
    return -(-value // unit) * unit


def params(mib):
    return pltpu.CompilerParams(vmem_limit_bytes=mib * 1024 * 1024)


def iota(shape, dim):
    return lax.broadcasted_iota(jnp.int32, shape, dim)


def split_cells(cells, width):
    if width & (width - 1) == 0:
        return lax.shift_right_logical(cells, width.bit_length() - 1), cells & (width - 1)
    row = lax.div(cells, width)
    return row, cells - row * width


def fill_columns(cells_ref, weight_ref, columns_ref):
    width, obs = columns_ref.shape[1:]
    _, col = split_cells(cells_ref[...], width)
    weights = [weight_ref[k] for k in range(9)]
    step = 32

    def chunk(i, carry):
        base = pl.multiple_of(i * step, step)
        for lane in range(0, obs, LANES):
            part = slice(lane, lane + LANES)
            away = iota((step, LANES), 0) + base - col[:, part]
            hit = [away == b - 1 for b in range(3)]
            for a in range(3):
                value = jnp.zeros((step, LANES), F32)
                for b in range(3):
                    value = jnp.where(hit[b], weights[3 * a + b][:, part], value)
                columns_ref[a, pl.ds(base, step), part] = value.astype(BF16)
        return carry

    lax.fori_loop(0, width // step, chunk, 0)


def row_stencil(columns_ref, row_of, r, part=slice(None)):
    total = None
    for a in range(3):
        keep = jnp.where(row_of == r - a + 1, 1.0, 0.0).astype(BF16)
        term = columns_ref[a, part, :] * keep
        total = term if total is None else total + term
    return total


def edge_weights(cells_ref, weight_ref, rows, width):
    lines = BLOCKS * EDGE
    obs = cells_ref.shape[1]
    row, col = split_cells(cells_ref[...], width)
    line = iota((lines, obs), 0)
    block = lax.shift_right_logical(line, 4)
    k = line & (EDGE - 1)
    none = -99
    west = k >= rows
    col_at = jnp.where(west, -1, width)
    row_at = jnp.where(west, k - rows, k)
    corner = jnp.where(row_at == rows - 1, -1, jnp.where(row_at == 0, rows, none))
    row_at = jnp.where(block == 1, corner, row_at)
    total = jnp.zeros((lines, obs), F32)
    for a in range(3):
        for b in range(3):
            hit = (row_at == row + (a - 1)) & (col_at == col + (b - 1))
            total = total + jnp.where(hit, weight_ref[3 * a + b], 0.0)
    return total.astype(BF16)


def pairs(count, offset, ring):
    swap = [(i, i + 1) for i in range(offset, count - 1, 2)]
    if ring and offset and count % 2 == 0 and count > 2:
        swap.append((0, count - 1))
    return sorted(swap + [(b, a) for a, b in swap])


def pair_place(axis):
    at = lax.axis_index(axis)
    return (at & 1) == 0, at


def pair_rows(rows, count):
    even, at = pair_place("lat")
    below = jnp.where(at < count - 1, rows, -99)
    above = jnp.where(at > 0, -1, -99)
    return jnp.where(even, below, above), jnp.where(even, above, below)


def choose(pred, a, b):
    return jnp.where(pred, a.astype(F32), b.astype(F32))


def from_sides(first, second, count):
    even, at = pair_place("lon")
    west = choose(even, second, first) * jnp.where(at > 0, 1.0, 0.0)
    east = choose(even, first, second) * jnp.where(at < count - 1, 1.0, 0.0)
    return west, east


def pack_kernel(dims, profiles_ref, cot_ref, rows_ref, first_ref, second_ref, edge_ref, send_ref, wide_ref):
    levels, rows, width, pad = dims
    for lane in range(0, width, LANES):
        part = profiles_ref[:, :, lane : lane + LANES]
        wide_ref[lane // LANES] = part.astype(F32).reshape(2 * levels * rows, LANES)
    edges = jnp.zeros((EDGE, 2 * pad), F32)
    k = iota((EDGE, LANES), 0)
    at_lane = iota((EDGE, LANES), 1)
    for r in range(rows):
        out = rows_ref.at[r]
        for v in range(2):
            for lane in range(0, width, LANES):
                value = wide_ref[lane // LANES, pl.ds(v * levels * rows + r, levels, stride=rows), :]
                value = jnp.concatenate([value, jnp.zeros((pad - levels, LANES), F32)], axis=0)
                out[v * pad : (v + 1) * pad, lane : lane + LANES] = value.astype(BF16)
        west = jnp.where((k == r) & (at_lane == 0), 1.0, 0.0).astype(BF16)
        east = jnp.where((k == rows + r) & (at_lane == LANES - 1), 1.0, 0.0).astype(BF16)
        edges = edges + dot(west, out[:, :LANES], NT) + dot(east, out[:, width - LANES :], NT)
    edge_ref[...] = jnp.zeros(edge_ref.shape, BF16)
    edge_ref[:, : 2 * pad] = edges.astype(BF16)
    even, _ = pair_place("lat")
    first_ref[...] = rows_ref[jnp.where(even, rows - 1, 0)]
    second_ref[...] = rows_ref[jnp.where(even, 0, rows - 1)]
    proc = cot_ref.shape[1]
    cot = cot_ref[0].astype(BF16)

    def share(s, carry):
        send_ref[s, 0:proc, :] = cot
        for t in range(edge_ref.shape[1] // LANES):
            send_ref[s, proc + EDGE * t : proc + EDGE * (t + 1), :] = edge_ref[:, t * LANES : (t + 1) * LANES]
        return carry

    lax.fori_loop(0, send_ref.shape[0], share, 0)


def lat_block(ref, proc, side):
    at = lax.axis_index("lat") + side
    valid = (at >= 0) & (at < ref.shape[0])
    at = jnp.where(valid, at, 0)
    keep = jnp.where(valid, 1.0, 0.0)
    parts = [ref[at, proc + EDGE * t : proc + EDGE * (t + 1), :] for t in range((ref.shape[1] - proc) // EDGE)]
    return [part.astype(F32) * keep for part in parts]


def blend_kernel(rows, proc, edge_ref, lat_ref, out_ref):
    k = iota((EDGE, LANES), 0)
    last = (k == rows - 1) | (k == 2 * rows - 1)
    first = (k == 0) | (k == rows)
    ups, downs = lat_block(lat_ref, proc, -1), lat_block(lat_ref, proc, 1)
    out_ref[0:EDGE, :] = edge_ref[...]
    for t in range(edge_ref.shape[1] // LANES):
        corner = jnp.where(last, ups[t], jnp.where(first, downs[t], 0.0))
        out_ref[EDGE : 2 * EDGE, t * LANES : (t + 1) * LANES] = corner.astype(BF16)


def gather_rows(rows, row, columns_ref, rows_ref, field_ref):
    for r in range(rows):
        value = dot(rows_ref[r], row_stencil(columns_ref, row, r))
        if r == 0:
            field_ref[...] = value
        else:
            field_ref[...] += value


def gather_halo(halo_rows, row, columns_ref, first_ref, second_ref, field_ref):
    field_ref[...] += dot(first_ref[...], row_stencil(columns_ref, row, halo_rows[0]))
    field_ref[...] += dot(second_ref[...], row_stencil(columns_ref, row, halo_rows[1]))


def gather_edges(rows, pad, n_lon, first_ref, second_ref, halo_ref, edge_w, field_ref):
    west = (iota(halo_ref.shape, 0) & (EDGE - 1)) >= rows
    from_west, from_east = from_sides(first_ref[...], second_ref[...], n_lon)
    halo_ref[...] = jnp.where(west, from_west, from_east)
    field_ref[...] += dot(halo_ref[:, : 2 * pad].astype(BF16), edge_w, TN)


def departures(batch, proc, dest_ref, lat_ref, cot_rows_ref, cot_t_ref):
    obs = cot_rows_ref.shape[0]
    owned = proc // batch
    for q in range(obs // batch):
        where = dest_ref[0, q]
        slot = jnp.maximum(where, 0)
        lat = lax.div(slot, owned)
        start = pl.multiple_of((slot - lat * owned) * batch, batch)
        value = lat_ref[lat, pl.ds(start, batch), :].astype(F32)
        cot_rows_ref[q * batch : (q + 1) * batch, :] = jnp.where(where >= 0, value, 0.0)
    for lane in range(0, obs, LANES):
        cot_t_ref[:, lane : lane + LANES] = cot_rows_ref[lane : lane + LANES, :].T


def chosen_instruments(batch, obs, instr_ref):
    lane_slot = lax.shift_right_logical(iota((1, obs), 1), batch.bit_length() - 1)
    chosen = jnp.zeros((1, obs), jnp.int32)
    for q in range(obs // batch):
        chosen = jnp.where(lane_slot == q, instr_ref[0, q], chosen)
    return chosen


def turn_absorption(absorb_ref, turned_ref):
    levels, instruments, channels = absorb_ref.shape
    per = LANES // instruments
    for b in range(turned_ref.shape[0]):
        count = min(per, levels - b * per)
        block = absorb_ref[b * per : b * per + count].astype(F32).reshape(count * instruments, channels)
        if count < per:
            block = jnp.concatenate([block, jnp.zeros(((per - count) * instruments, channels), F32)], axis=0)
        turned_ref[b] = block.T


def prepare_levels(pad, field_ref, step_ref, rate_ref):
    step_ref[...] = field_ref[1 : pad + 1, :] - field_ref[0:pad, :]
    rate_ref[...] = -LOG2E * (1.0 + 0.5 * jnp.tanh(field_ref[pad : 2 * pad, :]))


def walk_levels(levels, instruments, chosen, turned_ref, cot_t_ref, rate_ref, step_ref, signal_ref, s_part_ref, r_part_ref):
    channels, obs = cot_t_ref.shape
    groups, padded, _ = s_part_ref.shape
    per = LANES // instruments
    tail = jnp.zeros((groups, padded - levels * 8, LANES), F32)
    s_part_ref[:, levels * 8 :, :] = tail
    r_part_ref[:, levels * 8 :, :] = tail
    for lane in range(0, obs, LANES):
        lanes = slice(lane, lane + LANES)
        group = lane // LANES

        def level(b, row_base, j, rates, steps, cum, signal):
            index = jnp.broadcast_to(chosen[:, lanes] + instruments * j, (8, LANES))
            a = jnp.concatenate(
                [
                    jnp.take_along_axis(turned_ref[b, c : c + 8, :], index, axis=1, mode="promise_in_bounds")
                    for c in range(0, channels, 8)
                ],
                axis=0,
            )
            cot = cot_t_ref[:, lanes]
            cum = cum + a * rates[j : j + 1]
            transmit = jnp.exp2(cum)
            at = pl.ds(pl.multiple_of(row_base + 8 * j, 8), 8)
            r_part_ref[group, at, :] = jnp.sum((cot * signal * a).reshape(channels // 8, 8, LANES), axis=0)
            s_part_ref[group, at, :] = jnp.sum((cot * transmit).reshape(channels // 8, 8, LANES), axis=0)
            signal = signal + transmit * steps[j : j + 1]
            return cum, signal

        def block(b, carry):
            cum, signal = carry
            base = pl.multiple_of(b * per, per)
            rates = rate_ref[pl.ds(base, per), lanes]
            steps = step_ref[pl.ds(base, per), lanes]
            for j in range(per):
                cum, signal = level(b, b * (8 * per), j, rates, steps, cum, signal)
            return cum, signal

        start = jnp.zeros((channels, LANES), F32)
        full = levels // per
        cum, signal = lax.fori_loop(0, full, block, (start, start))
        if levels % per:
            rates = rate_ref[full * per : (full + 1) * per, lanes]
            steps = step_ref[full * per : (full + 1) * per, lanes]
            for j in range(levels % per):
                cum, signal = level(full, full * (8 * per), j, rates, steps, cum, signal)
        signal_ref[:, lanes] = signal


def radiances(batch, proc, dest_ref, signal_ref, field_ref, send_ref):
    obs = signal_ref.shape[1]
    owned = proc // batch
    send_ref[...] = jnp.zeros(send_ref.shape, BF16)
    for lane in range(0, obs, LANES):
        lanes = slice(lane, lane + LANES)
        value = (signal_ref[:, lanes] + field_ref[0:1, lanes]).T.astype(BF16)
        for q in range(LANES // batch):
            where = dest_ref[0, lane // batch + q]

            @pl.when(where >= 0)
            def _():
                lat = lax.div(where, owned)
                start = pl.multiple_of((where - lat * owned) * batch, batch)
                send_ref[lat, pl.ds(start, batch), :] = value[q * batch : (q + 1) * batch, :]


def held_part(levels, pick, absorb_ref, cot_t_ref, signal_ref, r_part_ref):
    channels, obs = cot_t_ref.shape
    instruments = absorb_ref.shape[1]
    held = cot_t_ref[...] * signal_ref[...]
    held_hi = held.astype(BF16)
    held_lo = (held - held_hi.astype(F32)).astype(BF16)
    halves = jnp.concatenate([held_hi, held_lo], axis=0)

    def contract(l0, count):
        rows_in = absorb_ref[pl.ds(l0, count)].reshape(count * instruments, channels)
        value = dot(jnp.concatenate([rows_in, rows_in], axis=1), halves)
        value = value.reshape(count, instruments, obs) * pick[None]
        value = jnp.sum(value.reshape(count, instruments // 8, 8, obs), axis=1)
        at = pl.ds(pl.multiple_of(l0 * 8, 8), count * 8)
        value = value.reshape(count * 8, obs)
        for lane in range(0, obs, LANES):
            r_part_ref[lane // LANES, at, :] -= value[:, lane : lane + LANES]

    step = 16

    def contract_block(b, carry):
        contract(b * step, step)
        return carry

    lax.fori_loop(0, levels // step, contract_block, 0)
    if levels % step:
        contract(levels // step * step, levels % step)


def gradients(pad, s_part_ref, r_part_ref, cot_t_ref, field_ref, shift_ref, grad_ref):
    obs = cot_t_ref.shape[1]
    for lane in range(0, obs, LANES):
        lanes = slice(lane, lane + LANES)
        group = lane // LANES
        s_sum = s_part_ref[group, pl.ds(0, pad, stride=8), :]
        r_sum = r_part_ref[group, pl.ds(0, pad, stride=8), :]
        for k in range(1, 8):
            s_sum = s_sum + s_part_ref[group, pl.ds(k, pad, stride=8), :]
            r_sum = r_sum + r_part_ref[group, pl.ds(k, pad, stride=8), :]
        shift_ref[7:8, lanes] = jnp.sum(cot_t_ref[:, lanes], axis=0, keepdims=True)
        shift_ref[8 : 8 + pad, lanes] = s_sum
        grad_ref[0:pad, lanes] = (shift_ref[7 : 7 + pad, lanes] - s_sum).astype(BF16)
        bent = jnp.tanh(field_ref[pad : 2 * pad, lanes])
        grad_ref[pad : 2 * pad, lanes] = (0.5 * (1.0 - bent * bent) * r_sum).astype(BF16)


def scatter_outside(
    rows, pad, proc, halo_rows, row, columns_ref, edge_w, grad_ref, first_ref, second_ref, edge_ref, send_ref
):
    grad = grad_ref[...]
    first_ref[...] = dot(grad, row_stencil(columns_ref, row, halo_rows[0]), NT).astype(BF16)
    second_ref[...] = dot(grad, row_stencil(columns_ref, row, halo_rows[1]), NT).astype(BF16)
    out = dot(edge_w, grad, NT)
    edge_ref[...] = jnp.zeros(edge_ref.shape, F32)
    edge_ref[:, : 2 * pad] = out
    k = iota((EDGE, LANES), 0)
    last = (k == rows - 1) | (k == 2 * rows - 1)
    first = (k == 0) | (k == rows)
    for side, mine in ((-1, last), (1, first)):
        at = lax.axis_index("lat") + side

        @pl.when((at >= 0) & (at < send_ref.shape[0]))
        def _():
            for t in range(edge_ref.shape[1] // LANES):
                part = edge_ref[EDGE : 2 * EDGE, t * LANES : (t + 1) * LANES]
                part = jnp.where(mine, part, 0.0).astype(BF16)
                send_ref[at, proc + EDGE * t : proc + EDGE * (t + 1), :] = part


def transfer_kernel(
    dims,
    cells_ref,
    weight_ref,
    instr_ref,
    dest_ref,
    absorb_ref,
    side_first_ref,
    side_second_ref,
    rows_hbm,
    row_first_hbm,
    row_second_hbm,
    lat_hbm,
    grad_ref,
    grad_first_ref,
    grad_second_ref,
    grad_edge_ref,
    send_ref,
    columns_ref,
    turned_ref,
    halo_ref,
    field_ref,
    rate_ref,
    step_ref,
    cot_rows_ref,
    cot_t_ref,
    signal_ref,
    s_part_ref,
    r_part_ref,
    shift_ref,
    rows_ref,
    row_first_ref,
    row_second_ref,
    lat_ref,
    sems,
):
    levels, rows, width, pad, batch, proc, n_lat, n_lon = dims
    moves = [
        pltpu.make_async_copy(source, target, sems.at[k])
        for k, (source, target) in enumerate(
            (
                (rows_hbm, rows_ref),
                (row_first_hbm, row_first_ref),
                (row_second_hbm, row_second_ref),
                (lat_hbm, lat_ref),
            )
        )
    ]
    for move in moves:
        move.start()
    obs = cells_ref.shape[1]
    instruments = absorb_ref.shape[1]
    fill_columns(cells_ref, weight_ref, columns_ref)
    row, _ = split_cells(cells_ref[...], width)
    halo_rows = pair_rows(rows, n_lat)
    edge_w = edge_weights(cells_ref, weight_ref, rows, width)
    turn_absorption(absorb_ref, turned_ref)
    moves[0].wait()
    gather_rows(rows, row, columns_ref, rows_ref, field_ref)
    for move in moves[1:]:
        move.wait()
    gather_halo(halo_rows, row, columns_ref, row_first_ref, row_second_ref, field_ref)
    gather_edges(rows, pad, n_lon, side_first_ref, side_second_ref, halo_ref, edge_w, field_ref)
    departures(batch, proc, dest_ref, lat_ref, cot_rows_ref, cot_t_ref)
    chosen = chosen_instruments(batch, obs, instr_ref)
    prepare_levels(pad, field_ref, step_ref, rate_ref)
    walk_levels(
        levels, instruments, chosen, turned_ref, cot_t_ref, rate_ref, step_ref, signal_ref, s_part_ref, r_part_ref
    )
    radiances(batch, proc, dest_ref, signal_ref, field_ref, send_ref)
    pick = jnp.where(iota((instruments, obs), 0) == chosen, 1.0, 0.0)
    held_part(levels, pick, absorb_ref, cot_t_ref, signal_ref, r_part_ref)
    gradients(pad, s_part_ref, r_part_ref, cot_t_ref, field_ref, shift_ref, grad_ref)
    scatter_outside(
        rows,
        pad,
        proc,
        halo_rows,
        row,
        columns_ref,
        edge_w,
        grad_ref,
        grad_first_ref,
        grad_second_ref,
        halo_ref,
        send_ref,
    )
    grad_edge_ref[...] = halo_ref[0:EDGE, :].astype(BF16)


def corner_kernel(proc, edge_ref, lat_ref, out_ref):
    ups, downs = lat_block(lat_ref, proc, -1), lat_block(lat_ref, proc, 1)
    for t in range(edge_ref.shape[1] // LANES):
        lanes = slice(t * LANES, (t + 1) * LANES)
        out_ref[:, lanes] = (edge_ref[:, lanes].astype(F32) + ups[t] + downs[t]).astype(BF16)


def scatter_kernel(
    dims,
    cells_ref,
    weight_ref,
    grad_ref,
    row_first_ref,
    row_second_ref,
    side_first_ref,
    side_second_ref,
    lat_ref,
    out_ref,
    rad_out_ref,
    columns_ref,
    halo_ref,
    wide_ref,
    sems,
):
    levels, rows, width, pad, proc, n_lat, n_lon = dims
    fill_columns(cells_ref, weight_ref, columns_ref)
    even, at_lat = pair_place("lat")
    inside = jnp.where(at_lat > 0, 1.0, 0.0), jnp.where(at_lat < n_lat - 1, 1.0, 0.0)
    rad_out_ref[...] = jnp.sum(lat_ref[:, 0:proc, :].astype(F32), axis=0)[None]
    row, _ = split_cells(cells_ref[...], width)
    west = iota(halo_ref.shape, 0) < rows
    from_west, from_east = from_sides(side_first_ref[...], side_second_ref[...], n_lon)
    halo_ref[...] = jnp.where(west, from_west, from_east)
    edges = halo_ref[:, : 2 * pad].T.astype(BF16)
    k = iota((EDGE, LANES), 0)
    at_lane = iota((EDGE, LANES), 1)
    moves = []
    half = 2 * LANES if width % (2 * LANES) == 0 else LANES
    for start in range(0, width, half):
        part = slice(start, start + half)
        for r in range(rows):
            value = dot(grad_ref[...], row_stencil(columns_ref, row, r, part), NT)
            if r == 0:
                value = value + choose(even, row_second_ref[:, part], row_first_ref[:, part]) * inside[0]
            if r == rows - 1:
                value = value + choose(even, row_first_ref[:, part], row_second_ref[:, part]) * inside[1]
            for lane in range(start, start + half, LANES):
                piece = value[:, lane - start : lane - start + LANES]
                if lane == 0:
                    piece = piece + dot(edges, jnp.where((k == r) & (at_lane == 0), 1.0, 0.0).astype(BF16))
                if lane + LANES == width:
                    last_at = jnp.where((k == rows + r) & (at_lane == LANES - 1), 1.0, 0.0).astype(BF16)
                    piece = piece + dot(edges, last_at)
                for v in range(2):
                    at = pl.ds(v * levels * rows + r, levels, stride=rows)
                    wide_ref[lane // LANES, at, :] = piece[v * pad : v * pad + levels, :]
        for lane in range(start, start + half, LANES):
            t = lane // LANES
            move = pltpu.make_async_copy(wide_ref.at[t], out_ref.at[:, lane : lane + LANES], sems.at[t])
            move.start()
            moves.append(move)
    for move in moves:
        move.wait()


def per_device(profiles, obs_cell, obs_weight, batch_instr, batch_dest, absorption, cotangent):
    n_lat, n_lon = lax.axis_size("lat"), lax.axis_size("lon")
    levels, rows, width = profiles.shape[1:]
    instruments, channels, _ = absorption.shape
    obs = obs_cell.shape[1]
    slots = batch_dest.shape[1]
    batch = obs // slots
    proc = cotangent.shape[1]
    pad = round_up(levels, 16)
    feat = round_up(2 * pad, LANES)
    lat_rows = proc + EDGE * (feat // LANES)
    blocks = -(-levels * instruments // LANES)
    lat_pairs = [pairs(n_lat, offset, False) for offset in (0, 1)]
    lon_pairs = [pairs(n_lon, offset, True) for offset in (0, 1)]
    shape = jax.ShapeDtypeStruct
    row_shape = shape((2 * pad, width), BF16)
    edge_shape = shape((EDGE, feat), BF16)
    lat_shape = shape((n_lat, lat_rows, channels), BF16)
    absorb = jnp.transpose(absorption, (2, 0, 1))

    row_data, row_first, row_second, edge, lat_send = pl.pallas_call(
        functools.partial(pack_kernel, (levels, rows, width, pad)),
        out_shape=(shape((rows, 2 * pad, width), BF16), row_shape, row_shape, edge_shape, lat_shape),
        in_specs=[VMEM] * 2,
        out_specs=(VMEM,) * 5,
        scratch_shapes=[pltpu.VMEM((width // LANES, 2 * levels * rows, LANES), F32)],
        compiler_params=params(12),
        name="pack",
    )(profiles.reshape(2 * levels, rows, width), cotangent)

    lat_in = lax.all_to_all(lat_send, "lat", 0, 0, tiled=True)
    row_first = lax.ppermute(row_first, "lat", lat_pairs[0])
    row_second = lax.ppermute(row_second, "lat", lat_pairs[1])

    side = pl.pallas_call(
        functools.partial(blend_kernel, rows, proc),
        out_shape=shape((BLOCKS * EDGE, feat), BF16),
        in_specs=[VMEM] * 2,
        out_specs=VMEM,
        compiler_params=params(4),
        cost_estimate=SMALL,
        name="blend",
    )(edge, lat_in)
    side_first = lax.ppermute(side, "lon", lon_pairs[0])
    side_second = lax.ppermute(side, "lon", lon_pairs[1])

    grad, grad_first, grad_second, grad_edge, lat_back = pl.pallas_call(
        functools.partial(transfer_kernel, (levels, rows, width, pad, batch, proc, n_lat, n_lon)),
        out_shape=(shape((2 * pad, obs), BF16), row_shape, row_shape, edge_shape, lat_shape),
        in_specs=[VMEM, VMEM, SMEM, SMEM] + [VMEM] * 3 + [HBM] * 4,
        out_specs=(VMEM,) * 5,
        scratch_shapes=[
            pltpu.VMEM((3, width, obs), BF16),
            pltpu.VMEM((blocks, channels, LANES), F32),
            pltpu.VMEM((BLOCKS * EDGE, feat), F32),
            pltpu.VMEM((2 * pad, obs), F32),
            pltpu.VMEM((pad, obs), F32),
            pltpu.VMEM((pad, obs), F32),
            pltpu.VMEM((obs, channels), F32),
            pltpu.VMEM((channels, obs), F32),
            pltpu.VMEM((channels, obs), F32),
            pltpu.VMEM((obs // LANES, pad * 8, LANES), F32),
            pltpu.VMEM((obs // LANES, pad * 8, LANES), F32),
            pltpu.VMEM((pad + 8, obs), F32),
            pltpu.VMEM((rows, 2 * pad, width), BF16),
            pltpu.VMEM(row_shape.shape, BF16),
            pltpu.VMEM(row_shape.shape, BF16),
            pltpu.VMEM(lat_shape.shape, BF16),
            pltpu.SemaphoreType.DMA((4,)),
        ],
        compiler_params=params(56),
        name="transfer",
    )(
        obs_cell,
        obs_weight,
        batch_instr,
        batch_dest,
        absorb,
        side_first,
        side_second,
        row_data,
        row_first,
        row_second,
        lat_in,
    )

    grad_first = lax.ppermute(grad_first, "lat", lat_pairs[0])
    grad_second = lax.ppermute(grad_second, "lat", lat_pairs[1])
    lat_got = lax.all_to_all(lat_back, "lat", 0, 0, tiled=True)
    grad_side = pl.pallas_call(
        functools.partial(corner_kernel, proc),
        out_shape=edge_shape,
        in_specs=[VMEM] * 2,
        out_specs=VMEM,
        compiler_params=params(4),
        cost_estimate=SMALL,
        name="corner",
    )(grad_edge, lat_got)
    grad_side_first = lax.ppermute(grad_side, "lon", lon_pairs[0])
    grad_side_second = lax.ppermute(grad_side, "lon", lon_pairs[1])

    gradient, radiance = pl.pallas_call(
        functools.partial(scatter_kernel, (levels, rows, width, pad, proc, n_lat, n_lon)),
        out_shape=(
            shape((2 * levels * rows, width), F32),
            shape((1, proc, channels), F32),
        ),
        in_specs=[VMEM] * 8,
        out_specs=(HBM, VMEM),
        scratch_shapes=[
            pltpu.VMEM((3, width, obs), BF16),
            pltpu.VMEM((EDGE, feat), F32),
            pltpu.VMEM((width // LANES, 2 * levels * rows, LANES), F32),
            pltpu.SemaphoreType.DMA((width // LANES,)),
        ],
        compiler_params=params(20),
        name="scatter",
    )(obs_cell, obs_weight, grad, grad_first, grad_second, grad_side_first, grad_side_second, lat_got)
    return radiance, gradient.reshape(2, levels, rows, width)


def solution(mesh):
    placed = (
        P("groups", None, "lat", "lon"),
        P(("groups", "lon"), "lat"),
        P("groups", "lon", "lat"),
        P(("groups", "lon"), "lat"),
        P(("groups", "lon"), "lat"),
        P(),
        P(("groups", "lon"), "lat", None),
    )
    return jax.shard_map(
        per_device,
        mesh=mesh,
        in_specs=placed,
        out_specs=(P(("groups", "lon"), "lat", None), P("groups", None, "lat", "lon")),
        check_vma=False,
    )
```

```python
import functools

import jax
import jax.numpy as jnp
from jax import lax
from jax.experimental import pallas as pl
from jax.experimental.pallas import tpu as pltpu
from jax.sharding import PartitionSpec as P

F32 = jnp.float32
BF16 = jnp.bfloat16
LOG2E = 1.4426950408889634
LANES = 128
EDGE = 16
BLOCKS = 2
VMEM = pl.BlockSpec(memory_space=pltpu.VMEM)
SMEM = pl.BlockSpec(memory_space=pltpu.SMEM)
HBM = pl.BlockSpec(memory_space=pltpu.HBM)
SMALL = pl.CostEstimate(flops=1000, bytes_accessed=1000, transcendentals=0)
NN = (((1,), (0,)), ((), ()))
NT = (((1,), (1,)), ((), ()))
TN = (((0,), (0,)), ((), ()))


def dot(a, b, dims=NN):
    return lax.dot_general(a, b, dims, preferred_element_type=F32)


def round_up(value, unit):
    return -(-value // unit) * unit


def params(mib):
    return pltpu.CompilerParams(vmem_limit_bytes=mib * 1024 * 1024)


def iota(shape, dim):
    return lax.broadcasted_iota(jnp.int32, shape, dim)


def split_cells(cells, width):
    if width & (width - 1) == 0:
        return lax.shift_right_logical(cells, width.bit_length() - 1), cells & (width - 1)
    row = lax.div(cells, width)
    return row, cells - row * width


def fill_columns(cells_ref, weight_ref, columns_ref):
    width, obs = columns_ref.shape[1:]
    _, col = split_cells(cells_ref[...], width)
    weights = [weight_ref[k] for k in range(9)]
    step = 32

    def chunk(i, carry):
        base = pl.multiple_of(i * step, step)
        for lane in range(0, obs, LANES):
            part = slice(lane, lane + LANES)
            away = iota((step, LANES), 0) + base - col[:, part]
            hit = [away == b - 1 for b in range(3)]
            for a in range(3):
                value = jnp.zeros((step, LANES), F32)
                for b in range(3):
                    value = jnp.where(hit[b], weights[3 * a + b][:, part], value)
                columns_ref[a, pl.ds(base, step), part] = value.astype(BF16)
        return carry

    lax.fori_loop(0, width // step, chunk, 0)


def row_stencil(columns_ref, row_of, r, part=slice(None)):
    total = None
    for a in range(3):
        keep = jnp.where(row_of == r - a + 1, 1.0, 0.0).astype(BF16)
        term = columns_ref[a, part, :] * keep
        total = term if total is None else total + term
    return total


def edge_weights(cells_ref, weight_ref, rows, width):
    lines = BLOCKS * EDGE
    obs = cells_ref.shape[1]
    row, col = split_cells(cells_ref[...], width)
    line = iota((lines, obs), 0)
    block = lax.shift_right_logical(line, 4)
    k = line & (EDGE - 1)
    none = -99
    west = k >= rows
    col_at = jnp.where(west, -1, width)
    row_at = jnp.where(west, k - rows, k)
    corner = jnp.where(row_at == rows - 1, -1, jnp.where(row_at == 0, rows, none))
    row_at = jnp.where(block == 1, corner, row_at)
    total = jnp.zeros((lines, obs), F32)
    for a in range(3):
        for b in range(3):
            hit = (row_at == row + (a - 1)) & (col_at == col + (b - 1))
            total = total + jnp.where(hit, weight_ref[3 * a + b], 0.0)
    return total.astype(BF16)


def pairs(count, offset, ring):
    swap = [(i, i + 1) for i in range(offset, count - 1, 2)]
    if ring and offset and count % 2 == 0 and count > 2:
        swap.append((0, count - 1))
    return sorted(swap + [(b, a) for a, b in swap])


def pair_place(axis):
    at = lax.axis_index(axis)
    return (at & 1) == 0, at


def pair_rows(rows, count):
    even, at = pair_place("lat")
    below = jnp.where(at < count - 1, rows, -99)
    above = jnp.where(at > 0, -1, -99)
    return jnp.where(even, below, above), jnp.where(even, above, below)


def choose(pred, a, b):
    return jnp.where(pred, a.astype(F32), b.astype(F32))


def from_sides(first, second, count):
    even, at = pair_place("lon")
    west = choose(even, second, first) * jnp.where(at > 0, 1.0, 0.0)
    east = choose(even, first, second) * jnp.where(at < count - 1, 1.0, 0.0)
    return west, east


def copies(pairs_of, sems):
    moves = [pltpu.make_async_copy(source, target, sems.at[k]) for k, (source, target) in enumerate(pairs_of)]
    for move in moves:
        move.start()
    return moves


def load_profiles(profiles_hbm, part_ref, sems):
    tiles = part_ref.shape[0]
    return copies(
        [(profiles_hbm.at[:, :, t * LANES : (t + 1) * LANES], part_ref.at[t]) for t in range(tiles)], sems
    )


def widen(t, part_ref, wide_ref):
    wide_ref[t] = part_ref[t].astype(F32).reshape(wide_ref.shape[1:])


def grid_row(levels, rows, pad, wide_ref, t, r):
    blank = jnp.zeros((pad - levels, LANES), F32)
    halves = []
    for v in range(2):
        halves += [wide_ref[t, pl.ds(v * levels * rows + r, levels, stride=rows), :], blank]
    return jnp.concatenate(halves, axis=0).astype(BF16)


def pack_kernel(
    dims,
    profiles_hbm,
    cot_hbm,
    first_ref,
    second_ref,
    edge_ref,
    send_ref,
    part_ref,
    wide_ref,
    ends_ref,
    cot_ref,
    sems,
    cot_sem,
):
    levels, rows, width, pad = dims
    tiles = width // LANES
    loads = load_profiles(profiles_hbm, part_ref, sems)
    cot_load = copies([(cot_hbm, cot_ref)], cot_sem)[0]
    edges = jnp.zeros((EDGE, 2 * pad), F32)
    k = iota((EDGE, LANES), 0)
    at_lane = iota((EDGE, LANES), 1)
    for t in range(tiles):
        loads[t].wait()
        widen(t, part_ref, wide_ref)
        for r in range(rows):
            if 0 < r < rows - 1 and 0 < t < tiles - 1:
                continue
            value = grid_row(levels, rows, pad, wide_ref, t, r)
            if r in (0, rows - 1):
                ends_ref[min(r, 1), :, t * LANES : (t + 1) * LANES] = value
            if t == 0:
                at = jnp.where((k == r) & (at_lane == 0), 1.0, 0.0).astype(BF16)
                edges = edges + dot(at, value, NT)
            if t == tiles - 1:
                at = jnp.where((k == rows + r) & (at_lane == LANES - 1), 1.0, 0.0).astype(BF16)
                edges = edges + dot(at, value, NT)
    edge_ref[...] = jnp.zeros(edge_ref.shape, BF16)
    edge_ref[:, : 2 * pad] = edges.astype(BF16)
    even, _ = pair_place("lat")
    first_ref[...] = ends_ref[jnp.where(even, 1, 0)]
    second_ref[...] = ends_ref[jnp.where(even, 0, 1)]
    proc = cot_ref.shape[1]
    cot_load.wait()
    cot = cot_ref[0].astype(BF16)

    def share(s, carry):
        send_ref[s, 0:proc, :] = cot
        for t in range(edge_ref.shape[1] // LANES):
            send_ref[s, proc + EDGE * t : proc + EDGE * (t + 1), :] = edge_ref[:, t * LANES : (t + 1) * LANES]
        return carry

    lax.fori_loop(0, send_ref.shape[0], share, 0)


def lat_block(ref, proc, side):
    at = lax.axis_index("lat") + side
    valid = (at >= 0) & (at < ref.shape[0])
    at = jnp.where(valid, at, 0)
    keep = jnp.where(valid, 1.0, 0.0)
    parts = [ref[at, proc + EDGE * t : proc + EDGE * (t + 1), :] for t in range((ref.shape[1] - proc) // EDGE)]
    return [part.astype(F32) * keep for part in parts]


def blend_kernel(rows, proc, edge_ref, lat_ref, out_ref):
    k = iota((EDGE, LANES), 0)
    last = (k == rows - 1) | (k == 2 * rows - 1)
    first = (k == 0) | (k == rows)
    ups, downs = lat_block(lat_ref, proc, -1), lat_block(lat_ref, proc, 1)
    out_ref[0:EDGE, :] = edge_ref[...]
    for t in range(edge_ref.shape[1] // LANES):
        corner = jnp.where(last, ups[t], jnp.where(first, downs[t], 0.0))
        out_ref[EDGE : 2 * EDGE, t * LANES : (t + 1) * LANES] = corner.astype(BF16)


def gather_rows(rows, row, columns_ref, rows_ref, field_ref):
    for r in range(rows):
        value = dot(rows_ref[r], row_stencil(columns_ref, row, r))
        if r == 0:
            field_ref[...] = value
        else:
            field_ref[...] += value


def gather_halo(halo_rows, row, columns_ref, first_ref, second_ref, field_ref):
    field_ref[...] += dot(first_ref[...], row_stencil(columns_ref, row, halo_rows[0]))
    field_ref[...] += dot(second_ref[...], row_stencil(columns_ref, row, halo_rows[1]))


def gather_edges(rows, pad, n_lon, first_ref, second_ref, halo_ref, edge_w, field_ref):
    west = (iota(halo_ref.shape, 0) & (EDGE - 1)) >= rows
    from_west, from_east = from_sides(first_ref[...], second_ref[...], n_lon)
    halo_ref[...] = jnp.where(west, from_west, from_east)
    field_ref[...] += dot(halo_ref[:, : 2 * pad].astype(BF16), edge_w, TN)


def departures(batch, proc, dest_ref, lat_ref, cot_rows_ref, cot_t_ref):
    obs = cot_rows_ref.shape[0]
    owned = proc // batch
    for q in range(obs // batch):
        where = dest_ref[0, q]
        slot = jnp.maximum(where, 0)
        lat = lax.div(slot, owned)
        start = pl.multiple_of((slot - lat * owned) * batch, batch)
        value = lat_ref[lat, pl.ds(start, batch), :].astype(F32)
        cot_rows_ref[q * batch : (q + 1) * batch, :] = jnp.where(where >= 0, value, 0.0)
    for lane in range(0, obs, LANES):
        cot_t_ref[:, lane : lane + LANES] = cot_rows_ref[lane : lane + LANES, :].T


def chosen_instruments(batch, obs, instr_ref):
    lane_slot = lax.shift_right_logical(iota((1, obs), 1), batch.bit_length() - 1)
    chosen = jnp.zeros((1, obs), jnp.int32)
    for q in range(obs // batch):
        chosen = jnp.where(lane_slot == q, instr_ref[0, q], chosen)
    return chosen


def turn_absorption(absorb_ref, turned_ref):
    levels, instruments, channels = absorb_ref.shape
    per = LANES // instruments
    for b in range(turned_ref.shape[0]):
        count = min(per, levels - b * per)
        block = absorb_ref[b * per : b * per + count].astype(F32).reshape(count * instruments, channels)
        if count < per:
            block = jnp.concatenate([block, jnp.zeros(((per - count) * instruments, channels), F32)], axis=0)
        turned_ref[b] = block.T


def prepare_levels(pad, field_ref, step_ref, rate_ref):
    step_ref[...] = field_ref[1 : pad + 1, :] - field_ref[0:pad, :]
    rate_ref[...] = -LOG2E * (1.0 + 0.5 * jnp.tanh(field_ref[pad : 2 * pad, :]))


def walk_levels(levels, instruments, chosen, turned_ref, cot_t_ref, rate_ref, step_ref, signal_ref, s_part_ref, r_part_ref):
    channels, obs = cot_t_ref.shape
    groups, padded, _ = s_part_ref.shape
    per = LANES // instruments
    tail = jnp.zeros((groups, padded - levels * 8, LANES), F32)
    s_part_ref[:, levels * 8 :, :] = tail
    r_part_ref[:, levels * 8 :, :] = tail
    for lane in range(0, obs, LANES):
        lanes = slice(lane, lane + LANES)
        group = lane // LANES

        def level(b, row_base, j, rates, steps, cum, signal):
            index = jnp.broadcast_to(chosen[:, lanes] + instruments * j, (8, LANES))
            a = jnp.concatenate(
                [
                    jnp.take_along_axis(turned_ref[b, c : c + 8, :], index, axis=1, mode="promise_in_bounds")
                    for c in range(0, channels, 8)
                ],
                axis=0,
            )
            cot = cot_t_ref[:, lanes]
            cum = cum + a * rates[j : j + 1]
            transmit = jnp.exp2(cum)
            at = pl.ds(pl.multiple_of(row_base + 8 * j, 8), 8)
            r_part_ref[group, at, :] = jnp.sum((cot * signal * a).reshape(channels // 8, 8, LANES), axis=0)
            s_part_ref[group, at, :] = jnp.sum((cot * transmit).reshape(channels // 8, 8, LANES), axis=0)
            signal = signal + transmit * steps[j : j + 1]
            return cum, signal

        def block(b, carry):
            cum, signal = carry
            base = pl.multiple_of(b * per, per)
            rates = rate_ref[pl.ds(base, per), lanes]
            steps = step_ref[pl.ds(base, per), lanes]
            for j in range(per):
                cum, signal = level(b, b * (8 * per), j, rates, steps, cum, signal)
            return cum, signal

        start = jnp.zeros((channels, LANES), F32)
        full = levels // per
        cum, signal = lax.fori_loop(0, full, block, (start, start))
        if levels % per:
            rates = rate_ref[full * per : (full + 1) * per, lanes]
            steps = step_ref[full * per : (full + 1) * per, lanes]
            for j in range(levels % per):
                cum, signal = level(full, full * (8 * per), j, rates, steps, cum, signal)
        signal_ref[:, lanes] = signal


def radiances(batch, proc, dest_ref, signal_ref, field_ref, send_ref):
    obs = signal_ref.shape[1]
    owned = proc // batch
    send_ref[...] = jnp.zeros(send_ref.shape, BF16)
    for lane in range(0, obs, LANES):
        lanes = slice(lane, lane + LANES)
        value = (signal_ref[:, lanes] + field_ref[0:1, lanes]).T.astype(BF16)
        for q in range(LANES // batch):
            where = dest_ref[0, lane // batch + q]

            @pl.when(where >= 0)
            def _():
                lat = lax.div(where, owned)
                start = pl.multiple_of((where - lat * owned) * batch, batch)
                send_ref[lat, pl.ds(start, batch), :] = value[q * batch : (q + 1) * batch, :]


def held_part(levels, pick, absorb_ref, cot_t_ref, signal_ref, r_part_ref):
    channels, obs = cot_t_ref.shape
    instruments = absorb_ref.shape[1]
    held = cot_t_ref[...] * signal_ref[...]
    held_hi = held.astype(BF16)
    held_lo = (held - held_hi.astype(F32)).astype(BF16)
    halves = jnp.concatenate([held_hi, held_lo], axis=0)

    def contract(l0, count):
        rows_in = absorb_ref[pl.ds(l0, count)].reshape(count * instruments, channels)
        value = dot(jnp.concatenate([rows_in, rows_in], axis=1), halves)
        value = value.reshape(count, instruments, obs) * pick[None]
        value = jnp.sum(value.reshape(count, instruments // 8, 8, obs), axis=1)
        at = pl.ds(pl.multiple_of(l0 * 8, 8), count * 8)
        value = value.reshape(count * 8, obs)
        for lane in range(0, obs, LANES):
            r_part_ref[lane // LANES, at, :] -= value[:, lane : lane + LANES]

    step = 16

    def contract_block(b, carry):
        contract(b * step, step)
        return carry

    lax.fori_loop(0, levels // step, contract_block, 0)
    if levels % step:
        contract(levels // step * step, levels % step)


def gradients(pad, s_part_ref, r_part_ref, cot_t_ref, field_ref, shift_ref, grad_ref):
    obs = cot_t_ref.shape[1]
    for lane in range(0, obs, LANES):
        lanes = slice(lane, lane + LANES)
        group = lane // LANES
        s_sum = s_part_ref[group, pl.ds(0, pad, stride=8), :]
        r_sum = r_part_ref[group, pl.ds(0, pad, stride=8), :]
        for k in range(1, 8):
            s_sum = s_sum + s_part_ref[group, pl.ds(k, pad, stride=8), :]
            r_sum = r_sum + r_part_ref[group, pl.ds(k, pad, stride=8), :]
        shift_ref[7:8, lanes] = jnp.sum(cot_t_ref[:, lanes], axis=0, keepdims=True)
        shift_ref[8 : 8 + pad, lanes] = s_sum
        grad_ref[0:pad, lanes] = (shift_ref[7 : 7 + pad, lanes] - s_sum).astype(BF16)
        bent = jnp.tanh(field_ref[pad : 2 * pad, lanes])
        grad_ref[pad : 2 * pad, lanes] = (0.5 * (1.0 - bent * bent) * r_sum).astype(BF16)


def scatter_outside(
    rows, pad, proc, halo_rows, row, columns_ref, edge_w, grad_ref, first_ref, second_ref, edge_ref, send_ref
):
    grad = grad_ref[...]
    first_ref[...] = dot(grad, row_stencil(columns_ref, row, halo_rows[0]), NT).astype(BF16)
    second_ref[...] = dot(grad, row_stencil(columns_ref, row, halo_rows[1]), NT).astype(BF16)
    out = dot(edge_w, grad, NT)
    edge_ref[...] = jnp.zeros(edge_ref.shape, F32)
    edge_ref[:, : 2 * pad] = out
    k = iota((EDGE, LANES), 0)
    last = (k == rows - 1) | (k == 2 * rows - 1)
    first = (k == 0) | (k == rows)
    for side, mine in ((-1, last), (1, first)):
        at = lax.axis_index("lat") + side

        @pl.when((at >= 0) & (at < send_ref.shape[0]))
        def _():
            for t in range(edge_ref.shape[1] // LANES):
                part = edge_ref[EDGE : 2 * EDGE, t * LANES : (t + 1) * LANES]
                part = jnp.where(mine, part, 0.0).astype(BF16)
                send_ref[at, proc + EDGE * t : proc + EDGE * (t + 1), :] = part


def gather_kernel(
    dims,
    cells_ref,
    weight_ref,
    absorb_ref,
    profiles_hbm,
    field_hbm,
    turned_hbm,
    part_ref,
    wide_ref,
    rows_ref,
    columns_ref,
    field_ref,
    turned_ref,
    sems,
    out_sems,
):
    levels, rows, width, pad = dims
    loads = load_profiles(profiles_hbm, part_ref, sems)
    fill_columns(cells_ref, weight_ref, columns_ref)
    row, _ = split_cells(cells_ref[...], width)
    turn_absorption(absorb_ref, turned_ref)
    outs = copies([(turned_ref, turned_hbm)], out_sems.at[pl.ds(0, 1)])
    for t in range(width // LANES):
        loads[t].wait()
        widen(t, part_ref, wide_ref)
        for r in range(rows):
            rows_ref[r, :, t * LANES : (t + 1) * LANES] = grid_row(levels, rows, pad, wide_ref, t, r)
    gather_rows(rows, row, columns_ref, rows_ref, field_ref)
    outs += copies([(field_ref, field_hbm)], out_sems.at[pl.ds(1, 1)])
    for move in outs:
        move.wait()


def transfer_kernel(
    dims,
    cells_ref,
    weight_ref,
    instr_ref,
    dest_ref,
    absorb_ref,
    side_first_ref,
    side_second_ref,
    field_hbm,
    turned_hbm,
    row_first_hbm,
    row_second_hbm,
    lat_hbm,
    grad_ref,
    grad_first_ref,
    grad_second_ref,
    grad_edge_ref,
    send_ref,
    columns_ref,
    turned_ref,
    halo_ref,
    field_ref,
    rate_ref,
    step_ref,
    cot_rows_ref,
    cot_t_ref,
    signal_ref,
    s_part_ref,
    r_part_ref,
    shift_ref,
    row_first_ref,
    row_second_ref,
    lat_ref,
    sems,
):
    levels, rows, width, pad, batch, proc, n_lat, n_lon = dims
    moves = [
        pltpu.make_async_copy(source, target, sems.at[k])
        for k, (source, target) in enumerate(
            (
                (field_hbm, field_ref),
                (turned_hbm, turned_ref),
                (row_first_hbm, row_first_ref),
                (row_second_hbm, row_second_ref),
                (lat_hbm, lat_ref),
            )
        )
    ]
    for move in moves:
        move.start()
    obs = cells_ref.shape[1]
    instruments = absorb_ref.shape[1]
    fill_columns(cells_ref, weight_ref, columns_ref)
    row, _ = split_cells(cells_ref[...], width)
    halo_rows = pair_rows(rows, n_lat)
    edge_w = edge_weights(cells_ref, weight_ref, rows, width)
    for move in moves:
        move.wait()
    gather_halo(halo_rows, row, columns_ref, row_first_ref, row_second_ref, field_ref)
    gather_edges(rows, pad, n_lon, side_first_ref, side_second_ref, halo_ref, edge_w, field_ref)
    departures(batch, proc, dest_ref, lat_ref, cot_rows_ref, cot_t_ref)
    chosen = chosen_instruments(batch, obs, instr_ref)
    prepare_levels(pad, field_ref, step_ref, rate_ref)
    walk_levels(
        levels, instruments, chosen, turned_ref, cot_t_ref, rate_ref, step_ref, signal_ref, s_part_ref, r_part_ref
    )
    radiances(batch, proc, dest_ref, signal_ref, field_ref, send_ref)
    pick = jnp.where(iota((instruments, obs), 0) == chosen, 1.0, 0.0)
    held_part(levels, pick, absorb_ref, cot_t_ref, signal_ref, r_part_ref)
    gradients(pad, s_part_ref, r_part_ref, cot_t_ref, field_ref, shift_ref, grad_ref)
    scatter_outside(
        rows,
        pad,
        proc,
        halo_rows,
        row,
        columns_ref,
        edge_w,
        grad_ref,
        grad_first_ref,
        grad_second_ref,
        halo_ref,
        send_ref,
    )
    grad_edge_ref[...] = halo_ref[0:EDGE, :].astype(BF16)


def corner_kernel(proc, edge_ref, lat_ref, out_ref):
    ups, downs = lat_block(lat_ref, proc, -1), lat_block(lat_ref, proc, 1)
    for t in range(edge_ref.shape[1] // LANES):
        lanes = slice(t * LANES, (t + 1) * LANES)
        out_ref[:, lanes] = (edge_ref[:, lanes].astype(F32) + ups[t] + downs[t]).astype(BF16)


def scatter_kernel(
    dims,
    cells_ref,
    weight_ref,
    grad_ref,
    row_first_ref,
    row_second_ref,
    side_first_ref,
    side_second_ref,
    lat_ref,
    out_ref,
    rad_out_ref,
    columns_ref,
    halo_ref,
    wide_ref,
    sems,
):
    levels, rows, width, pad, proc, n_lat, n_lon = dims
    fill_columns(cells_ref, weight_ref, columns_ref)
    even, at_lat = pair_place("lat")
    inside = jnp.where(at_lat > 0, 1.0, 0.0), jnp.where(at_lat < n_lat - 1, 1.0, 0.0)
    rad_out_ref[...] = jnp.sum(lat_ref[:, 0:proc, :].astype(F32), axis=0)[None]
    row, _ = split_cells(cells_ref[...], width)
    west = iota(halo_ref.shape, 0) < rows
    from_west, from_east = from_sides(side_first_ref[...], side_second_ref[...], n_lon)
    halo_ref[...] = jnp.where(west, from_west, from_east)
    edges = halo_ref[:, : 2 * pad].T.astype(BF16)
    k = iota((EDGE, LANES), 0)
    at_lane = iota((EDGE, LANES), 1)
    moves = []
    half = 2 * LANES if width % (2 * LANES) == 0 else LANES
    for start in range(0, width, half):
        part = slice(start, start + half)
        for r in range(rows):
            value = dot(grad_ref[...], row_stencil(columns_ref, row, r, part), NT)
            if r == 0:
                value = value + choose(even, row_second_ref[:, part], row_first_ref[:, part]) * inside[0]
            if r == rows - 1:
                value = value + choose(even, row_first_ref[:, part], row_second_ref[:, part]) * inside[1]
            for lane in range(start, start + half, LANES):
                piece = value[:, lane - start : lane - start + LANES]
                if lane == 0:
                    piece = piece + dot(edges, jnp.where((k == r) & (at_lane == 0), 1.0, 0.0).astype(BF16))
                if lane + LANES == width:
                    last_at = jnp.where((k == rows + r) & (at_lane == LANES - 1), 1.0, 0.0).astype(BF16)
                    piece = piece + dot(edges, last_at)
                for v in range(2):
                    at = pl.ds(v * levels * rows + r, levels, stride=rows)
                    wide_ref[lane // LANES, at, :] = piece[v * pad : v * pad + levels, :]
        for lane in range(start, start + half, LANES):
            t = lane // LANES
            move = pltpu.make_async_copy(wide_ref.at[t], out_ref.at[:, lane : lane + LANES], sems.at[t])
            move.start()
            moves.append(move)
    for move in moves:
        move.wait()


def per_device(profiles, obs_cell, obs_weight, batch_instr, batch_dest, absorption, cotangent):
    n_lat, n_lon = lax.axis_size("lat"), lax.axis_size("lon")
    levels, rows, width = profiles.shape[1:]
    instruments, channels, _ = absorption.shape
    obs = obs_cell.shape[1]
    slots = batch_dest.shape[1]
    batch = obs // slots
    proc = cotangent.shape[1]
    pad = round_up(levels, 16)
    feat = round_up(2 * pad, LANES)
    lat_rows = proc + EDGE * (feat // LANES)
    blocks = -(-levels * instruments // LANES)
    lat_pairs = [pairs(n_lat, offset, False) for offset in (0, 1)]
    lon_pairs = [pairs(n_lon, offset, True) for offset in (0, 1)]
    shape = jax.ShapeDtypeStruct
    row_shape = shape((2 * pad, width), BF16)
    edge_shape = shape((EDGE, feat), BF16)
    lat_shape = shape((n_lat, lat_rows, channels), BF16)
    absorb = jnp.transpose(absorption, (2, 0, 1))

    profiles = profiles.reshape(2 * levels, rows, width)
    tiles = width // LANES
    unpacked = [
        pltpu.VMEM((tiles, 2 * levels, rows, LANES), BF16),
        pltpu.VMEM((tiles, 2 * levels * rows, LANES), F32),
    ]
    row_first, row_second, edge, lat_send = pl.pallas_call(
        functools.partial(pack_kernel, (levels, rows, width, pad)),
        out_shape=(row_shape, row_shape, edge_shape, lat_shape),
        in_specs=[HBM] * 2,
        out_specs=(VMEM,) * 4,
        scratch_shapes=unpacked
        + [
            pltpu.VMEM((2, 2 * pad, width), BF16),
            pltpu.VMEM((1, proc, channels), F32),
            pltpu.SemaphoreType.DMA((tiles,)),
            pltpu.SemaphoreType.DMA((1,)),
        ],
        compiler_params=params(56),
        name="pack",
    )(profiles, cotangent)

    lat_in = lax.all_to_all(lat_send, "lat", 0, 0, tiled=True)
    row_first = lax.ppermute(row_first, "lat", lat_pairs[0])

    field, turned = pl.pallas_call(
        functools.partial(gather_kernel, (levels, rows, width, pad)),
        out_shape=(shape((2 * pad, obs), F32), shape((blocks, channels, LANES), F32)),
        in_specs=[VMEM] * 3 + [HBM],
        out_specs=(HBM,) * 2,
        scratch_shapes=unpacked
        + [
            pltpu.VMEM((rows, 2 * pad, width), BF16),
            pltpu.VMEM((3, width, obs), BF16),
            pltpu.VMEM((2 * pad, obs), F32),
            pltpu.VMEM((blocks, channels, LANES), F32),
            pltpu.SemaphoreType.DMA((tiles,)),
            pltpu.SemaphoreType.DMA((2,)),
        ],
        compiler_params=params(56),
        name="gather",
    )(obs_cell, obs_weight, absorb, profiles)
    row_second, field = lax.optimization_barrier((row_second, field))
    row_second = lax.ppermute(row_second, "lat", lat_pairs[1])

    side = pl.pallas_call(
        functools.partial(blend_kernel, rows, proc),
        out_shape=shape((BLOCKS * EDGE, feat), BF16),
        in_specs=[VMEM] * 2,
        out_specs=VMEM,
        compiler_params=params(4),
        cost_estimate=SMALL,
        name="blend",
    )(edge, lat_in)
    side_first = lax.ppermute(side, "lon", lon_pairs[0])
    side_second = lax.ppermute(side, "lon", lon_pairs[1])

    grad, grad_first, grad_second, grad_edge, lat_back = pl.pallas_call(
        functools.partial(transfer_kernel, (levels, rows, width, pad, batch, proc, n_lat, n_lon)),
        out_shape=(shape((2 * pad, obs), BF16), row_shape, row_shape, edge_shape, lat_shape),
        in_specs=[VMEM, VMEM, SMEM, SMEM] + [VMEM] * 3 + [HBM] * 5,
        out_specs=(VMEM,) * 5,
        scratch_shapes=[
            pltpu.VMEM((3, width, obs), BF16),
            pltpu.VMEM((blocks, channels, LANES), F32),
            pltpu.VMEM((BLOCKS * EDGE, feat), F32),
            pltpu.VMEM((2 * pad, obs), F32),
            pltpu.VMEM((pad, obs), F32),
            pltpu.VMEM((pad, obs), F32),
            pltpu.VMEM((obs, channels), F32),
            pltpu.VMEM((channels, obs), F32),
            pltpu.VMEM((channels, obs), F32),
            pltpu.VMEM((obs // LANES, pad * 8, LANES), F32),
            pltpu.VMEM((obs // LANES, pad * 8, LANES), F32),
            pltpu.VMEM((pad + 8, obs), F32),
            pltpu.VMEM(row_shape.shape, BF16),
            pltpu.VMEM(row_shape.shape, BF16),
            pltpu.VMEM(lat_shape.shape, BF16),
            pltpu.SemaphoreType.DMA((5,)),
        ],
        compiler_params=params(56),
        name="transfer",
    )(
        obs_cell,
        obs_weight,
        batch_instr,
        batch_dest,
        absorb,
        side_first,
        side_second,
        field,
        turned,
        row_first,
        row_second,
        lat_in,
    )

    grad_first = lax.ppermute(grad_first, "lat", lat_pairs[0])
    grad_second = lax.ppermute(grad_second, "lat", lat_pairs[1])
    lat_got = lax.all_to_all(lat_back, "lat", 0, 0, tiled=True)
    grad_side = pl.pallas_call(
        functools.partial(corner_kernel, proc),
        out_shape=edge_shape,
        in_specs=[VMEM] * 2,
        out_specs=VMEM,
        compiler_params=params(4),
        cost_estimate=SMALL,
        name="corner",
    )(grad_edge, lat_got)
    grad_side_first = lax.ppermute(grad_side, "lon", lon_pairs[0])
    grad_side_second = lax.ppermute(grad_side, "lon", lon_pairs[1])

    gradient, radiance = pl.pallas_call(
        functools.partial(scatter_kernel, (levels, rows, width, pad, proc, n_lat, n_lon)),
        out_shape=(
            shape((2 * levels * rows, width), F32),
            shape((1, proc, channels), F32),
        ),
        in_specs=[VMEM] * 8,
        out_specs=(HBM, VMEM),
        scratch_shapes=[
            pltpu.VMEM((3, width, obs), BF16),
            pltpu.VMEM((EDGE, feat), F32),
            pltpu.VMEM((width // LANES, 2 * levels * rows, LANES), F32),
            pltpu.SemaphoreType.DMA((width // LANES,)),
        ],
        compiler_params=params(20),
        name="scatter",
    )(obs_cell, obs_weight, grad, grad_first, grad_second, grad_side_first, grad_side_second, lat_got)
    return radiance, gradient.reshape(2, levels, rows, width)


def solution(mesh):
    placed = (
        P("groups", None, "lat", "lon"),
        P(("groups", "lon"), "lat"),
        P("groups", "lon", "lat"),
        P(("groups", "lon"), "lat"),
        P(("groups", "lon"), "lat"),
        P(),
        P(("groups", "lon"), "lat", None),
    )
    return jax.shard_map(
        per_device,
        mesh=mesh,
        in_specs=placed,
        out_specs=(P(("groups", "lon"), "lat", None), P("groups", None, "lat", "lon")),
        check_vma=False,
    )
```

```python
import functools

import jax
import jax.numpy as jnp
from jax import lax
from jax.experimental import pallas as pl
from jax.experimental.pallas import tpu as pltpu
from jax.sharding import PartitionSpec as P

F32 = jnp.float32
BF16 = jnp.bfloat16
LOG2E = 1.4426950408889634
LANES = 128
EDGE = 16
BLOCKS = 2
VMEM = pl.BlockSpec(memory_space=pltpu.VMEM)
SMEM = pl.BlockSpec(memory_space=pltpu.SMEM)
HBM = pl.BlockSpec(memory_space=pltpu.HBM)
SMALL = pl.CostEstimate(flops=1000, bytes_accessed=1000, transcendentals=0)
NN = (((1,), (0,)), ((), ()))
NT = (((1,), (1,)), ((), ()))
TN = (((0,), (0,)), ((), ()))


def dot(a, b, dims=NN):
    return lax.dot_general(a, b, dims, preferred_element_type=F32)


def round_up(value, unit):
    return -(-value // unit) * unit


def params(mib):
    return pltpu.CompilerParams(vmem_limit_bytes=mib * 1024 * 1024)


def iota(shape, dim):
    return lax.broadcasted_iota(jnp.int32, shape, dim)


def split_cells(cells, width):
    if width & (width - 1) == 0:
        return lax.shift_right_logical(cells, width.bit_length() - 1), cells & (width - 1)
    row = lax.div(cells, width)
    return row, cells - row * width


def fill_columns(cells_ref, weight_ref, columns_ref):
    width, obs = columns_ref.shape[1:]
    _, col = split_cells(cells_ref[...], width)
    weights = [weight_ref[k] for k in range(9)]
    step = 32

    def chunk(i, carry):
        base = pl.multiple_of(i * step, step)
        for lane in range(0, obs, LANES):
            part = slice(lane, lane + LANES)
            away = iota((step, LANES), 0) + base - col[:, part]
            hit = [away == b - 1 for b in range(3)]
            for a in range(3):
                value = jnp.zeros((step, LANES), F32)
                for b in range(3):
                    value = jnp.where(hit[b], weights[3 * a + b][:, part], value)
                columns_ref[a, pl.ds(base, step), part] = value.astype(BF16)
        return carry

    lax.fori_loop(0, width // step, chunk, 0)


def row_stencil(columns_ref, row_of, r, part=slice(None)):
    total = None
    for a in range(3):
        keep = jnp.where(row_of == r - a + 1, 1.0, 0.0).astype(BF16)
        term = columns_ref[a, part, :] * keep
        total = term if total is None else total + term
    return total


def edge_weights(cells_ref, weight_ref, rows, width):
    lines = BLOCKS * EDGE
    obs = cells_ref.shape[1]
    row, col = split_cells(cells_ref[...], width)
    line = iota((lines, obs), 0)
    block = lax.shift_right_logical(line, 4)
    k = line & (EDGE - 1)
    none = -99
    west = k >= rows
    col_at = jnp.where(west, -1, width)
    row_at = jnp.where(west, k - rows, k)
    corner = jnp.where(row_at == rows - 1, -1, jnp.where(row_at == 0, rows, none))
    row_at = jnp.where(block == 1, corner, row_at)
    total = jnp.zeros((lines, obs), F32)
    for a in range(3):
        for b in range(3):
            hit = (row_at == row + (a - 1)) & (col_at == col + (b - 1))
            total = total + jnp.where(hit, weight_ref[3 * a + b], 0.0)
    return total.astype(BF16)


def pairs(count, offset, ring):
    swap = [(i, i + 1) for i in range(offset, count - 1, 2)]
    if ring and offset and count % 2 == 0 and count > 2:
        swap.append((0, count - 1))
    return sorted(swap + [(b, a) for a, b in swap])


def pair_place(axis):
    at = lax.axis_index(axis)
    return (at & 1) == 0, at


def pair_rows(rows, count):
    even, at = pair_place("lat")
    below = jnp.where(at < count - 1, rows, -99)
    above = jnp.where(at > 0, -1, -99)
    return jnp.where(even, below, above), jnp.where(even, above, below)


def choose(pred, a, b):
    return jnp.where(pred, a.astype(F32), b.astype(F32))


def from_sides(first, second, count):
    even, at = pair_place("lon")
    west = choose(even, second, first) * jnp.where(at > 0, 1.0, 0.0)
    east = choose(even, first, second) * jnp.where(at < count - 1, 1.0, 0.0)
    return west, east


def copies(pairs_of, sems):
    moves = [pltpu.make_async_copy(source, target, sems.at[k]) for k, (source, target) in enumerate(pairs_of)]
    for move in moves:
        move.start()
    return moves


def load_profiles(profiles_hbm, part_ref, sems):
    tiles = part_ref.shape[0]
    return copies(
        [(profiles_hbm.at[:, :, t * LANES : (t + 1) * LANES], part_ref.at[t]) for t in range(tiles)], sems
    )


def widen(t, part_ref, wide_ref):
    wide_ref[t] = part_ref[t].astype(F32).reshape(wide_ref.shape[1:])


def grid_row(levels, rows, pad, wide_ref, t, r):
    blank = jnp.zeros((pad - levels, LANES), F32)
    halves = []
    for v in range(2):
        halves += [wide_ref[t, pl.ds(v * levels * rows + r, levels, stride=rows), :], blank]
    return jnp.concatenate(halves, axis=0).astype(BF16)


def pack_kernel(
    dims,
    profiles_hbm,
    cot_hbm,
    first_ref,
    second_ref,
    edge_ref,
    send_ref,
    part_ref,
    wide_ref,
    ends_ref,
    cot_ref,
    sems,
    cot_sem,
):
    levels, rows, width, pad = dims
    tiles = width // LANES
    loads = load_profiles(profiles_hbm, part_ref, sems)
    cot_load = copies([(cot_hbm, cot_ref)], cot_sem)[0]
    edges = jnp.zeros((EDGE, 2 * pad), F32)
    k = iota((EDGE, LANES), 0)
    at_lane = iota((EDGE, LANES), 1)
    for t in range(tiles):
        loads[t].wait()
        widen(t, part_ref, wide_ref)
        for r in range(rows):
            if 0 < r < rows - 1 and 0 < t < tiles - 1:
                continue
            value = grid_row(levels, rows, pad, wide_ref, t, r)
            if r in (0, rows - 1):
                ends_ref[min(r, 1), :, t * LANES : (t + 1) * LANES] = value
            if t == 0:
                at = jnp.where((k == r) & (at_lane == 0), 1.0, 0.0).astype(BF16)
                edges = edges + dot(at, value, NT)
            if t == tiles - 1:
                at = jnp.where((k == rows + r) & (at_lane == LANES - 1), 1.0, 0.0).astype(BF16)
                edges = edges + dot(at, value, NT)
    edge_ref[...] = jnp.zeros(edge_ref.shape, BF16)
    edge_ref[:, : 2 * pad] = edges.astype(BF16)
    even, _ = pair_place("lat")
    first_ref[...] = ends_ref[jnp.where(even, 1, 0)]
    second_ref[...] = ends_ref[jnp.where(even, 0, 1)]
    proc = cot_ref.shape[1]
    cot_load.wait()
    cot = cot_ref[0].astype(BF16)

    def share(s, carry):
        send_ref[s, 0:proc, :] = cot
        for t in range(edge_ref.shape[1] // LANES):
            send_ref[s, proc + EDGE * t : proc + EDGE * (t + 1), :] = edge_ref[:, t * LANES : (t + 1) * LANES]
        return carry

    lax.fori_loop(0, send_ref.shape[0], share, 0)


def lat_block(ref, proc, side):
    at = lax.axis_index("lat") + side
    valid = (at >= 0) & (at < ref.shape[0])
    at = jnp.where(valid, at, 0)
    keep = jnp.where(valid, 1.0, 0.0)
    parts = [ref[at, proc + EDGE * t : proc + EDGE * (t + 1), :] for t in range((ref.shape[1] - proc) // EDGE)]
    return [part.astype(F32) * keep for part in parts]


def blend_kernel(rows, proc, edge_ref, lat_ref, out_ref):
    k = iota((EDGE, LANES), 0)
    last = (k == rows - 1) | (k == 2 * rows - 1)
    first = (k == 0) | (k == rows)
    ups, downs = lat_block(lat_ref, proc, -1), lat_block(lat_ref, proc, 1)
    out_ref[0:EDGE, :] = edge_ref[...]
    for t in range(edge_ref.shape[1] // LANES):
        corner = jnp.where(last, ups[t], jnp.where(first, downs[t], 0.0))
        out_ref[EDGE : 2 * EDGE, t * LANES : (t + 1) * LANES] = corner.astype(BF16)


def gather_rows(rows, row, columns_ref, rows_ref, field_ref):
    for r in range(rows):
        value = dot(rows_ref[r], row_stencil(columns_ref, row, r))
        if r == 0:
            field_ref[...] = value
        else:
            field_ref[...] += value


def gather_halo(halo_rows, row, columns_ref, first_ref, second_ref, field_ref):
    field_ref[...] += dot(first_ref[...], row_stencil(columns_ref, row, halo_rows[0]))
    field_ref[...] += dot(second_ref[...], row_stencil(columns_ref, row, halo_rows[1]))


def gather_edges(rows, pad, n_lon, first_ref, second_ref, halo_ref, edge_w, field_ref):
    west = (iota(halo_ref.shape, 0) & (EDGE - 1)) >= rows
    from_west, from_east = from_sides(first_ref[...], second_ref[...], n_lon)
    halo_ref[...] = jnp.where(west, from_west, from_east)
    field_ref[...] += dot(halo_ref[:, : 2 * pad].astype(BF16), edge_w, TN)


def departures(batch, proc, dest_ref, lat_ref, cot_rows_ref, cot_t_ref):
    obs = cot_rows_ref.shape[0]
    owned = proc // batch
    for q in range(obs // batch):
        where = dest_ref[0, q]
        slot = jnp.maximum(where, 0)
        lat = lax.div(slot, owned)
        start = pl.multiple_of((slot - lat * owned) * batch, batch)
        value = lat_ref[lat, pl.ds(start, batch), :].astype(F32)
        cot_rows_ref[q * batch : (q + 1) * batch, :] = jnp.where(where >= 0, value, 0.0)
    for lane in range(0, obs, LANES):
        cot_t_ref[:, lane : lane + LANES] = cot_rows_ref[lane : lane + LANES, :].T


def chosen_instruments(batch, obs, instr_ref):
    lane_slot = lax.shift_right_logical(iota((1, obs), 1), batch.bit_length() - 1)
    chosen = jnp.zeros((1, obs), jnp.int32)
    for q in range(obs // batch):
        chosen = jnp.where(lane_slot == q, instr_ref[0, q], chosen)
    return chosen


def turn_absorption(absorb_ref, turned_ref):
    levels, instruments, channels = absorb_ref.shape
    per = LANES // instruments
    for b in range(turned_ref.shape[0]):
        count = min(per, levels - b * per)
        block = absorb_ref[b * per : b * per + count].astype(F32).reshape(count * instruments, channels)
        if count < per:
            block = jnp.concatenate([block, jnp.zeros(((per - count) * instruments, channels), F32)], axis=0)
        turned_ref[b] = block.T


def prepare_levels(pad, field_ref, step_ref, rate_ref):
    step_ref[...] = field_ref[1 : pad + 1, :] - field_ref[0:pad, :]
    rate_ref[...] = -LOG2E * (1.0 + 0.5 * jnp.tanh(field_ref[pad : 2 * pad, :]))


def walk_levels(levels, instruments, chosen, turned_ref, cot_t_ref, rate_ref, step_ref, signal_ref, s_part_ref, r_part_ref):
    channels, obs = cot_t_ref.shape
    groups, padded, _ = s_part_ref.shape
    per = LANES // instruments
    tail = jnp.zeros((groups, padded - levels * 8, LANES), F32)
    s_part_ref[:, levels * 8 :, :] = tail
    r_part_ref[:, levels * 8 :, :] = tail
    for lane in range(0, obs, LANES):
        lanes = slice(lane, lane + LANES)
        group = lane // LANES

        def level(b, row_base, j, rates, steps, cum, signal):
            index = jnp.broadcast_to(chosen[:, lanes] + instruments * j, (8, LANES))
            a = jnp.concatenate(
                [
                    jnp.take_along_axis(turned_ref[b, c : c + 8, :], index, axis=1, mode="promise_in_bounds")
                    for c in range(0, channels, 8)
                ],
                axis=0,
            )
            cot = cot_t_ref[:, lanes]
            cum = cum + a * rates[j : j + 1]
            transmit = jnp.exp2(cum)
            at = pl.ds(pl.multiple_of(row_base + 8 * j, 8), 8)
            r_part_ref[group, at, :] = jnp.sum((cot * signal * a).reshape(channels // 8, 8, LANES), axis=0)
            s_part_ref[group, at, :] = jnp.sum((cot * transmit).reshape(channels // 8, 8, LANES), axis=0)
            signal = signal + transmit * steps[j : j + 1]
            return cum, signal

        def block(b, carry):
            cum, signal = carry
            base = pl.multiple_of(b * per, per)
            rates = rate_ref[pl.ds(base, per), lanes]
            steps = step_ref[pl.ds(base, per), lanes]
            for j in range(per):
                cum, signal = level(b, b * (8 * per), j, rates, steps, cum, signal)
            return cum, signal

        start = jnp.zeros((channels, LANES), F32)
        full = levels // per
        cum, signal = lax.fori_loop(0, full, block, (start, start))
        if levels % per:
            rates = rate_ref[full * per : (full + 1) * per, lanes]
            steps = step_ref[full * per : (full + 1) * per, lanes]
            for j in range(levels % per):
                cum, signal = level(full, full * (8 * per), j, rates, steps, cum, signal)
        signal_ref[:, lanes] = signal


def radiances(batch, proc, dest_ref, signal_ref, field_ref, send_ref):
    obs = signal_ref.shape[1]
    owned = proc // batch
    send_ref[...] = jnp.zeros(send_ref.shape, BF16)
    for lane in range(0, obs, LANES):
        lanes = slice(lane, lane + LANES)
        value = (signal_ref[:, lanes] + field_ref[0:1, lanes]).T.astype(BF16)
        for q in range(LANES // batch):
            where = dest_ref[0, lane // batch + q]

            @pl.when(where >= 0)
            def _():
                lat = lax.div(where, owned)
                start = pl.multiple_of((where - lat * owned) * batch, batch)
                send_ref[lat, pl.ds(start, batch), :] = value[q * batch : (q + 1) * batch, :]


def held_part(levels, pick, absorb_ref, cot_t_ref, signal_ref, r_part_ref):
    channels, obs = cot_t_ref.shape
    instruments = absorb_ref.shape[1]
    held = cot_t_ref[...] * signal_ref[...]
    held_hi = held.astype(BF16)
    held_lo = (held - held_hi.astype(F32)).astype(BF16)
    halves = jnp.concatenate([held_hi, held_lo], axis=0)

    def contract(l0, count):
        rows_in = absorb_ref[pl.ds(l0, count)].reshape(count * instruments, channels)
        value = dot(jnp.concatenate([rows_in, rows_in], axis=1), halves)
        value = value.reshape(count, instruments, obs) * pick[None]
        value = jnp.sum(value.reshape(count, instruments // 8, 8, obs), axis=1)
        at = pl.ds(pl.multiple_of(l0 * 8, 8), count * 8)
        value = value.reshape(count * 8, obs)
        for lane in range(0, obs, LANES):
            r_part_ref[lane // LANES, at, :] -= value[:, lane : lane + LANES]

    step = 16

    def contract_block(b, carry):
        contract(b * step, step)
        return carry

    lax.fori_loop(0, levels // step, contract_block, 0)
    if levels % step:
        contract(levels // step * step, levels % step)


def gradients(pad, s_part_ref, r_part_ref, cot_t_ref, field_ref, shift_ref, grad_ref):
    obs = cot_t_ref.shape[1]
    for lane in range(0, obs, LANES):
        lanes = slice(lane, lane + LANES)
        group = lane // LANES
        s_sum = s_part_ref[group, pl.ds(0, pad, stride=8), :]
        r_sum = r_part_ref[group, pl.ds(0, pad, stride=8), :]
        for k in range(1, 8):
            s_sum = s_sum + s_part_ref[group, pl.ds(k, pad, stride=8), :]
            r_sum = r_sum + r_part_ref[group, pl.ds(k, pad, stride=8), :]
        shift_ref[7:8, lanes] = jnp.sum(cot_t_ref[:, lanes], axis=0, keepdims=True)
        shift_ref[8 : 8 + pad, lanes] = s_sum
        grad_ref[0:pad, lanes] = (shift_ref[7 : 7 + pad, lanes] - s_sum).astype(BF16)
        bent = jnp.tanh(field_ref[pad : 2 * pad, lanes])
        grad_ref[pad : 2 * pad, lanes] = (0.5 * (1.0 - bent * bent) * r_sum).astype(BF16)


def scatter_outside(
    rows, pad, proc, halo_rows, row, columns_ref, edge_w, grad_ref, first_ref, second_ref, edge_ref, send_ref
):
    grad = grad_ref[...]
    first_ref[...] = dot(grad, row_stencil(columns_ref, row, halo_rows[0]), NT).astype(BF16)
    second_ref[...] = dot(grad, row_stencil(columns_ref, row, halo_rows[1]), NT).astype(BF16)
    out = dot(edge_w, grad, NT)
    edge_ref[...] = jnp.zeros(edge_ref.shape, F32)
    edge_ref[:, : 2 * pad] = out
    k = iota((EDGE, LANES), 0)
    last = (k == rows - 1) | (k == 2 * rows - 1)
    first = (k == 0) | (k == rows)
    for side, mine in ((-1, last), (1, first)):
        at = lax.axis_index("lat") + side

        @pl.when((at >= 0) & (at < send_ref.shape[0]))
        def _():
            for t in range(edge_ref.shape[1] // LANES):
                part = edge_ref[EDGE : 2 * EDGE, t * LANES : (t + 1) * LANES]
                part = jnp.where(mine, part, 0.0).astype(BF16)
                send_ref[at, proc + EDGE * t : proc + EDGE * (t + 1), :] = part

    for t in range(edge_ref.shape[1] // LANES):
        part = edge_ref[0:EDGE, t * LANES : (t + 1) * LANES].astype(BF16)
        send_ref[lax.axis_index("lat"), proc + EDGE * t : proc + EDGE * (t + 1), :] = part


def gather_kernel(
    dims,
    cells_ref,
    weight_ref,
    absorb_ref,
    profiles_hbm,
    field_hbm,
    turned_hbm,
    part_ref,
    wide_ref,
    rows_ref,
    columns_ref,
    field_ref,
    turned_ref,
    sems,
    out_sems,
):
    levels, rows, width, pad = dims
    loads = load_profiles(profiles_hbm, part_ref, sems)
    fill_columns(cells_ref, weight_ref, columns_ref)
    row, _ = split_cells(cells_ref[...], width)
    turn_absorption(absorb_ref, turned_ref)
    outs = copies([(turned_ref, turned_hbm)], out_sems.at[pl.ds(0, 1)])
    for t in range(width // LANES):
        loads[t].wait()
        widen(t, part_ref, wide_ref)
        for r in range(rows):
            rows_ref[r, :, t * LANES : (t + 1) * LANES] = grid_row(levels, rows, pad, wide_ref, t, r)
    gather_rows(rows, row, columns_ref, rows_ref, field_ref)
    outs += copies([(field_ref, field_hbm)], out_sems.at[pl.ds(1, 1)])
    for move in outs:
        move.wait()


def transfer_kernel(
    dims,
    cells_ref,
    weight_ref,
    instr_ref,
    dest_ref,
    absorb_ref,
    side_first_ref,
    side_second_ref,
    field_hbm,
    turned_hbm,
    row_first_hbm,
    row_second_hbm,
    lat_hbm,
    grad_ref,
    grad_first_ref,
    grad_second_ref,
    send_ref,
    columns_ref,
    turned_ref,
    halo_ref,
    field_ref,
    rate_ref,
    step_ref,
    cot_rows_ref,
    cot_t_ref,
    signal_ref,
    s_part_ref,
    r_part_ref,
    shift_ref,
    row_first_ref,
    row_second_ref,
    lat_ref,
    sems,
):
    levels, rows, width, pad, batch, proc, n_lat, n_lon = dims
    moves = [
        pltpu.make_async_copy(source, target, sems.at[k])
        for k, (source, target) in enumerate(
            (
                (field_hbm, field_ref),
                (turned_hbm, turned_ref),
                (row_first_hbm, row_first_ref),
                (row_second_hbm, row_second_ref),
                (lat_hbm, lat_ref),
            )
        )
    ]
    for move in moves:
        move.start()
    obs = cells_ref.shape[1]
    instruments = absorb_ref.shape[1]
    fill_columns(cells_ref, weight_ref, columns_ref)
    row, _ = split_cells(cells_ref[...], width)
    halo_rows = pair_rows(rows, n_lat)
    edge_w = edge_weights(cells_ref, weight_ref, rows, width)
    moves[4].wait()
    departures(batch, proc, dest_ref, lat_ref, cot_rows_ref, cot_t_ref)
    for k in (0, 2, 3):
        moves[k].wait()
    gather_halo(halo_rows, row, columns_ref, row_first_ref, row_second_ref, field_ref)
    gather_edges(rows, pad, n_lon, side_first_ref, side_second_ref, halo_ref, edge_w, field_ref)
    chosen = chosen_instruments(batch, obs, instr_ref)
    prepare_levels(pad, field_ref, step_ref, rate_ref)
    moves[1].wait()
    walk_levels(
        levels, instruments, chosen, turned_ref, cot_t_ref, rate_ref, step_ref, signal_ref, s_part_ref, r_part_ref
    )
    radiances(batch, proc, dest_ref, signal_ref, field_ref, send_ref)
    pick = jnp.where(iota((instruments, obs), 0) == chosen, 1.0, 0.0)
    held_part(levels, pick, absorb_ref, cot_t_ref, signal_ref, r_part_ref)
    gradients(pad, s_part_ref, r_part_ref, cot_t_ref, field_ref, shift_ref, grad_ref)
    scatter_outside(
        rows,
        pad,
        proc,
        halo_rows,
        row,
        columns_ref,
        edge_w,
        grad_ref,
        grad_first_ref,
        grad_second_ref,
        halo_ref,
        send_ref,
    )


def corner_kernel(proc, lat_ref, out_ref):
    owns, ups, downs = [lat_block(lat_ref, proc, side) for side in (0, -1, 1)]
    for t in range(out_ref.shape[1] // LANES):
        out_ref[:, t * LANES : (t + 1) * LANES] = (owns[t] + ups[t] + downs[t]).astype(BF16)


def scatter_kernel(
    dims,
    cells_ref,
    weight_ref,
    grad_ref,
    row_first_ref,
    row_second_ref,
    side_first_ref,
    side_second_ref,
    lat_ref,
    out_ref,
    rad_out_ref,
    columns_ref,
    halo_ref,
    wide_ref,
    sems,
):
    levels, rows, width, pad, proc, n_lat, n_lon = dims
    fill_columns(cells_ref, weight_ref, columns_ref)
    even, at_lat = pair_place("lat")
    inside = jnp.where(at_lat > 0, 1.0, 0.0), jnp.where(at_lat < n_lat - 1, 1.0, 0.0)
    rad_out_ref[...] = jnp.sum(lat_ref[:, 0:proc, :].astype(F32), axis=0)[None]
    row, _ = split_cells(cells_ref[...], width)
    west = iota(halo_ref.shape, 0) < rows
    from_west, from_east = from_sides(side_first_ref[...], side_second_ref[...], n_lon)
    halo_ref[...] = jnp.where(west, from_west, from_east)
    edges = halo_ref[:, : 2 * pad].T.astype(BF16)
    k = iota((EDGE, LANES), 0)
    at_lane = iota((EDGE, LANES), 1)
    moves = []
    half = 2 * LANES if width % (2 * LANES) == 0 else LANES
    for start in range(0, width, half):
        part = slice(start, start + half)
        for r in range(rows):
            value = dot(grad_ref[...], row_stencil(columns_ref, row, r, part), NT)
            if r == 0:
                value = value + choose(even, row_second_ref[:, part], row_first_ref[:, part]) * inside[0]
            if r == rows - 1:
                value = value + choose(even, row_first_ref[:, part], row_second_ref[:, part]) * inside[1]
            for lane in range(start, start + half, LANES):
                piece = value[:, lane - start : lane - start + LANES]
                if lane == 0:
                    piece = piece + dot(edges, jnp.where((k == r) & (at_lane == 0), 1.0, 0.0).astype(BF16))
                if lane + LANES == width:
                    last_at = jnp.where((k == rows + r) & (at_lane == LANES - 1), 1.0, 0.0).astype(BF16)
                    piece = piece + dot(edges, last_at)
                for v in range(2):
                    at = pl.ds(v * levels * rows + r, levels, stride=rows)
                    wide_ref[lane // LANES, at, :] = piece[v * pad : v * pad + levels, :]
        for lane in range(start, start + half, LANES):
            t = lane // LANES
            move = pltpu.make_async_copy(wide_ref.at[t], out_ref.at[:, lane : lane + LANES], sems.at[t])
            move.start()
            moves.append(move)
    for move in moves:
        move.wait()


def per_device(profiles, obs_cell, obs_weight, batch_instr, batch_dest, absorption, cotangent):
    n_lat, n_lon = lax.axis_size("lat"), lax.axis_size("lon")
    levels, rows, width = profiles.shape[1:]
    instruments, channels, _ = absorption.shape
    obs = obs_cell.shape[1]
    slots = batch_dest.shape[1]
    batch = obs // slots
    proc = cotangent.shape[1]
    pad = round_up(levels, 16)
    feat = round_up(2 * pad, LANES)
    lat_rows = proc + EDGE * (feat // LANES)
    blocks = -(-levels * instruments // LANES)
    lat_pairs = [pairs(n_lat, offset, False) for offset in (0, 1)]
    lon_pairs = [pairs(n_lon, offset, True) for offset in (0, 1)]
    shape = jax.ShapeDtypeStruct
    row_shape = shape((2 * pad, width), BF16)
    edge_shape = shape((EDGE, feat), BF16)
    lat_shape = shape((n_lat, lat_rows, channels), BF16)
    absorb = jnp.transpose(absorption, (2, 0, 1))

    profiles = profiles.reshape(2 * levels, rows, width)
    tiles = width // LANES
    unpacked = [
        pltpu.VMEM((tiles, 2 * levels, rows, LANES), BF16),
        pltpu.VMEM((tiles, 2 * levels * rows, LANES), F32),
    ]
    row_first, row_second, edge, lat_send = pl.pallas_call(
        functools.partial(pack_kernel, (levels, rows, width, pad)),
        out_shape=(row_shape, row_shape, edge_shape, lat_shape),
        in_specs=[HBM] * 2,
        out_specs=(VMEM,) * 4,
        scratch_shapes=unpacked
        + [
            pltpu.VMEM((2, 2 * pad, width), BF16),
            pltpu.VMEM((1, proc, channels), F32),
            pltpu.SemaphoreType.DMA((tiles,)),
            pltpu.SemaphoreType.DMA((1,)),
        ],
        compiler_params=params(56),
        name="pack",
    )(profiles, cotangent)

    lat_in = lax.all_to_all(lat_send, "lat", 0, 0, tiled=True)
    row_first = lax.ppermute(row_first, "lat", lat_pairs[0])
    row_second = lax.ppermute(row_second, "lat", lat_pairs[1])

    field, turned = pl.pallas_call(
        functools.partial(gather_kernel, (levels, rows, width, pad)),
        out_shape=(shape((2 * pad, obs), F32), shape((blocks, channels, LANES), F32)),
        in_specs=[VMEM] * 3 + [HBM],
        out_specs=(HBM,) * 2,
        scratch_shapes=unpacked
        + [
            pltpu.VMEM((rows, 2 * pad, width), BF16),
            pltpu.VMEM((3, width, obs), BF16),
            pltpu.VMEM((2 * pad, obs), F32),
            pltpu.VMEM((blocks, channels, LANES), F32),
            pltpu.SemaphoreType.DMA((tiles,)),
            pltpu.SemaphoreType.DMA((2,)),
        ],
        compiler_params=params(56),
        name="gather",
    )(obs_cell, obs_weight, absorb, profiles)
    edge, field = lax.optimization_barrier((edge, field))

    side = pl.pallas_call(
        functools.partial(blend_kernel, rows, proc),
        out_shape=shape((BLOCKS * EDGE, feat), BF16),
        in_specs=[VMEM] * 2,
        out_specs=VMEM,
        compiler_params=params(4),
        cost_estimate=SMALL,
        name="blend",
    )(edge, lat_in)
    side_first = lax.ppermute(side, "lon", lon_pairs[0])
    side_second = lax.ppermute(side, "lon", lon_pairs[1])

    grad, grad_first, grad_second, lat_back = pl.pallas_call(
        functools.partial(transfer_kernel, (levels, rows, width, pad, batch, proc, n_lat, n_lon)),
        out_shape=(shape((2 * pad, obs), BF16), row_shape, row_shape, lat_shape),
        in_specs=[VMEM, VMEM, SMEM, SMEM] + [VMEM] * 3 + [HBM] * 5,
        out_specs=(VMEM,) * 4,
        scratch_shapes=[
            pltpu.VMEM((3, width, obs), BF16),
            pltpu.VMEM((blocks, channels, LANES), F32),
            pltpu.VMEM((BLOCKS * EDGE, feat), F32),
            pltpu.VMEM((2 * pad, obs), F32),
            pltpu.VMEM((pad, obs), F32),
            pltpu.VMEM((pad, obs), F32),
            pltpu.VMEM((obs, channels), F32),
            pltpu.VMEM((channels, obs), F32),
            pltpu.VMEM((channels, obs), F32),
            pltpu.VMEM((obs // LANES, pad * 8, LANES), F32),
            pltpu.VMEM((obs // LANES, pad * 8, LANES), F32),
            pltpu.VMEM((pad + 8, obs), F32),
            pltpu.VMEM(row_shape.shape, BF16),
            pltpu.VMEM(row_shape.shape, BF16),
            pltpu.VMEM(lat_shape.shape, BF16),
            pltpu.SemaphoreType.DMA((5,)),
        ],
        compiler_params=params(56),
        name="transfer",
    )(
        obs_cell,
        obs_weight,
        batch_instr,
        batch_dest,
        absorb,
        side_first,
        side_second,
        field,
        turned,
        row_first,
        row_second,
        lat_in,
    )

    grad_first = lax.ppermute(grad_first, "lat", lat_pairs[0])
    grad_second = lax.ppermute(grad_second, "lat", lat_pairs[1])
    lat_got = lax.all_to_all(lat_back, "lat", 0, 0, tiled=True)
    grad_side = pl.pallas_call(
        functools.partial(corner_kernel, proc),
        out_shape=edge_shape,
        in_specs=[VMEM],
        out_specs=VMEM,
        compiler_params=params(4),
        cost_estimate=SMALL,
        name="corner",
    )(lat_got)
    grad_side_first = lax.ppermute(grad_side, "lon", lon_pairs[0])
    grad_side_second = lax.ppermute(grad_side, "lon", lon_pairs[1])

    gradient, radiance = pl.pallas_call(
        functools.partial(scatter_kernel, (levels, rows, width, pad, proc, n_lat, n_lon)),
        out_shape=(
            shape((2 * levels * rows, width), F32),
            shape((1, proc, channels), F32),
        ),
        in_specs=[VMEM] * 8,
        out_specs=(HBM, VMEM),
        scratch_shapes=[
            pltpu.VMEM((3, width, obs), BF16),
            pltpu.VMEM((EDGE, feat), F32),
            pltpu.VMEM((width // LANES, 2 * levels * rows, LANES), F32),
            pltpu.SemaphoreType.DMA((width // LANES,)),
        ],
        compiler_params=params(20),
        name="scatter",
    )(obs_cell, obs_weight, grad, grad_first, grad_second, grad_side_first, grad_side_second, lat_got)
    return radiance, gradient.reshape(2, levels, rows, width)


def solution(mesh):
    placed = (
        P("groups", None, "lat", "lon"),
        P(("groups", "lon"), "lat"),
        P("groups", "lon", "lat"),
        P(("groups", "lon"), "lat"),
        P(("groups", "lon"), "lat"),
        P(),
        P(("groups", "lon"), "lat", None),
    )
    return jax.shard_map(
        per_device,
        mesh=mesh,
        in_specs=placed,
        out_specs=(P(("groups", "lon"), "lat", None), P("groups", None, "lat", "lon")),
        check_vma=False,
    )
```

```python
import functools

import jax
import jax.numpy as jnp
from jax import lax
from jax.experimental import pallas as pl
from jax.experimental.pallas import tpu as pltpu
from jax.sharding import PartitionSpec as P

F32 = jnp.float32
BF16 = jnp.bfloat16
LOG2E = 1.4426950408889634
LANES = 128
EDGE = 16
BLOCKS = 2
VMEM = pl.BlockSpec(memory_space=pltpu.VMEM)
SMEM = pl.BlockSpec(memory_space=pltpu.SMEM)
HBM = pl.BlockSpec(memory_space=pltpu.HBM)
SMALL = pl.CostEstimate(flops=1000, bytes_accessed=1000, transcendentals=0)
NN = (((1,), (0,)), ((), ()))
NT = (((1,), (1,)), ((), ()))
TN = (((0,), (0,)), ((), ()))


def dot(a, b, dims=NN):
    return lax.dot_general(a, b, dims, preferred_element_type=F32)


def round_up(value, unit):
    return -(-value // unit) * unit


def params(mib):
    return pltpu.CompilerParams(vmem_limit_bytes=mib * 1024 * 1024)


def iota(shape, dim):
    return lax.broadcasted_iota(jnp.int32, shape, dim)


def split_cells(cells, width):
    if width & (width - 1) == 0:
        return lax.shift_right_logical(cells, width.bit_length() - 1), cells & (width - 1)
    row = lax.div(cells, width)
    return row, cells - row * width


def fill_columns(cells_ref, weight_ref, columns_ref):
    width, obs = columns_ref.shape[1:]
    _, col = split_cells(cells_ref[...], width)
    weights = [weight_ref[k] for k in range(9)]
    step = 32

    def chunk(i, carry):
        base = pl.multiple_of(i * step, step)
        for lane in range(0, obs, LANES):
            part = slice(lane, lane + LANES)
            away = iota((step, LANES), 0) + base - col[:, part]
            hit = [away == b - 1 for b in range(3)]
            for a in range(3):
                value = jnp.zeros((step, LANES), F32)
                for b in range(3):
                    value = jnp.where(hit[b], weights[3 * a + b][:, part], value)
                columns_ref[a, pl.ds(base, step), part] = value.astype(BF16)
        return carry

    lax.fori_loop(0, width // step, chunk, 0)


def row_stencil(columns_ref, row_of, r, part=slice(None)):
    total = None
    for a in range(3):
        keep = jnp.where(row_of == r - a + 1, 1.0, 0.0).astype(BF16)
        term = columns_ref[a, part, :] * keep
        total = term if total is None else total + term
    return total


def edge_weights(cells_ref, weight_ref, rows, width):
    lines = BLOCKS * EDGE
    obs = cells_ref.shape[1]
    row, col = split_cells(cells_ref[...], width)
    line = iota((lines, obs), 0)
    block = lax.shift_right_logical(line, 4)
    k = line & (EDGE - 1)
    none = -99
    west = k >= rows
    col_at = jnp.where(west, -1, width)
    row_at = jnp.where(west, k - rows, k)
    corner = jnp.where(row_at == rows - 1, -1, jnp.where(row_at == 0, rows, none))
    row_at = jnp.where(block == 1, corner, row_at)
    total = jnp.zeros((lines, obs), F32)
    for a in range(3):
        for b in range(3):
            hit = (row_at == row + (a - 1)) & (col_at == col + (b - 1))
            total = total + jnp.where(hit, weight_ref[3 * a + b], 0.0)
    return total.astype(BF16)


def pairs(count, offset, ring):
    swap = [(i, i + 1) for i in range(offset, count - 1, 2)]
    if ring and offset and count % 2 == 0 and count > 2:
        swap.append((0, count - 1))
    return sorted(swap + [(b, a) for a, b in swap])


def pair_place(axis):
    at = lax.axis_index(axis)
    return (at & 1) == 0, at


def pair_rows(rows, count):
    even, at = pair_place("lat")
    below = jnp.where(at < count - 1, rows, -99)
    above = jnp.where(at > 0, -1, -99)
    return jnp.where(even, below, above), jnp.where(even, above, below)


def choose(pred, a, b):
    return jnp.where(pred, a.astype(F32), b.astype(F32))


def from_sides(first, second, count):
    even, at = pair_place("lon")
    west = choose(even, second, first) * jnp.where(at > 0, 1.0, 0.0)
    east = choose(even, first, second) * jnp.where(at < count - 1, 1.0, 0.0)
    return west, east


def copies(pairs_of, sems):
    moves = [pltpu.make_async_copy(source, target, sems.at[k]) for k, (source, target) in enumerate(pairs_of)]
    for move in moves:
        move.start()
    return moves


def load_profiles(profiles_hbm, part_ref, sems):
    tiles = part_ref.shape[0]
    return copies(
        [(profiles_hbm.at[:, :, t * LANES : (t + 1) * LANES], part_ref.at[t]) for t in range(tiles)], sems
    )


def widen(t, part_ref, wide_ref):
    wide_ref[t] = part_ref[t].astype(F32).reshape(wide_ref.shape[1:])


def grid_row(levels, rows, pad, wide_ref, t, r):
    blank = jnp.zeros((pad - levels, LANES), F32)
    halves = []
    for v in range(2):
        halves += [wide_ref[t, pl.ds(v * levels * rows + r, levels, stride=rows), :], blank]
    return jnp.concatenate(halves, axis=0).astype(BF16)


def pack_kernel(
    dims,
    profiles_hbm,
    cot_hbm,
    first_ref,
    second_ref,
    edge_ref,
    send_ref,
    part_ref,
    wide_ref,
    ends_ref,
    cot_ref,
    sems,
    cot_sem,
):
    levels, rows, width, pad = dims
    tiles = width // LANES
    loads = load_profiles(profiles_hbm, part_ref, sems)
    cot_load = copies([(cot_hbm, cot_ref)], cot_sem)[0]
    edges = jnp.zeros((EDGE, 2 * pad), F32)
    k = iota((EDGE, LANES), 0)
    at_lane = iota((EDGE, LANES), 1)
    for t in range(tiles):
        loads[t].wait()
        widen(t, part_ref, wide_ref)
        for r in range(rows):
            if 0 < r < rows - 1 and 0 < t < tiles - 1:
                continue
            value = grid_row(levels, rows, pad, wide_ref, t, r)
            if r in (0, rows - 1):
                ends_ref[min(r, 1), :, t * LANES : (t + 1) * LANES] = value
            if t == 0:
                at = jnp.where((k == r) & (at_lane == 0), 1.0, 0.0).astype(BF16)
                edges = edges + dot(at, value, NT)
            if t == tiles - 1:
                at = jnp.where((k == rows + r) & (at_lane == LANES - 1), 1.0, 0.0).astype(BF16)
                edges = edges + dot(at, value, NT)
    edge_ref[...] = jnp.zeros(edge_ref.shape, BF16)
    edge_ref[:, : 2 * pad] = edges.astype(BF16)
    even, _ = pair_place("lat")
    first_ref[...] = ends_ref[jnp.where(even, 1, 0)]
    second_ref[...] = ends_ref[jnp.where(even, 0, 1)]
    proc = cot_ref.shape[1]
    cot_load.wait()
    cot = cot_ref[0].astype(BF16)

    def share(s, carry):
        send_ref[s, 0:proc, :] = cot
        for t in range(edge_ref.shape[1] // LANES):
            send_ref[s, proc + EDGE * t : proc + EDGE * (t + 1), :] = edge_ref[:, t * LANES : (t + 1) * LANES]
        return carry

    lax.fori_loop(0, send_ref.shape[0], share, 0)


def lat_block(ref, proc, side):
    at = lax.axis_index("lat") + side
    valid = (at >= 0) & (at < ref.shape[0])
    at = jnp.where(valid, at, 0)
    keep = jnp.where(valid, 1.0, 0.0)
    parts = [ref[at, proc + EDGE * t : proc + EDGE * (t + 1), :] for t in range((ref.shape[1] - proc) // EDGE)]
    return [part.astype(F32) * keep for part in parts]


def blend_kernel(rows, proc, edge_ref, lat_ref, out_ref):
    k = iota((EDGE, LANES), 0)
    last = (k == rows - 1) | (k == 2 * rows - 1)
    first = (k == 0) | (k == rows)
    ups, downs = lat_block(lat_ref, proc, -1), lat_block(lat_ref, proc, 1)
    out_ref[0:EDGE, :] = edge_ref[...]
    for t in range(edge_ref.shape[1] // LANES):
        corner = jnp.where(last, ups[t], jnp.where(first, downs[t], 0.0))
        out_ref[EDGE : 2 * EDGE, t * LANES : (t + 1) * LANES] = corner.astype(BF16)


def gather_rows(rows, row, columns_ref, rows_ref, field_ref):
    for r in range(rows):
        value = dot(rows_ref[r], row_stencil(columns_ref, row, r))
        if r == 0:
            field_ref[...] = value
        else:
            field_ref[...] += value


def gather_halo(halo_rows, row, columns_ref, first_ref, second_ref, field_ref):
    field_ref[...] += dot(first_ref[...], row_stencil(columns_ref, row, halo_rows[0]))
    field_ref[...] += dot(second_ref[...], row_stencil(columns_ref, row, halo_rows[1]))


def gather_edges(rows, pad, n_lon, first_ref, second_ref, halo_ref, edge_w, field_ref):
    west = (iota(halo_ref.shape, 0) & (EDGE - 1)) >= rows
    from_west, from_east = from_sides(first_ref[...], second_ref[...], n_lon)
    halo_ref[...] = jnp.where(west, from_west, from_east)
    field_ref[...] += dot(halo_ref[:, : 2 * pad].astype(BF16), edge_w, TN)


def departures(batch, proc, dest_ref, lat_ref, cot_rows_ref, cot_t_ref):
    obs = cot_rows_ref.shape[0]
    owned = proc // batch
    for q in range(obs // batch):
        where = dest_ref[0, q]
        slot = jnp.maximum(where, 0)
        lat = lax.div(slot, owned)
        start = pl.multiple_of((slot - lat * owned) * batch, batch)
        value = lat_ref[lat, pl.ds(start, batch), :].astype(F32)
        cot_rows_ref[q * batch : (q + 1) * batch, :] = jnp.where(where >= 0, value, 0.0)
    for lane in range(0, obs, LANES):
        cot_t_ref[:, lane : lane + LANES] = cot_rows_ref[lane : lane + LANES, :].T


def chosen_instruments(batch, obs, instr_ref):
    lane_slot = lax.shift_right_logical(iota((1, obs), 1), batch.bit_length() - 1)
    chosen = jnp.zeros((1, obs), jnp.int32)
    for q in range(obs // batch):
        chosen = jnp.where(lane_slot == q, instr_ref[0, q], chosen)
    return chosen


def turn_absorption(absorb_ref, turned_ref):
    levels, instruments, channels = absorb_ref.shape
    per = LANES // instruments
    for b in range(turned_ref.shape[0]):
        count = min(per, levels - b * per)
        block = absorb_ref[b * per : b * per + count].astype(F32).reshape(count * instruments, channels)
        if count < per:
            block = jnp.concatenate([block, jnp.zeros(((per - count) * instruments, channels), F32)], axis=0)
        turned_ref[b] = block.T


def prepare_levels(pad, field_ref, step_ref, rate_ref):
    step_ref[...] = field_ref[1 : pad + 1, :] - field_ref[0:pad, :]
    rate_ref[...] = -LOG2E * (1.0 + 0.5 * jnp.tanh(field_ref[pad : 2 * pad, :]))


def walk_levels(levels, instruments, chosen, turned_ref, cot_t_ref, rate_ref, step_ref, signal_ref, s_part_ref, r_part_ref):
    channels, obs = cot_t_ref.shape
    groups, padded, _ = s_part_ref.shape
    per = LANES // instruments
    tail = jnp.zeros((groups, padded - levels * 8, LANES), F32)
    s_part_ref[:, levels * 8 :, :] = tail
    r_part_ref[:, levels * 8 :, :] = tail
    for lane in range(0, obs, LANES):
        lanes = slice(lane, lane + LANES)
        group = lane // LANES

        def level(b, row_base, j, rates, steps, cum, signal):
            index = jnp.broadcast_to(chosen[:, lanes] + instruments * j, (8, LANES))
            a = jnp.concatenate(
                [
                    jnp.take_along_axis(turned_ref[b, c : c + 8, :], index, axis=1, mode="promise_in_bounds")
                    for c in range(0, channels, 8)
                ],
                axis=0,
            )
            cot = cot_t_ref[:, lanes]
            cum = cum + a * rates[j : j + 1]
            transmit = jnp.exp2(cum)
            at = pl.ds(pl.multiple_of(row_base + 8 * j, 8), 8)
            r_part_ref[group, at, :] = jnp.sum((cot * signal * a).reshape(channels // 8, 8, LANES), axis=0)
            s_part_ref[group, at, :] = jnp.sum((cot * transmit).reshape(channels // 8, 8, LANES), axis=0)
            signal = signal + transmit * steps[j : j + 1]
            return cum, signal

        def block(b, carry):
            cum, signal = carry
            base = pl.multiple_of(b * per, per)
            rates = rate_ref[pl.ds(base, per), lanes]
            steps = step_ref[pl.ds(base, per), lanes]
            for j in range(per):
                cum, signal = level(b, b * (8 * per), j, rates, steps, cum, signal)
            return cum, signal

        start = jnp.zeros((channels, LANES), F32)
        full = levels // per
        cum, signal = lax.fori_loop(0, full, block, (start, start))
        if levels % per:
            rates = rate_ref[full * per : (full + 1) * per, lanes]
            steps = step_ref[full * per : (full + 1) * per, lanes]
            for j in range(levels % per):
                cum, signal = level(full, full * (8 * per), j, rates, steps, cum, signal)
        signal_ref[:, lanes] = signal


def radiances(batch, proc, dest_ref, signal_ref, field_ref, send_ref):
    obs = signal_ref.shape[1]
    owned = proc // batch
    send_ref[...] = jnp.zeros(send_ref.shape, BF16)
    for lane in range(0, obs, LANES):
        lanes = slice(lane, lane + LANES)
        value = (signal_ref[:, lanes] + field_ref[0:1, lanes]).T.astype(BF16)
        for q in range(LANES // batch):
            where = dest_ref[0, lane // batch + q]

            @pl.when(where >= 0)
            def _():
                lat = lax.div(where, owned)
                start = pl.multiple_of((where - lat * owned) * batch, batch)
                send_ref[lat, pl.ds(start, batch), :] = value[q * batch : (q + 1) * batch, :]


def held_part(levels, pick, absorb_ref, cot_t_ref, signal_ref, r_part_ref):
    channels, obs = cot_t_ref.shape
    instruments = absorb_ref.shape[1]
    held = cot_t_ref[...] * signal_ref[...]
    held_hi = held.astype(BF16)
    held_lo = (held - held_hi.astype(F32)).astype(BF16)
    halves = jnp.concatenate([held_hi, held_lo], axis=0)

    def contract(l0, count):
        rows_in = absorb_ref[pl.ds(l0, count)].reshape(count * instruments, channels)
        value = dot(jnp.concatenate([rows_in, rows_in], axis=1), halves)
        value = value.reshape(count, instruments, obs) * pick[None]
        value = jnp.sum(value.reshape(count, instruments // 8, 8, obs), axis=1)
        at = pl.ds(pl.multiple_of(l0 * 8, 8), count * 8)
        value = value.reshape(count * 8, obs)
        for lane in range(0, obs, LANES):
            r_part_ref[lane // LANES, at, :] -= value[:, lane : lane + LANES]

    step = 32

    def contract_block(b, carry):
        contract(b * step, step)
        return carry

    lax.fori_loop(0, levels // step, contract_block, 0)
    if levels % step:
        contract(levels // step * step, levels % step)


def gradients(pad, s_part_ref, r_part_ref, cot_t_ref, field_ref, shift_ref, grad_ref):
    obs = cot_t_ref.shape[1]
    for lane in range(0, obs, LANES):
        lanes = slice(lane, lane + LANES)
        group = lane // LANES
        s_sum = s_part_ref[group, pl.ds(0, pad, stride=8), :]
        r_sum = r_part_ref[group, pl.ds(0, pad, stride=8), :]
        for k in range(1, 8):
            s_sum = s_sum + s_part_ref[group, pl.ds(k, pad, stride=8), :]
            r_sum = r_sum + r_part_ref[group, pl.ds(k, pad, stride=8), :]
        shift_ref[7:8, lanes] = jnp.sum(cot_t_ref[:, lanes], axis=0, keepdims=True)
        shift_ref[8 : 8 + pad, lanes] = s_sum
        grad_ref[0:pad, lanes] = (shift_ref[7 : 7 + pad, lanes] - s_sum).astype(BF16)
        bent = jnp.tanh(field_ref[pad : 2 * pad, lanes])
        grad_ref[pad : 2 * pad, lanes] = (0.5 * (1.0 - bent * bent) * r_sum).astype(BF16)


def scatter_outside(
    rows, pad, proc, halo_rows, row, columns_ref, edge_w, grad_ref, first_ref, second_ref, edge_ref, send_ref
):
    grad = grad_ref[...]
    first_ref[...] = dot(grad, row_stencil(columns_ref, row, halo_rows[0]), NT).astype(BF16)
    second_ref[...] = dot(grad, row_stencil(columns_ref, row, halo_rows[1]), NT).astype(BF16)
    out = dot(edge_w, grad, NT)
    edge_ref[...] = jnp.zeros(edge_ref.shape, F32)
    edge_ref[:, : 2 * pad] = out
    k = iota((EDGE, LANES), 0)
    last = (k == rows - 1) | (k == 2 * rows - 1)
    first = (k == 0) | (k == rows)
    for side, mine in ((-1, last), (1, first)):
        at = lax.axis_index("lat") + side

        @pl.when((at >= 0) & (at < send_ref.shape[0]))
        def _():
            for t in range(edge_ref.shape[1] // LANES):
                part = edge_ref[EDGE : 2 * EDGE, t * LANES : (t + 1) * LANES]
                part = jnp.where(mine, part, 0.0).astype(BF16)
                send_ref[at, proc + EDGE * t : proc + EDGE * (t + 1), :] = part

    for t in range(edge_ref.shape[1] // LANES):
        part = edge_ref[0:EDGE, t * LANES : (t + 1) * LANES].astype(BF16)
        send_ref[lax.axis_index("lat"), proc + EDGE * t : proc + EDGE * (t + 1), :] = part


def gather_kernel(
    dims,
    cells_ref,
    weight_ref,
    absorb_ref,
    profiles_hbm,
    field_hbm,
    turned_hbm,
    part_ref,
    wide_ref,
    rows_ref,
    columns_ref,
    field_ref,
    turned_ref,
    sems,
    out_sems,
):
    levels, rows, width, pad = dims
    loads = load_profiles(profiles_hbm, part_ref, sems)
    fill_columns(cells_ref, weight_ref, columns_ref)
    row, _ = split_cells(cells_ref[...], width)
    turn_absorption(absorb_ref, turned_ref)
    outs = copies([(turned_ref, turned_hbm)], out_sems.at[pl.ds(0, 1)])
    for t in range(width // LANES):
        loads[t].wait()
        widen(t, part_ref, wide_ref)
        for r in range(rows):
            rows_ref[r, :, t * LANES : (t + 1) * LANES] = grid_row(levels, rows, pad, wide_ref, t, r)
    gather_rows(rows, row, columns_ref, rows_ref, field_ref)
    outs += copies([(field_ref, field_hbm)], out_sems.at[pl.ds(1, 1)])
    for move in outs:
        move.wait()


def transfer_kernel(
    dims,
    cells_ref,
    weight_ref,
    instr_ref,
    dest_ref,
    absorb_ref,
    side_first_ref,
    side_second_ref,
    field_hbm,
    turned_hbm,
    row_first_hbm,
    row_second_hbm,
    lat_hbm,
    grad_ref,
    grad_first_ref,
    grad_second_ref,
    send_ref,
    columns_ref,
    turned_ref,
    halo_ref,
    field_ref,
    rate_ref,
    step_ref,
    cot_rows_ref,
    cot_t_ref,
    signal_ref,
    s_part_ref,
    r_part_ref,
    shift_ref,
    row_first_ref,
    row_second_ref,
    lat_ref,
    sems,
):
    levels, rows, width, pad, batch, proc, n_lat, n_lon = dims
    moves = [
        pltpu.make_async_copy(source, target, sems.at[k])
        for k, (source, target) in enumerate(
            (
                (field_hbm, field_ref),
                (turned_hbm, turned_ref),
                (row_first_hbm, row_first_ref),
                (row_second_hbm, row_second_ref),
                (lat_hbm, lat_ref),
            )
        )
    ]
    for move in moves:
        move.start()
    obs = cells_ref.shape[1]
    instruments = absorb_ref.shape[1]
    fill_columns(cells_ref, weight_ref, columns_ref)
    row, _ = split_cells(cells_ref[...], width)
    halo_rows = pair_rows(rows, n_lat)
    edge_w = edge_weights(cells_ref, weight_ref, rows, width)
    moves[4].wait()
    departures(batch, proc, dest_ref, lat_ref, cot_rows_ref, cot_t_ref)
    for k in (0, 2, 3):
        moves[k].wait()
    gather_halo(halo_rows, row, columns_ref, row_first_ref, row_second_ref, field_ref)
    gather_edges(rows, pad, n_lon, side_first_ref, side_second_ref, halo_ref, edge_w, field_ref)
    chosen = chosen_instruments(batch, obs, instr_ref)
    prepare_levels(pad, field_ref, step_ref, rate_ref)
    moves[1].wait()
    walk_levels(
        levels, instruments, chosen, turned_ref, cot_t_ref, rate_ref, step_ref, signal_ref, s_part_ref, r_part_ref
    )
    radiances(batch, proc, dest_ref, signal_ref, field_ref, send_ref)
    pick = jnp.where(iota((instruments, obs), 0) == chosen, 1.0, 0.0)
    held_part(levels, pick, absorb_ref, cot_t_ref, signal_ref, r_part_ref)
    gradients(pad, s_part_ref, r_part_ref, cot_t_ref, field_ref, shift_ref, grad_ref)
    scatter_outside(
        rows,
        pad,
        proc,
        halo_rows,
        row,
        columns_ref,
        edge_w,
        grad_ref,
        grad_first_ref,
        grad_second_ref,
        halo_ref,
        send_ref,
    )


def corner_kernel(proc, lat_ref, out_ref):
    owns, ups, downs = [lat_block(lat_ref, proc, side) for side in (0, -1, 1)]
    for t in range(out_ref.shape[1] // LANES):
        out_ref[:, t * LANES : (t + 1) * LANES] = (owns[t] + ups[t] + downs[t]).astype(BF16)


def scatter_kernel(
    dims,
    cells_ref,
    weight_ref,
    grad_ref,
    row_first_ref,
    row_second_ref,
    side_first_ref,
    side_second_ref,
    lat_ref,
    out_ref,
    rad_out_ref,
    columns_ref,
    halo_ref,
    wide_ref,
    sems,
):
    levels, rows, width, pad, proc, n_lat, n_lon = dims
    fill_columns(cells_ref, weight_ref, columns_ref)
    even, at_lat = pair_place("lat")
    inside = jnp.where(at_lat > 0, 1.0, 0.0), jnp.where(at_lat < n_lat - 1, 1.0, 0.0)
    rad_out_ref[...] = jnp.sum(lat_ref[:, 0:proc, :].astype(F32), axis=0)[None]
    row, _ = split_cells(cells_ref[...], width)
    west = iota(halo_ref.shape, 0) < rows
    from_west, from_east = from_sides(side_first_ref[...], side_second_ref[...], n_lon)
    halo_ref[...] = jnp.where(west, from_west, from_east)
    edges = halo_ref[:, : 2 * pad].T.astype(BF16)
    k = iota((EDGE, LANES), 0)
    at_lane = iota((EDGE, LANES), 1)
    moves = []
    half = 2 * LANES if width % (2 * LANES) == 0 else LANES
    for start in range(0, width, half):
        part = slice(start, start + half)
        for r in range(rows):
            value = dot(grad_ref[...], row_stencil(columns_ref, row, r, part), NT)
            if r == 0:
                value = value + choose(even, row_second_ref[:, part], row_first_ref[:, part]) * inside[0]
            if r == rows - 1:
                value = value + choose(even, row_first_ref[:, part], row_second_ref[:, part]) * inside[1]
            for lane in range(start, start + half, LANES):
                piece = value[:, lane - start : lane - start + LANES]
                if lane == 0:
                    piece = piece + dot(edges, jnp.where((k == r) & (at_lane == 0), 1.0, 0.0).astype(BF16))
                if lane + LANES == width:
                    last_at = jnp.where((k == rows + r) & (at_lane == LANES - 1), 1.0, 0.0).astype(BF16)
                    piece = piece + dot(edges, last_at)
                for v in range(2):
                    at = pl.ds(v * levels * rows + r, levels, stride=rows)
                    wide_ref[lane // LANES, at, :] = piece[v * pad : v * pad + levels, :]
        for lane in range(start, start + half, LANES):
            t = lane // LANES
            move = pltpu.make_async_copy(wide_ref.at[t], out_ref.at[:, lane : lane + LANES], sems.at[t])
            move.start()
            moves.append(move)
    for move in moves:
        move.wait()


def per_device(profiles, obs_cell, obs_weight, batch_instr, batch_dest, absorption, cotangent):
    n_lat, n_lon = lax.axis_size("lat"), lax.axis_size("lon")
    levels, rows, width = profiles.shape[1:]
    instruments, channels, _ = absorption.shape
    obs = obs_cell.shape[1]
    slots = batch_dest.shape[1]
    batch = obs // slots
    proc = cotangent.shape[1]
    pad = round_up(levels, 16)
    feat = round_up(2 * pad, LANES)
    lat_rows = proc + EDGE * (feat // LANES)
    blocks = -(-levels * instruments // LANES)
    lat_pairs = [pairs(n_lat, offset, False) for offset in (0, 1)]
    lon_pairs = [pairs(n_lon, offset, True) for offset in (0, 1)]
    shape = jax.ShapeDtypeStruct
    row_shape = shape((2 * pad, width), BF16)
    edge_shape = shape((EDGE, feat), BF16)
    lat_shape = shape((n_lat, lat_rows, channels), BF16)
    absorb = jnp.transpose(absorption, (2, 0, 1))

    profiles = profiles.reshape(2 * levels, rows, width)
    tiles = width // LANES
    unpacked = [
        pltpu.VMEM((tiles, 2 * levels, rows, LANES), BF16),
        pltpu.VMEM((tiles, 2 * levels * rows, LANES), F32),
    ]
    row_first, row_second, edge, lat_send = pl.pallas_call(
        functools.partial(pack_kernel, (levels, rows, width, pad)),
        out_shape=(row_shape, row_shape, edge_shape, lat_shape),
        in_specs=[HBM] * 2,
        out_specs=(VMEM,) * 4,
        scratch_shapes=unpacked
        + [
            pltpu.VMEM((2, 2 * pad, width), BF16),
            pltpu.VMEM((1, proc, channels), F32),
            pltpu.SemaphoreType.DMA((tiles,)),
            pltpu.SemaphoreType.DMA((1,)),
        ],
        compiler_params=params(56),
        name="pack",
    )(profiles, cotangent)

    lat_in = lax.all_to_all(lat_send, "lat", 0, 0, tiled=True)
    row_first = lax.ppermute(row_first, "lat", lat_pairs[0])
    row_second = lax.ppermute(row_second, "lat", lat_pairs[1])

    field, turned = pl.pallas_call(
        functools.partial(gather_kernel, (levels, rows, width, pad)),
        out_shape=(shape((2 * pad, obs), F32), shape((blocks, channels, LANES), F32)),
        in_specs=[VMEM] * 3 + [HBM],
        out_specs=(HBM,) * 2,
        scratch_shapes=unpacked
        + [
            pltpu.VMEM((rows, 2 * pad, width), BF16),
            pltpu.VMEM((3, width, obs), BF16),
            pltpu.VMEM((2 * pad, obs), F32),
            pltpu.VMEM((blocks, channels, LANES), F32),
            pltpu.SemaphoreType.DMA((tiles,)),
            pltpu.SemaphoreType.DMA((2,)),
        ],
        compiler_params=params(56),
        name="gather",
    )(obs_cell, obs_weight, absorb, profiles)
    edge, field = lax.optimization_barrier((edge, field))

    side = pl.pallas_call(
        functools.partial(blend_kernel, rows, proc),
        out_shape=shape((BLOCKS * EDGE, feat), BF16),
        in_specs=[VMEM] * 2,
        out_specs=VMEM,
        compiler_params=params(4),
        cost_estimate=SMALL,
        name="blend",
    )(edge, lat_in)
    side_first = lax.ppermute(side, "lon", lon_pairs[0])
    side_second = lax.ppermute(side, "lon", lon_pairs[1])

    grad, grad_first, grad_second, lat_back = pl.pallas_call(
        functools.partial(transfer_kernel, (levels, rows, width, pad, batch, proc, n_lat, n_lon)),
        out_shape=(shape((2 * pad, obs), BF16), row_shape, row_shape, lat_shape),
        in_specs=[VMEM, VMEM, SMEM, SMEM] + [VMEM] * 3 + [HBM] * 5,
        out_specs=(VMEM,) * 4,
        scratch_shapes=[
            pltpu.VMEM((3, width, obs), BF16),
            pltpu.VMEM((blocks, channels, LANES), F32),
            pltpu.VMEM((BLOCKS * EDGE, feat), F32),
            pltpu.VMEM((2 * pad, obs), F32),
            pltpu.VMEM((pad, obs), F32),
            pltpu.VMEM((pad, obs), F32),
            pltpu.VMEM((obs, channels), F32),
            pltpu.VMEM((channels, obs), F32),
            pltpu.VMEM((channels, obs), F32),
            pltpu.VMEM((obs // LANES, pad * 8, LANES), F32),
            pltpu.VMEM((obs // LANES, pad * 8, LANES), F32),
            pltpu.VMEM((pad + 8, obs), F32),
            pltpu.VMEM(row_shape.shape, BF16),
            pltpu.VMEM(row_shape.shape, BF16),
            pltpu.VMEM(lat_shape.shape, BF16),
            pltpu.SemaphoreType.DMA((5,)),
        ],
        compiler_params=params(56),
        name="transfer",
    )(
        obs_cell,
        obs_weight,
        batch_instr,
        batch_dest,
        absorb,
        side_first,
        side_second,
        field,
        turned,
        row_first,
        row_second,
        lat_in,
    )

    grad_first = lax.ppermute(grad_first, "lat", lat_pairs[0])
    grad_second = lax.ppermute(grad_second, "lat", lat_pairs[1])
    lat_got = lax.all_to_all(lat_back, "lat", 0, 0, tiled=True)
    grad_side = pl.pallas_call(
        functools.partial(corner_kernel, proc),
        out_shape=edge_shape,
        in_specs=[VMEM],
        out_specs=VMEM,
        compiler_params=params(4),
        cost_estimate=SMALL,
        name="corner",
    )(lat_got)
    grad_side_first = lax.ppermute(grad_side, "lon", lon_pairs[0])
    grad_side_second = lax.ppermute(grad_side, "lon", lon_pairs[1])

    gradient, radiance = pl.pallas_call(
        functools.partial(scatter_kernel, (levels, rows, width, pad, proc, n_lat, n_lon)),
        out_shape=(
            shape((2 * levels * rows, width), F32),
            shape((1, proc, channels), F32),
        ),
        in_specs=[VMEM] * 8,
        out_specs=(HBM, VMEM),
        scratch_shapes=[
            pltpu.VMEM((3, width, obs), BF16),
            pltpu.VMEM((EDGE, feat), F32),
            pltpu.VMEM((width // LANES, 2 * levels * rows, LANES), F32),
            pltpu.SemaphoreType.DMA((width // LANES,)),
        ],
        compiler_params=params(20),
        name="scatter",
    )(obs_cell, obs_weight, grad, grad_first, grad_second, grad_side_first, grad_side_second, lat_got)
    return radiance, gradient.reshape(2, levels, rows, width)


def solution(mesh):
    placed = (
        P("groups", None, "lat", "lon"),
        P(("groups", "lon"), "lat"),
        P("groups", "lon", "lat"),
        P(("groups", "lon"), "lat"),
        P(("groups", "lon"), "lat"),
        P(),
        P(("groups", "lon"), "lat", None),
    )
    return jax.shard_map(
        per_device,
        mesh=mesh,
        in_specs=placed,
        out_specs=(P(("groups", "lon"), "lat", None), P("groups", None, "lat", "lon")),
        check_vma=False,
    )
```

```python
import functools

import jax
import jax.numpy as jnp
from jax import lax
from jax.experimental import pallas as pl
from jax.experimental.pallas import tpu as pltpu
from jax.sharding import PartitionSpec as P

F32 = jnp.float32
BF16 = jnp.bfloat16
LOG2E = 1.4426950408889634
LANES = 128
EDGE = 16
BLOCKS = 2
VMEM = pl.BlockSpec(memory_space=pltpu.VMEM)
SMEM = pl.BlockSpec(memory_space=pltpu.SMEM)
HBM = pl.BlockSpec(memory_space=pltpu.HBM)
SMALL = pl.CostEstimate(flops=1000, bytes_accessed=1000, transcendentals=0)
NN = (((1,), (0,)), ((), ()))
NT = (((1,), (1,)), ((), ()))
TN = (((0,), (0,)), ((), ()))


def dot(a, b, dims=NN):
    return lax.dot_general(a, b, dims, preferred_element_type=F32)


def round_up(value, unit):
    return -(-value // unit) * unit


def params(mib):
    return pltpu.CompilerParams(vmem_limit_bytes=mib * 1024 * 1024)


def iota(shape, dim):
    return lax.broadcasted_iota(jnp.int32, shape, dim)


def split_cells(cells, width):
    if width & (width - 1) == 0:
        return lax.shift_right_logical(cells, width.bit_length() - 1), cells & (width - 1)
    row = lax.div(cells, width)
    return row, cells - row * width


def fill_columns(cells_ref, weight_ref, columns_ref):
    width, obs = columns_ref.shape[1:]
    _, col = split_cells(cells_ref[...], width)
    weights = [weight_ref[k] for k in range(9)]
    step = 64

    def chunk(i, carry):
        base = pl.multiple_of(i * step, step)
        for lane in range(0, obs, LANES):
            part = slice(lane, lane + LANES)
            away = iota((step, LANES), 0) + base - col[:, part]
            hit = [away == b - 1 for b in range(3)]
            for a in range(3):
                value = jnp.zeros((step, LANES), F32)
                for b in range(3):
                    value = jnp.where(hit[b], weights[3 * a + b][:, part], value)
                columns_ref[a, pl.ds(base, step), part] = value.astype(BF16)
        return carry

    lax.fori_loop(0, width // step, chunk, 0)


def row_stencil(columns_ref, row_of, r, part=slice(None)):
    total = None
    for a in range(3):
        keep = jnp.where(row_of == r - a + 1, 1.0, 0.0).astype(BF16)
        term = columns_ref[a, part, :] * keep
        total = term if total is None else total + term
    return total


def edge_weights(cells_ref, weight_ref, rows, width):
    lines = BLOCKS * EDGE
    obs = cells_ref.shape[1]
    row, col = split_cells(cells_ref[...], width)
    line = iota((lines, obs), 0)
    block = lax.shift_right_logical(line, 4)
    k = line & (EDGE - 1)
    none = -99
    west = k >= rows
    col_at = jnp.where(west, -1, width)
    row_at = jnp.where(west, k - rows, k)
    corner = jnp.where(row_at == rows - 1, -1, jnp.where(row_at == 0, rows, none))
    row_at = jnp.where(block == 1, corner, row_at)
    total = jnp.zeros((lines, obs), F32)
    for a in range(3):
        for b in range(3):
            hit = (row_at == row + (a - 1)) & (col_at == col + (b - 1))
            total = total + jnp.where(hit, weight_ref[3 * a + b], 0.0)
    return total.astype(BF16)


def pairs(count, offset, ring):
    swap = [(i, i + 1) for i in range(offset, count - 1, 2)]
    if ring and offset and count % 2 == 0 and count > 2:
        swap.append((0, count - 1))
    return sorted(swap + [(b, a) for a, b in swap])


def pair_place(axis):
    at = lax.axis_index(axis)
    return (at & 1) == 0, at


def pair_rows(rows, count):
    even, at = pair_place("lat")
    below = jnp.where(at < count - 1, rows, -99)
    above = jnp.where(at > 0, -1, -99)
    return jnp.where(even, below, above), jnp.where(even, above, below)


def choose(pred, a, b):
    return jnp.where(pred, a.astype(F32), b.astype(F32))


def from_sides(first, second, count):
    even, at = pair_place("lon")
    west = choose(even, second, first) * jnp.where(at > 0, 1.0, 0.0)
    east = choose(even, first, second) * jnp.where(at < count - 1, 1.0, 0.0)
    return west, east


def copies(pairs_of, sems):
    moves = [pltpu.make_async_copy(source, target, sems.at[k]) for k, (source, target) in enumerate(pairs_of)]
    for move in moves:
        move.start()
    return moves


def load_profiles(profiles_hbm, part_ref, sems):
    tiles = part_ref.shape[0]
    return copies(
        [(profiles_hbm.at[:, :, t * LANES : (t + 1) * LANES], part_ref.at[t]) for t in range(tiles)], sems
    )


def widen(t, part_ref, wide_ref):
    wide_ref[t] = part_ref[t].astype(F32).reshape(wide_ref.shape[1:])


def grid_row(levels, rows, pad, wide_ref, t, r):
    blank = jnp.zeros((pad - levels, LANES), F32)
    halves = []
    for v in range(2):
        halves += [wide_ref[t, pl.ds(v * levels * rows + r, levels, stride=rows), :], blank]
    return jnp.concatenate(halves, axis=0).astype(BF16)


def pack_kernel(
    dims,
    profiles_hbm,
    cot_hbm,
    first_ref,
    second_ref,
    edge_ref,
    send_ref,
    part_ref,
    wide_ref,
    ends_ref,
    cot_ref,
    sems,
    cot_sem,
):
    levels, rows, width, pad = dims
    tiles = width // LANES
    loads = load_profiles(profiles_hbm, part_ref, sems)
    cot_load = copies([(cot_hbm, cot_ref)], cot_sem)[0]
    edges = jnp.zeros((EDGE, 2 * pad), F32)
    k = iota((EDGE, LANES), 0)
    at_lane = iota((EDGE, LANES), 1)
    for t in range(tiles):
        loads[t].wait()
        widen(t, part_ref, wide_ref)
        for r in range(rows):
            if 0 < r < rows - 1 and 0 < t < tiles - 1:
                continue
            value = grid_row(levels, rows, pad, wide_ref, t, r)
            if r in (0, rows - 1):
                ends_ref[min(r, 1), :, t * LANES : (t + 1) * LANES] = value
            if t == 0:
                at = jnp.where((k == r) & (at_lane == 0), 1.0, 0.0).astype(BF16)
                edges = edges + dot(at, value, NT)
            if t == tiles - 1:
                at = jnp.where((k == rows + r) & (at_lane == LANES - 1), 1.0, 0.0).astype(BF16)
                edges = edges + dot(at, value, NT)
    edge_ref[...] = jnp.zeros(edge_ref.shape, BF16)
    edge_ref[:, : 2 * pad] = edges.astype(BF16)
    even, _ = pair_place("lat")
    first_ref[...] = ends_ref[jnp.where(even, 1, 0)]
    second_ref[...] = ends_ref[jnp.where(even, 0, 1)]
    proc = cot_ref.shape[1]
    cot_load.wait()
    cot = cot_ref[0].astype(BF16)

    def share(s, carry):
        send_ref[s, 0:proc, :] = cot
        for t in range(edge_ref.shape[1] // LANES):
            send_ref[s, proc + EDGE * t : proc + EDGE * (t + 1), :] = edge_ref[:, t * LANES : (t + 1) * LANES]
        return carry

    lax.fori_loop(0, send_ref.shape[0], share, 0)


def lat_block(ref, proc, side):
    at = lax.axis_index("lat") + side
    valid = (at >= 0) & (at < ref.shape[0])
    at = jnp.where(valid, at, 0)
    keep = jnp.where(valid, 1.0, 0.0)
    parts = [ref[at, proc + EDGE * t : proc + EDGE * (t + 1), :] for t in range((ref.shape[1] - proc) // EDGE)]
    return [part.astype(F32) * keep for part in parts]


def blend_kernel(rows, proc, edge_ref, lat_ref, out_ref):
    k = iota((EDGE, LANES), 0)
    last = (k == rows - 1) | (k == 2 * rows - 1)
    first = (k == 0) | (k == rows)
    ups, downs = lat_block(lat_ref, proc, -1), lat_block(lat_ref, proc, 1)
    out_ref[0:EDGE, :] = edge_ref[...]
    for t in range(edge_ref.shape[1] // LANES):
        corner = jnp.where(last, ups[t], jnp.where(first, downs[t], 0.0))
        out_ref[EDGE : 2 * EDGE, t * LANES : (t + 1) * LANES] = corner.astype(BF16)


def gather_rows(rows, row, columns_ref, rows_ref, field_ref):
    for r in range(rows):
        value = dot(rows_ref[r], row_stencil(columns_ref, row, r))
        if r == 0:
            field_ref[...] = value
        else:
            field_ref[...] += value


def gather_halo(halo_rows, row, columns_ref, first_ref, second_ref, field_ref):
    field_ref[...] += dot(first_ref[...], row_stencil(columns_ref, row, halo_rows[0]))
    field_ref[...] += dot(second_ref[...], row_stencil(columns_ref, row, halo_rows[1]))


def gather_edges(rows, pad, n_lon, first_ref, second_ref, halo_ref, edge_w, field_ref):
    west = (iota(halo_ref.shape, 0) & (EDGE - 1)) >= rows
    from_west, from_east = from_sides(first_ref[...], second_ref[...], n_lon)
    halo_ref[...] = jnp.where(west, from_west, from_east)
    field_ref[...] += dot(halo_ref[:, : 2 * pad].astype(BF16), edge_w, TN)


def departures(batch, proc, dest_ref, lat_ref, cot_rows_ref, cot_t_ref):
    obs = cot_rows_ref.shape[0]
    owned = proc // batch
    for q in range(obs // batch):
        where = dest_ref[0, q]
        slot = jnp.maximum(where, 0)
        lat = lax.div(slot, owned)
        start = pl.multiple_of((slot - lat * owned) * batch, batch)
        value = lat_ref[lat, pl.ds(start, batch), :].astype(F32)
        cot_rows_ref[q * batch : (q + 1) * batch, :] = jnp.where(where >= 0, value, 0.0)
    for lane in range(0, obs, LANES):
        cot_t_ref[:, lane : lane + LANES] = cot_rows_ref[lane : lane + LANES, :].T


def chosen_instruments(batch, obs, instr_ref):
    lane_slot = lax.shift_right_logical(iota((1, obs), 1), batch.bit_length() - 1)
    chosen = jnp.zeros((1, obs), jnp.int32)
    for q in range(obs // batch):
        chosen = jnp.where(lane_slot == q, instr_ref[0, q], chosen)
    return chosen


def turn_absorption(absorb_ref, turned_ref):
    levels, instruments, channels = absorb_ref.shape
    per = LANES // instruments
    for b in range(turned_ref.shape[0]):
        count = min(per, levels - b * per)
        block = absorb_ref[b * per : b * per + count].astype(F32).reshape(count * instruments, channels)
        if count < per:
            block = jnp.concatenate([block, jnp.zeros(((per - count) * instruments, channels), F32)], axis=0)
        turned_ref[b] = block.T


def prepare_levels(pad, field_ref, step_ref, rate_ref):
    step_ref[...] = field_ref[1 : pad + 1, :] - field_ref[0:pad, :]
    rate_ref[...] = -LOG2E * (1.0 + 0.5 * jnp.tanh(field_ref[pad : 2 * pad, :]))


def walk_levels(levels, instruments, chosen, turned_ref, cot_t_ref, rate_ref, step_ref, signal_ref, s_part_ref, r_part_ref):
    channels, obs = cot_t_ref.shape
    groups, padded, _ = s_part_ref.shape
    per = LANES // instruments
    tail = jnp.zeros((groups, padded - levels * 8, LANES), F32)
    s_part_ref[:, levels * 8 :, :] = tail
    r_part_ref[:, levels * 8 :, :] = tail
    for lane in range(0, obs, LANES):
        lanes = slice(lane, lane + LANES)
        group = lane // LANES

        def level(b, row_base, j, rates, steps, cum, signal):
            index = jnp.broadcast_to(chosen[:, lanes] + instruments * j, (8, LANES))
            a = jnp.concatenate(
                [
                    jnp.take_along_axis(turned_ref[b, c : c + 8, :], index, axis=1, mode="promise_in_bounds")
                    for c in range(0, channels, 8)
                ],
                axis=0,
            )
            cot = cot_t_ref[:, lanes]
            cum = cum + a * rates[j : j + 1]
            transmit = jnp.exp2(cum)
            at = pl.ds(pl.multiple_of(row_base + 8 * j, 8), 8)
            r_part_ref[group, at, :] = jnp.sum((cot * signal * a).reshape(channels // 8, 8, LANES), axis=0)
            s_part_ref[group, at, :] = jnp.sum((cot * transmit).reshape(channels // 8, 8, LANES), axis=0)
            signal = signal + transmit * steps[j : j + 1]
            return cum, signal

        def block(b, carry):
            cum, signal = carry
            base = pl.multiple_of(b * per, per)
            rates = rate_ref[pl.ds(base, per), lanes]
            steps = step_ref[pl.ds(base, per), lanes]
            for j in range(per):
                cum, signal = level(b, b * (8 * per), j, rates, steps, cum, signal)
            return cum, signal

        start = jnp.zeros((channels, LANES), F32)
        full = levels // per
        cum, signal = lax.fori_loop(0, full, block, (start, start))
        if levels % per:
            rates = rate_ref[full * per : (full + 1) * per, lanes]
            steps = step_ref[full * per : (full + 1) * per, lanes]
            for j in range(levels % per):
                cum, signal = level(full, full * (8 * per), j, rates, steps, cum, signal)
        signal_ref[:, lanes] = signal


def radiances(batch, proc, dest_ref, signal_ref, field_ref, send_ref):
    obs = signal_ref.shape[1]
    owned = proc // batch
    send_ref[...] = jnp.zeros(send_ref.shape, BF16)
    for lane in range(0, obs, LANES):
        lanes = slice(lane, lane + LANES)
        value = (signal_ref[:, lanes] + field_ref[0:1, lanes]).T.astype(BF16)
        for q in range(LANES // batch):
            where = dest_ref[0, lane // batch + q]

            @pl.when(where >= 0)
            def _():
                lat = lax.div(where, owned)
                start = pl.multiple_of((where - lat * owned) * batch, batch)
                send_ref[lat, pl.ds(start, batch), :] = value[q * batch : (q + 1) * batch, :]


def held_part(levels, pick, absorb_ref, cot_t_ref, signal_ref, r_part_ref):
    channels, obs = cot_t_ref.shape
    instruments = absorb_ref.shape[1]
    held = cot_t_ref[...] * signal_ref[...]
    held_hi = held.astype(BF16)
    held_lo = (held - held_hi.astype(F32)).astype(BF16)
    halves = jnp.concatenate([held_hi, held_lo], axis=0)

    def contract(l0, count):
        rows_in = absorb_ref[pl.ds(l0, count)].reshape(count * instruments, channels)
        value = dot(jnp.concatenate([rows_in, rows_in], axis=1), halves)
        value = value.reshape(count, instruments, obs) * pick[None]
        value = jnp.sum(value.reshape(count, instruments // 8, 8, obs), axis=1)
        at = pl.ds(pl.multiple_of(l0 * 8, 8), count * 8)
        value = value.reshape(count * 8, obs)
        for lane in range(0, obs, LANES):
            r_part_ref[lane // LANES, at, :] -= value[:, lane : lane + LANES]

    step = 32

    def contract_block(b, carry):
        contract(b * step, step)
        return carry

    lax.fori_loop(0, levels // step, contract_block, 0)
    if levels % step:
        contract(levels // step * step, levels % step)


def gradients(pad, s_part_ref, r_part_ref, cot_t_ref, field_ref, shift_ref, grad_ref):
    obs = cot_t_ref.shape[1]
    for lane in range(0, obs, LANES):
        lanes = slice(lane, lane + LANES)
        group = lane // LANES
        s_sum = s_part_ref[group, pl.ds(0, pad, stride=8), :]
        r_sum = r_part_ref[group, pl.ds(0, pad, stride=8), :]
        for k in range(1, 8):
            s_sum = s_sum + s_part_ref[group, pl.ds(k, pad, stride=8), :]
            r_sum = r_sum + r_part_ref[group, pl.ds(k, pad, stride=8), :]
        shift_ref[7:8, lanes] = jnp.sum(cot_t_ref[:, lanes], axis=0, keepdims=True)
        shift_ref[8 : 8 + pad, lanes] = s_sum
        grad_ref[0:pad, lanes] = (shift_ref[7 : 7 + pad, lanes] - s_sum).astype(BF16)
        bent = jnp.tanh(field_ref[pad : 2 * pad, lanes])
        grad_ref[pad : 2 * pad, lanes] = (0.5 * (1.0 - bent * bent) * r_sum).astype(BF16)


def scatter_outside(
    rows, pad, proc, halo_rows, row, columns_ref, edge_w, grad_ref, first_ref, second_ref, edge_ref, send_ref
):
    grad = grad_ref[...]
    first_ref[...] = dot(grad, row_stencil(columns_ref, row, halo_rows[0]), NT).astype(BF16)
    second_ref[...] = dot(grad, row_stencil(columns_ref, row, halo_rows[1]), NT).astype(BF16)
    out = dot(edge_w, grad, NT)
    edge_ref[...] = jnp.zeros(edge_ref.shape, F32)
    edge_ref[:, : 2 * pad] = out
    k = iota((EDGE, LANES), 0)
    last = (k == rows - 1) | (k == 2 * rows - 1)
    first = (k == 0) | (k == rows)
    for side, mine in ((-1, last), (1, first)):
        at = lax.axis_index("lat") + side

        @pl.when((at >= 0) & (at < send_ref.shape[0]))
        def _():
            for t in range(edge_ref.shape[1] // LANES):
                part = edge_ref[EDGE : 2 * EDGE, t * LANES : (t + 1) * LANES]
                part = jnp.where(mine, part, 0.0).astype(BF16)
                send_ref[at, proc + EDGE * t : proc + EDGE * (t + 1), :] = part

    for t in range(edge_ref.shape[1] // LANES):
        part = edge_ref[0:EDGE, t * LANES : (t + 1) * LANES].astype(BF16)
        send_ref[lax.axis_index("lat"), proc + EDGE * t : proc + EDGE * (t + 1), :] = part


def gather_kernel(
    dims,
    cells_ref,
    weight_ref,
    absorb_ref,
    profiles_hbm,
    field_hbm,
    turned_hbm,
    part_ref,
    wide_ref,
    rows_ref,
    columns_ref,
    field_ref,
    turned_ref,
    sems,
    out_sems,
):
    levels, rows, width, pad = dims
    loads = load_profiles(profiles_hbm, part_ref, sems)
    fill_columns(cells_ref, weight_ref, columns_ref)
    row, _ = split_cells(cells_ref[...], width)
    turn_absorption(absorb_ref, turned_ref)
    outs = copies([(turned_ref, turned_hbm)], out_sems.at[pl.ds(0, 1)])
    for t in range(width // LANES):
        loads[t].wait()
        widen(t, part_ref, wide_ref)
        for r in range(rows):
            rows_ref[r, :, t * LANES : (t + 1) * LANES] = grid_row(levels, rows, pad, wide_ref, t, r)
    gather_rows(rows, row, columns_ref, rows_ref, field_ref)
    outs += copies([(field_ref, field_hbm)], out_sems.at[pl.ds(1, 1)])
    for move in outs:
        move.wait()


def transfer_kernel(
    dims,
    cells_ref,
    weight_ref,
    instr_ref,
    dest_ref,
    absorb_ref,
    side_first_ref,
    side_second_ref,
    field_hbm,
    turned_hbm,
    row_first_hbm,
    row_second_hbm,
    lat_hbm,
    grad_ref,
    grad_first_ref,
    grad_second_ref,
    send_ref,
    columns_ref,
    turned_ref,
    halo_ref,
    field_ref,
    rate_ref,
    step_ref,
    cot_rows_ref,
    cot_t_ref,
    signal_ref,
    s_part_ref,
    r_part_ref,
    shift_ref,
    row_first_ref,
    row_second_ref,
    lat_ref,
    sems,
):
    levels, rows, width, pad, batch, proc, n_lat, n_lon = dims
    moves = [
        pltpu.make_async_copy(source, target, sems.at[k])
        for k, (source, target) in enumerate(
            (
                (field_hbm, field_ref),
                (turned_hbm, turned_ref),
                (row_first_hbm, row_first_ref),
                (row_second_hbm, row_second_ref),
                (lat_hbm, lat_ref),
            )
        )
    ]
    for move in moves:
        move.start()
    obs = cells_ref.shape[1]
    instruments = absorb_ref.shape[1]
    fill_columns(cells_ref, weight_ref, columns_ref)
    row, _ = split_cells(cells_ref[...], width)
    halo_rows = pair_rows(rows, n_lat)
    edge_w = edge_weights(cells_ref, weight_ref, rows, width)
    moves[4].wait()
    departures(batch, proc, dest_ref, lat_ref, cot_rows_ref, cot_t_ref)
    for k in (0, 2, 3):
        moves[k].wait()
    gather_halo(halo_rows, row, columns_ref, row_first_ref, row_second_ref, field_ref)
    gather_edges(rows, pad, n_lon, side_first_ref, side_second_ref, halo_ref, edge_w, field_ref)
    chosen = chosen_instruments(batch, obs, instr_ref)
    prepare_levels(pad, field_ref, step_ref, rate_ref)
    moves[1].wait()
    walk_levels(
        levels, instruments, chosen, turned_ref, cot_t_ref, rate_ref, step_ref, signal_ref, s_part_ref, r_part_ref
    )
    radiances(batch, proc, dest_ref, signal_ref, field_ref, send_ref)
    pick = jnp.where(iota((instruments, obs), 0) == chosen, 1.0, 0.0)
    held_part(levels, pick, absorb_ref, cot_t_ref, signal_ref, r_part_ref)
    gradients(pad, s_part_ref, r_part_ref, cot_t_ref, field_ref, shift_ref, grad_ref)
    scatter_outside(
        rows,
        pad,
        proc,
        halo_rows,
        row,
        columns_ref,
        edge_w,
        grad_ref,
        grad_first_ref,
        grad_second_ref,
        halo_ref,
        send_ref,
    )


def corner_kernel(proc, lat_ref, out_ref):
    owns, ups, downs = [lat_block(lat_ref, proc, side) for side in (0, -1, 1)]
    for t in range(out_ref.shape[1] // LANES):
        out_ref[:, t * LANES : (t + 1) * LANES] = (owns[t] + ups[t] + downs[t]).astype(BF16)


def scatter_kernel(
    dims,
    cells_ref,
    weight_ref,
    grad_ref,
    row_first_ref,
    row_second_ref,
    side_first_ref,
    side_second_ref,
    lat_ref,
    out_ref,
    rad_out_ref,
    columns_ref,
    halo_ref,
    wide_ref,
    sems,
):
    levels, rows, width, pad, proc, n_lat, n_lon = dims
    fill_columns(cells_ref, weight_ref, columns_ref)
    even, at_lat = pair_place("lat")
    inside = jnp.where(at_lat > 0, 1.0, 0.0), jnp.where(at_lat < n_lat - 1, 1.0, 0.0)
    rad_out_ref[...] = jnp.sum(lat_ref[:, 0:proc, :].astype(F32), axis=0)[None]
    row, _ = split_cells(cells_ref[...], width)
    west = iota(halo_ref.shape, 0) < rows
    from_west, from_east = from_sides(side_first_ref[...], side_second_ref[...], n_lon)
    halo_ref[...] = jnp.where(west, from_west, from_east)
    edges = halo_ref[:, : 2 * pad].T.astype(BF16)
    k = iota((EDGE, LANES), 0)
    at_lane = iota((EDGE, LANES), 1)
    moves = []
    half = 2 * LANES if width % (2 * LANES) == 0 else LANES
    for start in range(0, width, half):
        part = slice(start, start + half)
        for r in range(rows):
            value = dot(grad_ref[...], row_stencil(columns_ref, row, r, part), NT)
            if r == 0:
                value = value + choose(even, row_second_ref[:, part], row_first_ref[:, part]) * inside[0]
            if r == rows - 1:
                value = value + choose(even, row_first_ref[:, part], row_second_ref[:, part]) * inside[1]
            for lane in range(start, start + half, LANES):
                piece = value[:, lane - start : lane - start + LANES]
                if lane == 0:
                    piece = piece + dot(edges, jnp.where((k == r) & (at_lane == 0), 1.0, 0.0).astype(BF16))
                if lane + LANES == width:
                    last_at = jnp.where((k == rows + r) & (at_lane == LANES - 1), 1.0, 0.0).astype(BF16)
                    piece = piece + dot(edges, last_at)
                for v in range(2):
                    at = pl.ds(v * levels * rows + r, levels, stride=rows)
                    wide_ref[lane // LANES, at, :] = piece[v * pad : v * pad + levels, :]
        for lane in range(start, start + half, LANES):
            t = lane // LANES
            move = pltpu.make_async_copy(wide_ref.at[t], out_ref.at[:, lane : lane + LANES], sems.at[t])
            move.start()
            moves.append(move)
    for move in moves:
        move.wait()


def per_device(profiles, obs_cell, obs_weight, batch_instr, batch_dest, absorption, cotangent):
    n_lat, n_lon = lax.axis_size("lat"), lax.axis_size("lon")
    levels, rows, width = profiles.shape[1:]
    instruments, channels, _ = absorption.shape
    obs = obs_cell.shape[1]
    slots = batch_dest.shape[1]
    batch = obs // slots
    proc = cotangent.shape[1]
    pad = round_up(levels, 16)
    feat = round_up(2 * pad, LANES)
    lat_rows = proc + EDGE * (feat // LANES)
    blocks = -(-levels * instruments // LANES)
    lat_pairs = [pairs(n_lat, offset, False) for offset in (0, 1)]
    lon_pairs = [pairs(n_lon, offset, True) for offset in (0, 1)]
    shape = jax.ShapeDtypeStruct
    row_shape = shape((2 * pad, width), BF16)
    edge_shape = shape((EDGE, feat), BF16)
    lat_shape = shape((n_lat, lat_rows, channels), BF16)
    absorb = jnp.transpose(absorption, (2, 0, 1))

    profiles = profiles.reshape(2 * levels, rows, width)
    tiles = width // LANES
    unpacked = [
        pltpu.VMEM((tiles, 2 * levels, rows, LANES), BF16),
        pltpu.VMEM((tiles, 2 * levels * rows, LANES), F32),
    ]
    row_first, row_second, edge, lat_send = pl.pallas_call(
        functools.partial(pack_kernel, (levels, rows, width, pad)),
        out_shape=(row_shape, row_shape, edge_shape, lat_shape),
        in_specs=[HBM] * 2,
        out_specs=(VMEM,) * 4,
        scratch_shapes=unpacked
        + [
            pltpu.VMEM((2, 2 * pad, width), BF16),
            pltpu.VMEM((1, proc, channels), F32),
            pltpu.SemaphoreType.DMA((tiles,)),
            pltpu.SemaphoreType.DMA((1,)),
        ],
        compiler_params=params(56),
        name="pack",
    )(profiles, cotangent)

    lat_in = lax.all_to_all(lat_send, "lat", 0, 0, tiled=True)
    row_first = lax.ppermute(row_first, "lat", lat_pairs[0])
    row_second = lax.ppermute(row_second, "lat", lat_pairs[1])

    field, turned = pl.pallas_call(
        functools.partial(gather_kernel, (levels, rows, width, pad)),
        out_shape=(shape((2 * pad, obs), F32), shape((blocks, channels, LANES), F32)),
        in_specs=[VMEM] * 3 + [HBM],
        out_specs=(HBM,) * 2,
        scratch_shapes=unpacked
        + [
            pltpu.VMEM((rows, 2 * pad, width), BF16),
            pltpu.VMEM((3, width, obs), BF16),
            pltpu.VMEM((2 * pad, obs), F32),
            pltpu.VMEM((blocks, channels, LANES), F32),
            pltpu.SemaphoreType.DMA((tiles,)),
            pltpu.SemaphoreType.DMA((2,)),
        ],
        compiler_params=params(56),
        name="gather",
    )(obs_cell, obs_weight, absorb, profiles)
    edge, field = lax.optimization_barrier((edge, field))

    side = pl.pallas_call(
        functools.partial(blend_kernel, rows, proc),
        out_shape=shape((BLOCKS * EDGE, feat), BF16),
        in_specs=[VMEM] * 2,
        out_specs=VMEM,
        compiler_params=params(4),
        cost_estimate=SMALL,
        name="blend",
    )(edge, lat_in)
    side_first = lax.ppermute(side, "lon", lon_pairs[0])
    side_second = lax.ppermute(side, "lon", lon_pairs[1])

    grad, grad_first, grad_second, lat_back = pl.pallas_call(
        functools.partial(transfer_kernel, (levels, rows, width, pad, batch, proc, n_lat, n_lon)),
        out_shape=(shape((2 * pad, obs), BF16), row_shape, row_shape, lat_shape),
        in_specs=[VMEM, VMEM, SMEM, SMEM] + [VMEM] * 3 + [HBM] * 5,
        out_specs=(VMEM,) * 4,
        scratch_shapes=[
            pltpu.VMEM((3, width, obs), BF16),
            pltpu.VMEM((blocks, channels, LANES), F32),
            pltpu.VMEM((BLOCKS * EDGE, feat), F32),
            pltpu.VMEM((2 * pad, obs), F32),
            pltpu.VMEM((pad, obs), F32),
            pltpu.VMEM((pad, obs), F32),
            pltpu.VMEM((obs, channels), F32),
            pltpu.VMEM((channels, obs), F32),
            pltpu.VMEM((channels, obs), F32),
            pltpu.VMEM((obs // LANES, pad * 8, LANES), F32),
            pltpu.VMEM((obs // LANES, pad * 8, LANES), F32),
            pltpu.VMEM((pad + 8, obs), F32),
            pltpu.VMEM(row_shape.shape, BF16),
            pltpu.VMEM(row_shape.shape, BF16),
            pltpu.VMEM(lat_shape.shape, BF16),
            pltpu.SemaphoreType.DMA((5,)),
        ],
        compiler_params=params(56),
        name="transfer",
    )(
        obs_cell,
        obs_weight,
        batch_instr,
        batch_dest,
        absorb,
        side_first,
        side_second,
        field,
        turned,
        row_first,
        row_second,
        lat_in,
    )

    grad_first = lax.ppermute(grad_first, "lat", lat_pairs[0])
    grad_second = lax.ppermute(grad_second, "lat", lat_pairs[1])
    lat_got = lax.all_to_all(lat_back, "lat", 0, 0, tiled=True)
    grad_side = pl.pallas_call(
        functools.partial(corner_kernel, proc),
        out_shape=edge_shape,
        in_specs=[VMEM],
        out_specs=VMEM,
        compiler_params=params(4),
        cost_estimate=SMALL,
        name="corner",
    )(lat_got)
    grad_side_first = lax.ppermute(grad_side, "lon", lon_pairs[0])
    grad_side_second = lax.ppermute(grad_side, "lon", lon_pairs[1])

    gradient, radiance = pl.pallas_call(
        functools.partial(scatter_kernel, (levels, rows, width, pad, proc, n_lat, n_lon)),
        out_shape=(
            shape((2 * levels * rows, width), F32),
            shape((1, proc, channels), F32),
        ),
        in_specs=[VMEM] * 8,
        out_specs=(HBM, VMEM),
        scratch_shapes=[
            pltpu.VMEM((3, width, obs), BF16),
            pltpu.VMEM((EDGE, feat), F32),
            pltpu.VMEM((width // LANES, 2 * levels * rows, LANES), F32),
            pltpu.SemaphoreType.DMA((width // LANES,)),
        ],
        compiler_params=params(20),
        name="scatter",
    )(obs_cell, obs_weight, grad, grad_first, grad_second, grad_side_first, grad_side_second, lat_got)
    return radiance, gradient.reshape(2, levels, rows, width)


def solution(mesh):
    placed = (
        P("groups", None, "lat", "lon"),
        P(("groups", "lon"), "lat"),
        P("groups", "lon", "lat"),
        P(("groups", "lon"), "lat"),
        P(("groups", "lon"), "lat"),
        P(),
        P(("groups", "lon"), "lat", None),
    )
    return jax.shard_map(
        per_device,
        mesh=mesh,
        in_specs=placed,
        out_specs=(P(("groups", "lon"), "lat", None), P("groups", None, "lat", "lon")),
        check_vma=False,
    )
```
